32 devices in a mesh: dp: 8 (over y, x, core), mp: 4 (over z).
Axes of the slice: x: 2, y: 2, z: 4, core: 2. Of those that a mesh axis runs over, the one named last changes fastest.
Arguments:
- tokens: bfloat16 [10240, 768], P(('dp', 'mp')), may hold values from -6 to 6
- segment_ids: int32 [64, 160], P('dp'), may hold values from 0 to 3, as said below
- live_mask: int32 [64, 160], P('dp'), may hold values from 0 to 1, as said below
- query_weight: bfloat16 [768, 768], P(None, 'mp'), may hold values from -0.21875 to 0.21875
- key_weight: bfloat16 [768, 768], P(None, 'mp'), may hold values from -0.21875 to 0.21875
- value_weight: bfloat16 [768, 768], P(None, 'mp'), may hold values from -0.21875 to 0.21875
- query_bias: bfloat16 [768], P('mp'), may hold values from -3 to 3
- value_bias: bfloat16 [768], P('mp'), may hold values from -3 to 3
- output_weight: bfloat16 [768, 768], P('mp'), may hold values from -1.25 to 1.25
- output_bias: bfloat16 [768], replicated, may hold values from -3 to 3
- first_gain: bfloat16 [768], replicated, may hold values from 0.5 to 1.5
- first_shift: bfloat16 [768], replicated, may hold values from -3 to 3
- inner_weight: bfloat16 [768, 3072], P(None, 'mp'), may hold values from -0.21875 to 0.21875
- inner_bias: bfloat16 [3072], P('mp'), may hold values from -3 to 3
- outer_weight: bfloat16 [3072, 768], P('mp'), may hold values from -0.109375 to 0.109375
- outer_bias: bfloat16 [768], replicated, may hold values from -3 to 3
- second_gain: bfloat16 [768], replicated, may hold values from 0.5 to 1.5
- second_shift: bfloat16 [768], replicated, may hold values from -3 to 3
- cotangent: bfloat16 [10240, 768], P(('dp', 'mp')), may hold values from -6 to 6
Outputs:
- output: bfloat16 [10240, 768], P(('dp', 'mp'))
- input_grad: bfloat16 [10240, 768], P(('dp', 'mp'))
- query_weight_grad: float32 [768, 768], P(None, 'mp')
- key_weight_grad: float32 [768, 768], P(None, 'mp')
- value_weight_grad: float32 [768, 768], P(None, 'mp')
- query_bias_grad: float32 [768], P('mp')
- value_bias_grad: float32 [768], P('mp')
- output_weight_grad: float32 [768, 768], P('mp')
- output_bias_grad: float32 [768], replicated
- first_gain_grad: float32 [768], replicated
- first_shift_grad: float32 [768], replicated
- inner_weight_grad: float32 [768, 3072], P(None, 'mp')
- inner_bias_grad: float32 [3072], P('mp')
- outer_weight_grad: float32 [3072, 768], P('mp')
- outer_bias_grad: float32 [768], replicated
- second_gain_grad: float32 [768], replicated
- second_shift_grad: float32 [768], replicated
The draws below stay inside these ranges and needn't reach their ends.
Inputs may be any that keep to these rules, and one draw needn't show every extreme that they name: `segment_ids`: each row packs one to four chains: ids never fall along a row, start at 0 and take every value up to the row's number of chains less one; padding after a row's live tokens keeps the last chain's id; every chain has 16 or more live tokens; row 0 holds four chains. `live_mask`: 1 on a row's leading live tokens, 0 on the padding after them, at most 40 padding tokens a row; row 0 has padding.
All inputs are finite; a program needn't handle non-finite values.
Results may differ from the reference program's by a relative error of at most 0.02.
Values may be sent and summed in bfloat16 or wider, within the bound.
A program may use at most 128 MiB of HBM per device.

```python
import jax
import jax.numpy as jnp
from jax import lax

D = 768
H = 12
DH = 64
FF = 3072
SEQ = 160
ROWS_DEV = 8
ROWS = 64
TOKENS = 10240
N_DP = 8


def chain_layout(key):
    first_key, second_key, third_key = jax.random.split(key, 3)
    row_index = jnp.arange(ROWS)
    chains = jax.random.randint(first_key, (ROWS,), 1, 5)
    chains = jnp.where(row_index == 0, 4, chains)
    padding = jax.random.randint(second_key, (ROWS,), 0, SEQ // 4 + 1)
    padding = jnp.where(row_index == 0, jnp.maximum(padding, 1), padding)
    live_length = SEQ - padding
    margin = SEQ // 10
    stratum = (live_length - 2 * margin) // 3
    spread = jnp.maximum(stratum - margin, 1)
    offsets = jax.random.randint(third_key, (ROWS, 3), 0, 1 << 20) % spread[:, None]
    cuts = margin + jnp.arange(3)[None, :] * stratum[:, None] + offsets
    cuts = jnp.where(jnp.arange(3)[None, :] < chains[:, None] - 1, cuts, SEQ + 1)
    positions = jnp.arange(SEQ)
    segments = jnp.sum((cuts[:, None, :] <= positions[None, :, None]).astype(jnp.int32), -1)
    live_rows = (positions[None, :] < live_length[:, None]).astype(jnp.int32)
    return (segments.astype(jnp.int32), live_rows)


def draw_segment_ids(key, part):
    segments, live_rows = chain_layout(key)
    return segments


def draw_live_mask(key, part):
    segments, live_rows = chain_layout(key)
    return live_rows


def shard_levels(stream_key, dims, shards, low, high):
    level, own = 1.0, jax.random.fold_in(stream_key, 6)
    for position, blocks in shards:
        heights = jnp.exp(jax.random.uniform(jax.random.fold_in(own, position), (blocks,), jnp.float32, low / len(shards), high / len(shards)))
        level = level * jnp.repeat(heights, dims[position] // blocks).reshape([-1 if axis == position else 1 for axis in range(len(dims))])
    return level


def scatter_about(rng, extent, scale, limit, cuts=(), dtype=jnp.bfloat16):
    drawn = scale * jax.random.normal(rng, extent, jnp.float32)
    if cuts:
        drawn = drawn * shard_levels(rng, extent, cuts, -0.22, 0.18)
    return jnp.clip(drawn, -limit, limit).astype(dtype)


def setup_inputs(seed: int = 0) -> dict:
    keys = jax.random.split(jax.random.key(seed), 20)
    return {
        "tokens": scatter_about(keys[0], (TOKENS, D), 1.0, 6.0, ((0, 32),)),
        "segment_ids": draw_segment_ids(jax.random.fold_in(keys[19], 71), 0),
        "live_mask": draw_live_mask(jax.random.fold_in(keys[19], 71), 0),
        "query_weight": scatter_about(keys[3], (D, D), D ** -0.5, 0.21875, ((1, 4),)),
        "key_weight": scatter_about(keys[4], (D, D), D ** -0.5, 0.21875, ((1, 4),)),
        "value_weight": scatter_about(keys[5], (D, D), D ** -0.5, 0.21875, ((1, 4),)),
        "query_bias": scatter_about(keys[6], (D,), 0.5, 3.0, ((0, 4),)),
        "value_bias": scatter_about(keys[7], (D,), 0.5, 3.0, ((0, 4),)),
        "output_weight": scatter_about(keys[8], (D, D), (D // 32) ** -0.5, 1.25, ((0, 4),)),
        "output_bias": scatter_about(keys[9], (D,), 0.5, 3.0),
        "first_gain": jnp.clip(1.0 + 0.1 * jax.random.normal(keys[10], (D,), jnp.float32), 0.5, 1.5).astype(jnp.bfloat16),
        "first_shift": scatter_about(keys[11], (D,), 0.5, 3.0),
        "inner_weight": scatter_about(keys[12], (D, FF), D ** -0.5, 0.21875, ((1, 4),)),
        "inner_bias": scatter_about(keys[13], (FF,), 0.5, 3.0, ((0, 4),)),
        "outer_weight": scatter_about(keys[14], (FF, D), FF ** -0.5, 0.109375, ((0, 4),)),
        "outer_bias": scatter_about(keys[15], (D,), 0.5, 3.0),
        "second_gain": jnp.clip(1.0 + 0.1 * jax.random.normal(keys[16], (D,), jnp.float32), 0.5, 1.5).astype(jnp.bfloat16),
        "second_shift": scatter_about(keys[17], (D,), 0.5, 3.0),
        "cotangent": scatter_about(keys[18], (TOKENS, D), 1.0, 6.0, ((0, 32),)),
    }


EPSILON = 1e-06
NEG_FILL = -1000000000.0
ROOT_HALF = 0.7071067811865476

@jax.custom_vjp
def low(v):
    return lax.optimization_barrier(v.astype(jnp.bfloat16)).astype(jnp.float32)

@jax.custom_vjp
def low_back(v):
    return v

def low_keep(v):
    return (low(v), None)

def low_pass(kept, grad):
    return (grad,)

def back_keep(v):
    return (v, None)

def back_low(kept, grad):
    return (low(grad),)
low.defvjp(low_keep, low_pass)
low_back.defvjp(back_keep, back_low)

def product(left, right):
    return jnp.dot(left, right, precision=lax.Precision.HIGHEST, preferred_element_type=jnp.float32)

def layer_norm(summed, gain_row, shift_row):
    centre_mean = lax.optimization_barrier(jnp.mean(summed, -1, keepdims=True))
    centred = summed - centre_mean
    variance = lax.optimization_barrier(jnp.mean(centred * centred, -1, keepdims=True))
    return centred * lax.rsqrt(variance + EPSILON) * gain_row + shift_row

def gelu_exact(values):
    return 0.5 * values * (1.0 + lax.erf(values * ROOT_HALF))

def forward(group_rows, allowed, query_weight, key_weight, value_weight, query_bias, value_bias, output_weight, output_bias, first_gain, first_shift, inner_weight, inner_bias, outer_weight, outer_bias, second_gain, second_shift):
    row_count = allowed.shape[0]
    score_scale = DH ** (-0.5)
    shape_heads = (row_count, SEQ, H, DH)
    queries = low(low_back(product(group_rows, query_weight) + query_bias))
    key_rows = low(low_back(product(group_rows, key_weight)))
    value_rows = low(low_back(product(group_rows, value_weight) + value_bias))
    scores = jnp.einsum('rqhd,rkhd->rhqk', queries.reshape(shape_heads), key_rows.reshape(shape_heads), precision=lax.Precision.HIGHEST) * score_scale
    scores = jnp.where(allowed[:, None] == 1, low_back(scores), NEG_FILL)
    row_max = lax.optimization_barrier(jnp.max(scores, -1, keepdims=True))
    exponent = jnp.exp(scores - row_max)
    probability = exponent / lax.optimization_barrier(jnp.sum(exponent, -1, keepdims=True))
    context = jnp.einsum('rhqk,rkhd->rqhd', low(probability), value_rows.reshape(shape_heads), precision=lax.Precision.HIGHEST).reshape(row_count * SEQ, H * DH)
    context = low(low_back(context))
    first_sum = low_back(product(context, output_weight)) + output_bias + group_rows
    first_normed = layer_norm(first_sum, first_gain, first_shift)
    activated = low(gelu_exact(low_back(product(low(first_normed), inner_weight) + inner_bias)))
    second_sum = low_back(product(activated, outer_weight)) + outer_bias + first_normed
    return layer_norm(second_sum, second_gain, second_shift)

def reference(tokens, segment_ids, live_mask, query_weight, key_weight, value_weight, query_bias, value_bias, output_weight, output_bias, first_gain, first_shift, inner_weight, inner_bias, outer_weight, outer_bias, second_gain, second_shift, cotangent):
    params = tuple((weight.astype(jnp.float32) for weight in (query_weight, key_weight, value_weight, query_bias, value_bias, output_weight, output_bias, first_gain, first_shift, inner_weight, inner_bias, outer_weight, outer_bias, second_gain, second_shift)))
    group_tokens = tokens.astype(jnp.float32).reshape(N_DP, ROWS_DEV * SEQ, D)
    group_cots = cotangent.astype(jnp.float32).reshape(N_DP, ROWS_DEV * SEQ, D)
    group_segments = segment_ids.reshape(N_DP, ROWS_DEV, SEQ)
    group_live = live_mask.reshape(N_DP, ROWS_DEV, SEQ)

    def scan_step(running, block_item):
        group_rows, segments, live_rows, cot_rows = block_item
        allowed = ((segments[:, :, None] == segments[:, None, :]) & (live_rows[:, None, :] == 1)).astype(jnp.int32)

        def apply_layer(inputs, *weights):
            return forward(inputs, allowed, *weights)
        result, pullback = jax.vjp(apply_layer, group_rows, *params)
        gradients = pullback(cot_rows)
        running = tuple((accumulated + grad_part for accumulated, grad_part in zip(running, gradients[1:])))
        return (running, (result.astype(jnp.bfloat16), gradients[0].astype(jnp.bfloat16)))
    initial = tuple((jnp.zeros_like(weight) for weight in params))
    running, (outputs, input_grads) = lax.scan(scan_step, initial, (group_tokens, group_segments, group_live, group_cots))
    outputs = outputs.reshape(TOKENS, D)
    input_grads = input_grads.reshape(TOKENS, D)
    return (outputs, input_grads, running[0], running[1], running[2], running[3], running[4], running[5], running[6], running[7], running[8], running[9], running[10], running[11], running[12], running[13], running[14])
```

```python
import functools

import jax
import jax.numpy as jnp
from jax import lax
from jax.experimental import pallas as pl
from jax.experimental.pallas import tpu as pltpu
from jax.sharding import PartitionSpec as P

DH = 64
EPSILON = 1e-06
NEG_FILL = -1000000000.0
ROOT_HALF = 0.7071067811865476
PDF_SCALE = 0.3989422804014327
BF = jnp.bfloat16
F32 = jnp.float32
MESH = pl.DeviceIdType.MESH

NN = (((1,), (0,)), ((), ()))
NT = (((1,), (1,)), ((), ()))
TN = (((0,), (0,)), ((), ()))

ATT, INN, OUT = 0, 1, 2
V_OB, V_G1, V_S1, V_EB, V_G2, V_S2 = 8, 9, 10, 11, 12, 13


def dot(left, right, dims):
    return lax.dot_general(left, right, dims, preferred_element_type=F32)


def layer_kernel(
    cfg,
    tok, cot, wq, wk, wv, wo, wi, wout, vin, seg, live,
    out_ref, dx_ref, grad_ref, vec_ref,
    wbuf, bias, xs, cots, qkv, ka, ks, prob, mask, acc, tmp, nh1, r1,
    nb, nhalf, af, asib, al, gp, g, sg, di, fg, fgf,
    gr, rf, rz1, rz2, rs, rx, vrecv,
    loc_sem, ag_s, ag_r, gr_s, gr_r, x_s, x_r, b_s, b_r, v_s, v_r, e_s, e_r,
):
    n_dp, d, seq, rows = cfg["dp"], cfg["d"], cfg["seq"], cfg["rows"]
    tl = seq * rows
    ml = d // 4
    hs = ml // DH
    half, qtr, eig = d // 2, d // 4, d // 8
    scale = DH ** (-0.5)
    bits = n_dp.bit_length() - 1
    dp, z = lax.axis_index("dp"), lax.axis_index("mp")
    c = dp % 2
    df = 2 + 2 * c
    ds_ = 6 - df
    f, s = (dp // df) % 2, (dp // ds_) % 2
    p_f, p_s, p_c = dp + df * (1 - 2 * f), dp + ds_ * (1 - 2 * s), dp + 1 - 2 * c
    z0, zh = z % 2, z // 2
    z1, z2, z3 = z + 1 - 2 * z0, z + 2 - 4 * zh, 3 - z
    h0 = pl.multiple_of(c * half, 128)
    ho = pl.multiple_of((1 - c) * half, 128)
    q0 = pl.multiple_of(c * half + f * qtr, 16)
    e0 = pl.multiple_of(c * half + f * qtr + s * eig, 16)
    qo = pl.multiple_of(c * half + (1 - f) * qtr, 16)
    eo = pl.multiple_of(c * half + f * qtr + (1 - s) * eig, 16)
    shard = (z, z1, z2, z3)

    def shard_of(k):
        k0, kh = k % 2, k // 2
        return z0 + k0 - 2 * z0 * k0 + 2 * (zh + kh - 2 * zh * kh)

    def remote(src, dst, ssem, rsem, dev):
        return pltpu.make_async_remote_copy(
            src_ref=src, dst_ref=dst, send_sem=ssem, recv_sem=rsem, device_id=dev, device_id_type=MESH
        )

    pending = []

    def send(make):
        remote(*make()).start()
        pending.append(make)

    loads = [
        pltpu.make_async_copy(tok, xs.at[pl.ds(0, rows)], loc_sem.at[0]),
        pltpu.make_async_copy(wo, wbuf.at[ATT, z, pl.ds(3 * ml, ml)], loc_sem.at[1]),
        pltpu.make_async_copy(wi, wbuf.at[INN, z], loc_sem.at[2]),
        pltpu.make_async_copy(wout, wbuf.at[OUT, z], loc_sem.at[3]),
        pltpu.make_async_copy(cot, cots, loc_sem.at[4]),
    ]
    for cp in loads:
        cp.start()
    barrier = pltpu.get_barrier_semaphore()
    extra = [dp + (1 << b) * (1 - 2 * ((dp // (1 << b)) % 2)) for b in range(3, bits)]
    greet = [(p_c, z), (p_f, z), (p_s, z), (dp, z1), (dp, z2), (dp, z3)] + [(e, z) for e in extra]
    for dev in greet:
        pl.semaphore_signal(barrier, inc=1, device_id=dev, device_id_type=MESH)
    for j, w_ref in enumerate((wq, wk, wv)):
        wbuf[ATT, z, pl.ds(j * ml, ml), :] = w_ref[...].T
    bias[z] = vin[...]
    loads[1].wait()
    pl.semaphore_wait(barrier, len(greet))

    wide = {ATT: False, INN: False, OUT: True}

    def own(piece, off, n):
        if piece == ATT:
            return wbuf.at[ATT, z, pl.ds(off, n)]
        return (wi, wout)[piece - 1].at[pl.ds(off, n)]

    def reg(piece, k, off, n):
        return wbuf.at[piece, shard[k], pl.ds(off, n)]

    def ag_send(piece, slot, where, dev, mine=False):
        def make():
            region = reg(piece, *where)
            src = own(piece, *where[1:]) if mine else region
            return src, region, ag_s.at[piece, slot], ag_r.at[piece, slot], dev

        send(make)

    def ag_wait(piece, slot, where):
        region = reg(piece, *where)
        remote(region, region, ag_s.at[piece, slot], ag_r.at[piece, slot], (dp, z1)).wait_recv()

    def first(piece):
        return (q0, qtr) if wide[piece] else (e0, eig)

    def a_z(piece):
        off, n = first(piece)
        ag_send(piece, 1, (0, off, n), (dp, z1), True)
        ag_send(piece, 0, (0, off, n), (dp, z2), True)

    def a_zf(piece):
        off, n = first(piece)
        ag_wait(piece, 0, (2, off, n))
        ag_send(piece, 2, (2, off, n), (dp, z1))

    def a_arrive(piece, k):
        off, n = first(piece)
        if k != 2:
            ag_wait(piece, {1: 1, 3: 2}[k], (k, off, n))

    def a_s(piece, k):
        a_arrive(piece, k)
        ag_send(piece, 2 + k, (k, e0, eig), (p_s, z))

    def a_f(piece, k):
        if wide[piece]:
            a_arrive(piece, k)
        else:
            ag_wait(piece, 2 + k, (k, eo, eig))
        ag_send(piece, 5 + k, (k, q0, qtr), (p_f, z))

    def a_c(piece, k):
        ag_wait(piece, 5 + k, (k, qo, qtr))
        ag_send(piece, 8 + k, (k, h0, half), (p_c, z))

    def a_done(piece, k):
        ag_wait(piece, 8 + k, (k, ho, half))

    X_TOK, X_N, X_G, X_FG, X_A, X_DI, X_KA = 0, 1, 2, 3, 4, 8, 12

    def core_send(slot, pair):
        send(lambda: (*pair(), x_s.at[slot], x_r.at[slot], (p_c, z)))

    def core_wait(slot, dst):
        remote(dst, dst, x_s.at[slot], x_r.at[slot], (p_c, z)).wait_recv()

    for j, zz in enumerate((z1, z2, z3)):
        send(lambda j=j, zz=zz: (vin, bias.at[z], b_s.at[j], b_r.at[j], (dp, zz)))
    a_z(ATT)
    a_z(INN)
    a_z(OUT)
    core_send(X_TOK, lambda: (tok, xs.at[pl.ds(rows, rows)]))

    for r in range(rows):
        seg_row = seg[pl.ds(z * rows + r, 1), :]
        live_row = live[pl.ds(z * rows + r, 1), :]
        code = jnp.where(live_row == 1, seg_row, -1)
        ids = lax.broadcasted_iota(jnp.int32, (8, seq), 0)
        key_hot = (jnp.broadcast_to(code, (8, seq)) == ids).astype(F32).astype(BF)
        query_hot = (jnp.broadcast_to(seg_row, (8, seq)) == ids).astype(F32).astype(BF)
        mask[r] = jnp.where(dot(key_hot, query_hot, TN) > 0.5, 0.0, NEG_FILL)
    acc[...] = jnp.zeros_like(acc)
    first_row = (lax.broadcasted_iota(jnp.int32, (8, seq), 0) == 0).astype(F32).astype(BF)
    loads[0].wait()

    def attend(t):
        def row(r, carry):
            x_row = xs[r]
            bias_rows = bias[t].astype(BF)[:, : 3 * ml]
            qkv[t, r] = (
                dot(wbuf[ATT, t, pl.ds(0, 3 * ml), :], x_row, NT) + dot(bias_rows, first_row, TN)
            ).astype(BF)
            for h in range(hs):
                query = qkv[t, r, pl.ds(h * DH, DH), :]
                key = qkv[t, r, pl.ds(ml + h * DH, DH), :]
                value = qkv[t, r, pl.ds(2 * ml + h * DH, DH), :]
                scores = dot(key, query, TN) * scale + mask[r]
                top = jnp.max(scores, 0, keepdims=True)
                exponent = jnp.exp(scores - top)
                total = jnp.sum(exponent, 0, keepdims=True)
                prob_t = (exponent * (1.0 / total)).astype(BF)
                prob[t, r, h] = prob_t
                ka[t, r, pl.ds(3 * ml + h * DH, DH), :] = dot(value, prob_t, NN).astype(BF)
            part = dot(ka[t, r, pl.ds(3 * ml, ml), :], wbuf[ATT, t, pl.ds(3 * ml, ml), :], TN)
            sl = pl.ds(pl.multiple_of(r * seq, 16), seq)
            acc[sl, :] = acc[sl, :] + part
            return carry

        lax.fori_loop(0, rows, row, 0)

    def attend_loop(i, carry):
        @pl.when(i == 1)
        def _():
            remote(vin, bias.at[z1], b_s.at[0], b_r.at[0], (dp, z1)).wait_recv()
            remote(vin, bias.at[z2], b_s.at[1], b_r.at[1], (dp, z2)).wait_recv()
            remote(vin, bias.at[z3], b_s.at[2], b_r.at[2], (dp, z3)).wait_recv()
            a_s(ATT, 1)
            a_zf(ATT)
            a_s(ATT, 2)
            a_f(ATT, 1)
            a_s(INN, 1)
            a_s(ATT, 3)
            a_f(ATT, 2)
            a_c(ATT, 1)
            a_zf(INN)
            a_s(INN, 2)
            a_done(ATT, 1)

        @pl.when(i == 2)
        def _():
            a_f(ATT, 3)
            a_c(ATT, 2)
            a_s(INN, 3)
            a_f(INN, 1)
            a_done(ATT, 2)

        @pl.when(i == 3)
        def _():
            a_c(ATT, 3)
            a_f(INN, 2)
            a_c(INN, 1)
            a_done(ATT, 3)

        attend(shard_of(i))
        return carry

    lax.fori_loop(0, 4, attend_loop, 0)

    rb = 32

    def norm_rows(summed):
        mean = jnp.mean(summed, -1, keepdims=True)
        centred = summed - mean
        variance = jnp.mean(centred * centred, -1, keepdims=True)
        rs_ = lax.rsqrt(variance + EPSILON)
        return centred * rs_, rs_

    def norm_back(grad, hat, rs_):
        return rs_ * (grad - jnp.mean(grad, -1, keepdims=True) - hat * jnp.mean(grad * hat, -1, keepdims=True))

    def vrow(j):
        return vin[pl.ds(j, 1), :]

    a_f(INN, 3)
    a_c(INN, 2)
    a_zf(OUT)
    a_f(OUT, 1)

    def norm1(j, carry):
        sl = pl.ds(pl.multiple_of(j * rb, 16), rb)
        per = seq // rb
        x_blk = xs[j // per, pl.ds(pl.multiple_of((j % per) * rb, 16), rb), :].astype(F32)
        hat, rs_ = norm_rows(acc[sl, :] + vrow(2) + x_blk)
        nh1[sl, :] = hat
        r1[sl, :] = jnp.broadcast_to(rs_, (rb, 128))
        nb[sl, :] = (hat * vrow(3) + vrow(4)).astype(BF)
        acc[sl, :] = jnp.zeros((rb, d), F32)
        return carry

    lax.fori_loop(0, tl // rb, norm1, 0)
    core_send(X_N, lambda: (nb.at[:, pl.ds(ho, half)], nhalf.at[pl.ds(tl, tl)]))
    nhalf[pl.ds(0, tl), :] = nb[:, pl.ds(h0, half)]

    loads[2].wait()

    def up(i, carry):
        @pl.when(i == 1)
        def _():
            a_done(INN, 1)
            a_f(OUT, 2)
            a_c(INN, 3)

        @pl.when(i == 2)
        def _():
            a_done(INN, 2)
            a_c(OUT, 1)

        @pl.when(i == 3)
        def _():
            a_done(INN, 3)
            a_c(OUT, 2)

        t = shard_of(i)
        tmp[...] = dot(nb[...], wbuf[INN, t], NN)
        b_row = bias[t, pl.ds(1, 1), :]

        def act(j, carry):
            sl = pl.ds(pl.multiple_of(j * rb, 16), rb)
            u = tmp[sl, :] + b_row
            cdf = 0.5 * (1.0 + lax.erf(u * ROOT_HALF))
            af[t, sl, :] = (u * cdf).astype(BF)
            gp[t, sl, :] = (cdf + u * (PDF_SCALE * jnp.exp(-0.5 * u * u))).astype(BF)
            return carry

        lax.fori_loop(0, tl // rb, act, 0)
        remote(af.at[t, :, pl.ds(ho, half)], asib.at[t], x_s.at[X_A + i], x_r.at[X_A + i], (p_c, z)).start()
        return carry

    lax.fori_loop(0, 4, up, 0)
    loads[3].wait()
    loads[4].wait()

    def down(i, carry):
        @pl.when(i == 1)
        def _():
            a_f(OUT, 3)
            a_done(OUT, 1)

        @pl.when(i == 2)
        def _():
            a_done(OUT, 2)
            a_c(OUT, 3)

        @pl.when(i == 3)
        def _():
            a_done(OUT, 3)

        t = shard_of(i)
        acc[...] += dot(af[t], wbuf[OUT, t], NN)
        return carry

    lax.fori_loop(0, 4, down, 0)

    vec_ref[...] = jnp.zeros_like(vec_ref)

    def add_vec(row, value):
        vec_ref[pl.ds(row, 1), :] = vec_ref[pl.ds(row, 1), :] + value

    def norm2(j, carry):
        sl = pl.ds(pl.multiple_of(j * rb, 16), rb)
        normed = nh1[sl, :] * vrow(3) + vrow(4)
        hat, rs_ = norm_rows(acc[sl, :] + vrow(5) + normed)
        out_ref[sl, :] = (hat * vrow(6) + vrow(7)).astype(BF)
        c_blk = cots[sl, :].astype(F32)
        back = norm_back(c_blk * vrow(6), hat, rs_)
        sg[sl, :] = back
        g[sl, :] = back.astype(BF)
        acc[sl, :] = jnp.zeros((rb, d), F32)
        add_vec(V_G2, jnp.sum(c_blk * hat, 0, keepdims=True))
        add_vec(V_S2, jnp.sum(c_blk, 0, keepdims=True))
        add_vec(V_EB, jnp.sum(back, 0, keepdims=True))
        return carry

    lax.fori_loop(0, tl // rb, norm2, 0)
    core_send(X_G, lambda: (g.at[pl.ds(0, tl)], g.at[pl.ds(tl, tl)]))

    fq = pl.multiple_of(f * qtr, 16)
    fo = pl.multiple_of((1 - f) * qtr, 16)
    sq = pl.multiple_of(f * qtr + s * eig, 16)
    so = pl.multiple_of(f * qtr + (1 - s) * eig, 16)

    def g_sem(piece, slot):
        return gr_s.at[piece, slot], gr_r.at[piece, slot]

    def g_send(piece, slot, pair, dev):
        send(lambda: (*pair(), *g_sem(piece, slot), dev))

    def g_wait(piece, slot, dst):
        remote(dst, dst, *g_sem(piece, slot), (dp, z1)).wait_recv()

    def add_into(dst, src, n):
        def blk(j, carry):
            sl = pl.ds(pl.multiple_of(j * 48, 16), 48)
            dst[sl, :] = (dst[sl, :].astype(F32) + src[sl, :].astype(F32)).astype(BF)
            return carry

        lax.fori_loop(0, n // 48, blk, 0)

    def fs_dynamic(piece, k):
        ssem, rsem = g_sem(piece, k)
        remote(gr.at[piece, k, pl.ds(fo, qtr)], rf.at[piece, k], ssem, rsem, (p_f, z)).start()

    def fr(piece, k):
        g_wait(piece, k, rf.at[piece, k])
        add_into(gr.at[piece, k, pl.ds(fq, qtr)], rf.at[piece, k], qtr)
        if k == 3:
            g_send(piece, 4, lambda: (gr.at[piece, 3, pl.ds(fq, qtr)], rz1.at[piece, 0]), (dp, z1))
        if k == 1:
            g_send(piece, 5, lambda: (gr.at[piece, 1, pl.ds(fq, qtr)], rz1.at[piece, 1]), (dp, z1))

    def z1r2(piece):
        g_wait(piece, 4, rz1.at[piece, 0])
        add_into(gr.at[piece, 2, pl.ds(fq, qtr)], rz1.at[piece, 0], qtr)
        g_send(piece, 6, lambda: (gr.at[piece, 2, pl.ds(fq, qtr)], rz2.at[piece]), (dp, z2))

    def z1r0(piece):
        g_wait(piece, 5, rz1.at[piece, 1])
        add_into(gr.at[piece, 0, pl.ds(fq, qtr)], rz1.at[piece, 1], qtr)

    def z2r(piece):
        g_wait(piece, 6, rz2.at[piece])
        add_into(gr.at[piece, 0, pl.ds(fq, qtr)], rz2.at[piece], qtr)
        g_send(piece, 7, lambda: (gr.at[piece, 0, pl.ds(so, eig)], rs.at[piece]), (p_s, z))

    def sr(piece):
        g_wait(piece, 7, rs.at[piece])
        mine = gr.at[piece, 0, pl.ds(sq, eig)]
        add_into(mine, rs.at[piece], eig)
        for j, partner in enumerate(extra):
            cp = remote(mine, rx.at[piece, j], e_s.at[piece, j], e_r.at[piece, j], (partner, z))
            cp.start()
            cp.wait()
            add_into(mine, rx.at[piece, j], eig)
        g_send(
            piece, 8, lambda: (gr.at[piece, 0, pl.ds(sq, eig)], grad_ref.at[piece, pl.ds(e0, eig)]), (p_s, z)
        )
        cp = pltpu.make_async_copy(mine, grad_ref.at[piece, pl.ds(e0, eig)], loc_sem.at[5 + piece])
        cp.start()
        return cp

    local_out = {}

    def sr_(piece):
        local_out[piece] = sr(piece)

    def s2r(piece):
        g_wait(piece, 8, grad_ref.at[piece, pl.ds(eo, eig)])
        local_out[piece].wait()
        g_send(piece, 9, lambda: (grad_ref.at[piece, pl.ds(q0, qtr)],) * 2, (p_f, z))

    def f2r(piece):
        g_wait(piece, 9, grad_ref.at[piece, pl.ds(qo, qtr)])
        g_send(piece, 10, lambda: (grad_ref.at[piece, pl.ds(h0, half)],) * 2, (p_c, z))

    def c2r(piece):
        g_wait(piece, 10, grad_ref.at[piece, pl.ds(ho, half)])

    def order(i):
        return 3 - 2 * (i % 2) - i // 2

    def ffn_back(i, carry):
        @pl.when(i < 4)
        def _():
            k = order(i)
            t = shard_of(k)
            tmp[...] = dot(g[pl.ds(0, tl), :], wbuf[OUT, t], NT)

            def act(j, carry):
                sl = pl.ds(pl.multiple_of(j * rb, 16), rb)
                blk = (tmp[sl, :] * gp[t, sl, :].astype(F32)).astype(BF)
                di[t, sl, :] = blk
                return carry + jnp.sum(blk.astype(F32), 0, keepdims=True)

            vec_ref[pl.ds(4 + t, 1), :] = lax.fori_loop(0, tl // rb, act, jnp.zeros((1, d), F32))
            remote(
                di.at[t, pl.ds(0, tl)], di.at[t, pl.ds(tl, tl)], x_s.at[X_DI + k], x_r.at[X_DI + k], (p_c, z)
            ).start()

            @pl.when(i == 0)
            def _():
                core_wait(X_G, g.at[pl.ds(tl, tl)])
                core_wait(X_N, nhalf.at[pl.ds(tl, tl)])

            core_wait(X_A + k, asib.at[t])
            al[pl.ds(0, tl), :] = af[t, :, pl.ds(h0, half)]
            al[pl.ds(tl, tl), :] = asib[t]
            gr[OUT, k] = dot(al[...], g[...], TN).astype(BF)
            fs_dynamic(OUT, k)
            acc[...] += dot(di[t, pl.ds(0, tl), :], wbuf[INN, t], NT)

        @pl.when(i == 2)
        def _():
            fr(OUT, 3)

        @pl.when(i == 4)
        def _():
            fr(OUT, 1)

        @pl.when(i > 0)
        def _():
            k = order(i - 1)
            t = shard_of(k)
            core_wait(X_DI + k, di.at[t, pl.ds(tl, tl)])
            gr[INN, k] = dot(nhalf[...], di[t], TN).astype(BF)
            fs_dynamic(INN, k)

        return carry

    lax.fori_loop(0, 5, ffn_back, 0)

    def norm1_back(j, carry):
        sl = pl.ds(pl.multiple_of(j * rb, 16), rb)
        per = seq // rb
        hat = nh1[sl, :]
        total = acc[sl, :] + sg[sl, :]
        back = norm_back(total * vrow(3), hat, r1[sl, 0:1])
        fgf[sl, :] = back
        fg[j // per, pl.ds(pl.multiple_of((j % per) * rb, 16), rb), :] = back.astype(BF)
        acc[sl, :] = jnp.zeros((rb, d), F32)
        add_vec(V_G1, jnp.sum(total * hat, 0, keepdims=True))
        add_vec(V_S1, jnp.sum(total, 0, keepdims=True))
        add_vec(V_OB, jnp.sum(back, 0, keepdims=True))
        return carry

    lax.fori_loop(0, tl // rb, norm1_back, 0)
    core_send(X_FG, lambda: (fg.at[pl.ds(0, rows)], fg.at[pl.ds(rows, rows)]))
    ones = jnp.ones((8, seq), BF)

    def attend_back(t):
        def row(r, carry):
            dctx = dot(wbuf[ATT, t, pl.ds(3 * ml, ml), :], fg[r], NT).astype(BF)
            for h in range(hs):
                query = qkv[t, r, pl.ds(h * DH, DH), :]
                key = qkv[t, r, pl.ds(ml + h * DH, DH), :]
                value = qkv[t, r, pl.ds(2 * ml + h * DH, DH), :]
                prob_t = prob[t, r, h]
                grad = dctx[h * DH : (h + 1) * DH]
                ka[t, r, pl.ds(2 * ml + h * DH, DH), :] = dot(grad, prob_t, NT).astype(BF)
                prob_grad = dot(value, grad, TN)
                wide_prob = prob_t.astype(F32)
                inner = jnp.sum(wide_prob * prob_grad, 0, keepdims=True)
                score_grad = (wide_prob * (prob_grad - inner)).astype(BF)
                ka[t, r, pl.ds(h * DH, DH), :] = (dot(key, score_grad, NN) * scale).astype(BF)
                ka[t, r, pl.ds(ml + h * DH, DH), :] = (dot(query, score_grad, NT) * scale).astype(BF)
            grads = ka[t, r, pl.ds(0, 3 * ml), :]
            vec_ref[pl.ds(t, 1), pl.ds(0, 3 * ml)] += dot(ones, grads, NT)[0:1]
            sl = pl.ds(pl.multiple_of(r * seq, 16), seq)
            acc[sl, :] = acc[sl, :] + dot(grads, wbuf[ATT, t, pl.ds(0, 3 * ml), :], TN)
            return carry

        lax.fori_loop(0, rows, row, 0)

    def att_back(i, carry):
        @pl.when(i < 4)
        def _():
            k = order(i)
            t = shard_of(k)
            attend_back(t)
            remote(
                ka.at[t, :, pl.ds(ho, half)], ks.at[t], x_s.at[X_KA + k], x_r.at[X_KA + k], (p_c, z)
            ).start()

        @pl.when(i == 0)
        def _():
            core_wait(X_TOK, xs.at[pl.ds(rows, rows)])
            core_wait(X_FG, fg.at[pl.ds(rows, rows)])
            fr(OUT, 2)
            fr(OUT, 0)

        @pl.when(i == 1)
        def _():
            z1r2(OUT)
            fr(INN, 3)

        @pl.when(i == 2)
        def _():
            z1r0(OUT)
            fr(INN, 1)

        @pl.when(i == 3)
        def _():
            z2r(OUT)
            fr(INN, 2)

        @pl.when(i == 4)
        def _():
            fr(INN, 0)
            z1r2(INN)

        @pl.when(i > 0)
        def _():
            k = order(i - 1)
            t = shard_of(k)
            core_wait(X_KA + k, ks.at[t])
            for j in range(2):
                rowsel = pl.ds(pl.multiple_of(h0 + j * ml, 16), ml)
                use = c * j
                total = jnp.zeros((ml, d), F32)
                for r in range(rows):
                    right_own = xs[r] if j == 0 else jnp.where(use == 1, fg[r], xs[r])
                    right_sib = xs[rows + r] if j == 0 else jnp.where(use == 1, fg[rows + r], xs[rows + r])
                    total += dot(ka[t, r, rowsel, :], right_own, NN)
                    total += dot(ks[t, r, pl.ds(j * ml, ml), :], right_sib, NN)
                gr[ATT, k, pl.ds(j * ml, ml), :] = total.astype(BF)
            fs_dynamic(ATT, k)

        return carry

    lax.fori_loop(0, 5, att_back, 0)

    def finish(j, carry):
        sl = pl.ds(pl.multiple_of(j * rb, 16), rb)
        dx_ref[sl, :] = (fgf[sl, :] + acc[sl, :]).astype(BF)
        return carry

    lax.fori_loop(0, tl // rb, finish, 0)

    partners = [(p_c, z), (p_f, z), (p_s, z)] + [(e, z) for e in extra] + [(dp, z1), (dp, z2)]

    def v_step(j):
        cp = remote(vec_ref, vrecv.at[j], v_s.at[j], v_r.at[j], partners[j])
        cp.start()
        return cp

    def v_end(cp, j):
        cp.wait()
        vec_ref[...] += vrecv[j]

    v0 = v_step(0)
    sr_(OUT)
    z1r0(INN)
    v_end(v0, 0)
    v1 = v_step(1)
    fr(ATT, 3)
    z2r(INN)
    fr(ATT, 1)
    s2r(OUT)
    v_end(v1, 1)
    v2 = v_step(2)
    fr(ATT, 2)
    sr_(INN)
    f2r(OUT)
    fr(ATT, 0)
    v_end(v2, 2)
    v3 = v_step(3)
    z1r2(ATT)
    s2r(INN)
    z1r0(ATT)
    v_end(v3, 3)
    v4 = v_step(4)
    f2r(INN)
    z2r(ATT)
    v_end(v4, 4)
    for j in range(5, len(partners)):
        v_end(v_step(j), j)
    sr_(ATT)
    s2r(ATT)
    f2r(ATT)
    c2r(OUT)
    c2r(INN)
    c2r(ATT)

    for make in pending:
        remote(*make()).wait_send()

    def sent(k, carry):
        t = shard_of(k)
        remote(af.at[t, :, pl.ds(ho, half)], asib.at[t], x_s.at[X_A + k], x_r.at[X_A + k], (p_c, z)).wait_send()
        remote(
            di.at[t, pl.ds(0, tl)], di.at[t, pl.ds(tl, tl)], x_s.at[X_DI + k], x_r.at[X_DI + k], (p_c, z)
        ).wait_send()
        remote(ka.at[t, :, pl.ds(ho, half)], ks.at[t], x_s.at[X_KA + k], x_r.at[X_KA + k], (p_c, z)).wait_send()
        for piece in range(3):
            ssem, rsem = g_sem(piece, k)
            remote(gr.at[piece, k, pl.ds(fo, qtr)], rf.at[piece, k], ssem, rsem, (p_f, z)).wait_send()
        return carry

    lax.fori_loop(0, 4, sent, 0)


def spread_kernel(
    ml, grads, vec, out_in, dx_in,
    out_ref, dx_ref, gq, gk, gv, go, gi, ge,
):
    out_ref[...] = out_in[...]
    dx_ref[...] = dx_in[...]
    for j, ref in enumerate((gq, gk, gv)):
        ref[...] = grads[0, pl.ds(j * ml, ml), :].astype(F32).T
    go[...] = grads[0, pl.ds(3 * ml, ml), :].astype(F32)
    gi[...] = grads[1].astype(F32)
    ge[...] = grads[2].astype(F32)


def per_device(
    n_dp,
    tokens, segment_ids, live_mask, query_weight, key_weight, value_weight, query_bias, value_bias,
    output_weight, output_bias, first_gain, first_shift, inner_weight, inner_bias, outer_weight,
    outer_bias, second_gain, second_shift, cotangent,
):
    tl, d = tokens.shape
    seq_rows, seq = segment_ids.shape
    rows = tl // seq
    ml = query_weight.shape[1]
    half, qtr, eig = d // 2, d // 4, d // 8
    bits = n_dp.bit_length() - 1
    n_extra = max(bits - 3, 1)
    n_vec = bits + 2
    zeros = jnp.zeros((ml,), F32)
    att_bias = jnp.concatenate([query_bias.astype(F32), zeros, value_bias.astype(F32), zeros])
    vin = jnp.stack(
        [att_bias]
        + [
            v.astype(F32)
            for v in (inner_bias, output_bias, first_gain, first_shift, outer_bias, second_gain, second_shift)
        ]
    )
    cfg = {"dp": n_dp, "d": d, "seq": seq, "rows": rows}
    vmem = pl.BlockSpec(memory_space=pltpu.VMEM)
    hbm = pl.BlockSpec(memory_space=pl.ANY)
    scratch = [
        pltpu.VMEM((3, 4, d, d), BF),
        pltpu.VMEM((4, 8, d), F32),
        pltpu.VMEM((2 * rows, seq, d), BF),
        pltpu.VMEM((tl, d), BF),
        pltpu.VMEM((4, rows, 3 * ml, seq), BF),
        pltpu.VMEM((4, rows, d, seq), BF),
        pltpu.VMEM((4, rows, half, seq), BF),
        pltpu.VMEM((4, rows, ml // DH, seq, seq), BF),
        pltpu.VMEM((rows, seq, seq), F32),
        pltpu.VMEM((tl, d), F32),
        pltpu.VMEM((tl, d), F32),
        pltpu.VMEM((tl, d), F32),
        pltpu.VMEM((tl, 128), F32),
        pltpu.VMEM((tl, d), BF),
        pltpu.VMEM((2 * tl, half), BF),
        pltpu.VMEM((4, tl, d), BF),
        pltpu.VMEM((4, tl, half), BF),
        pltpu.VMEM((2 * tl, half), BF),
        pltpu.VMEM((4, tl, d), BF),
        pltpu.VMEM((2 * tl, d), BF),
        pltpu.VMEM((tl, d), F32),
        pltpu.VMEM((4, 2 * tl, d), BF),
        pltpu.VMEM((2 * rows, seq, d), BF),
        pltpu.VMEM((tl, d), F32),
        pltpu.VMEM((3, 4, half, d), BF),
        pltpu.VMEM((3, 4, qtr, d), BF),
        pltpu.VMEM((3, 2, qtr, d), BF),
        pltpu.VMEM((3, qtr, d), BF),
        pltpu.VMEM((3, eig, d), BF),
        pltpu.VMEM((3, n_extra, eig, d), BF) if bits > 3 else pltpu.VMEM((1, 1, 16, 128), BF),
        pltpu.VMEM((n_vec, 16, d), F32),
        pltpu.SemaphoreType.DMA((8,)),
        pltpu.SemaphoreType.DMA((3, 12)),
        pltpu.SemaphoreType.DMA((3, 12)),
        pltpu.SemaphoreType.DMA((3, 11)),
        pltpu.SemaphoreType.DMA((3, 11)),
        pltpu.SemaphoreType.DMA((16,)),
        pltpu.SemaphoreType.DMA((16,)),
        pltpu.SemaphoreType.DMA((3,)),
        pltpu.SemaphoreType.DMA((3,)),
        pltpu.SemaphoreType.DMA((n_vec,)),
        pltpu.SemaphoreType.DMA((n_vec,)),
        pltpu.SemaphoreType.DMA((3, n_extra)),
        pltpu.SemaphoreType.DMA((3, n_extra)),
    ]
    out, dx, grads, vec = pl.pallas_call(
        functools.partial(layer_kernel, cfg),
        out_shape=(
            jax.ShapeDtypeStruct((tl, d), BF),
            jax.ShapeDtypeStruct((tl, d), BF),
            jax.ShapeDtypeStruct((3, d, d), BF),
            jax.ShapeDtypeStruct((16, d), F32),
        ),
        in_specs=[hbm, hbm, vmem, vmem, vmem, hbm, hbm, hbm, vmem, vmem, vmem],
        out_specs=(vmem, vmem, hbm, vmem),
        scratch_shapes=scratch,
        compiler_params=pltpu.CompilerParams(
            collective_id=0, has_side_effects=True, vmem_limit_bytes=62 * 1024 * 1024
        ),
        name="layer",
    )(
        tokens.reshape(rows, seq, d), cotangent, query_weight, key_weight, value_weight, output_weight,
        inner_weight, outer_weight, vin, segment_ids, live_mask,
    )
    ff = inner_weight.shape[1]
    out, dx, gq, gk, gv, go, gi, ge = pl.pallas_call(
        functools.partial(spread_kernel, ml),
        out_shape=(
            jax.ShapeDtypeStruct((tl, d), BF),
            jax.ShapeDtypeStruct((tl, d), BF),
            jax.ShapeDtypeStruct((d, ml), F32),
            jax.ShapeDtypeStruct((d, ml), F32),
            jax.ShapeDtypeStruct((d, ml), F32),
            jax.ShapeDtypeStruct((ml, d), F32),
            jax.ShapeDtypeStruct((d, ff), F32),
            jax.ShapeDtypeStruct((ff, d), F32),
        ),
        in_specs=[vmem] * 4,
        out_specs=(vmem,) * 8,
        compiler_params=pltpu.CompilerParams(vmem_limit_bytes=40 * 1024 * 1024),
        name="spread",
    )(grads, vec, out, dx)
    z = lax.axis_index("mp")
    att_row = lax.dynamic_slice(vec, (z, 0), (1, d))[0]
    inner_row = lax.dynamic_slice(vec, (4 + z, 0), (1, d))[0]
    return (
        out, dx, gq, gk, gv, att_row[:ml], att_row[2 * ml : 3 * ml], go, vec[V_OB], vec[V_G1], vec[V_S1],
        gi, inner_row, ge, vec[V_EB], vec[V_G2], vec[V_S2],
    )


def solution(mesh):
    tok, shared = P(("dp", "mp"), None), P()
    cols, rows, vec = P(None, "mp"), P("mp", None), P("mp")
    in_specs = (
        tok, P("dp", None), P("dp", None), cols, cols, cols, vec, vec, rows, shared, shared, shared,
        cols, vec, rows, shared, shared, shared, tok,
    )
    out_specs = (
        tok, tok, cols, cols, cols, vec, vec, rows, shared, shared, shared, cols, vec, rows,
        shared, shared, shared,
    )
    return jax.shard_map(
        functools.partial(per_device, mesh.shape["dp"]),
        mesh=mesh,
        in_specs=in_specs,
        out_specs=out_specs,
        check_vma=False,
    )
```

```python
import functools

import jax
import jax.numpy as jnp
from jax import lax
from jax.experimental import pallas as pl
from jax.experimental.pallas import tpu as pltpu
from jax.sharding import PartitionSpec as P

DH = 64
EPSILON = 1e-06
NEG_FILL = -1000000000.0
ROOT_HALF = 0.7071067811865476
PDF_SCALE = 0.3989422804014327
BF = jnp.bfloat16
F32 = jnp.float32
MESH = pl.DeviceIdType.MESH

NN = (((1,), (0,)), ((), ()))
NT = (((1,), (1,)), ((), ()))
TN = (((0,), (0,)), ((), ()))

ATT, INN, OUT = 0, 1, 2
V_OB, V_G1, V_S1, V_EB, V_G2, V_S2 = 8, 9, 10, 11, 12, 13


def dot(left, right, dims):
    return lax.dot_general(left, right, dims, preferred_element_type=F32)


def layer_kernel(
    cfg,
    tok, cot, wq, wk, wv, wo, wi, wout, bq, bv, bi, bo, g1, s1, be, g2, s2, seg, live,
    out_ref, dx_ref, grad_ref, vec_ref,
    wbuf, bias, xs, cots, qkv, ka, ks, prob, mask, acc, tmp, nh1, r1,
    nb, nhalf, af, asib, al, gp, g, sg, di, fg, fgf,
    gr, rf, rz1, rz2, rs, rx, vrecv, vin,
    loc_sem, ag_s, ag_r, gr_s, gr_r, x_s, x_r, b_s, b_r, v_s, v_r, e_s, e_r,
):
    n_dp, d, seq, rows = cfg["dp"], cfg["d"], cfg["seq"], cfg["rows"]
    tl = seq * rows
    ml = d // 4
    hs = ml // DH
    half, qtr, eig = d // 2, d // 4, d // 8
    scale = DH ** (-0.5)
    bits = n_dp.bit_length() - 1
    dp, z = lax.axis_index("dp"), lax.axis_index("mp")
    c = dp % 2
    df = 2 + 2 * c
    ds_ = 6 - df
    f, s = (dp // df) % 2, (dp // ds_) % 2
    p_f, p_s, p_c = dp + df * (1 - 2 * f), dp + ds_ * (1 - 2 * s), dp + 1 - 2 * c
    z0, zh = z % 2, z // 2
    z1, z2, z3 = z + 1 - 2 * z0, z + 2 - 4 * zh, 3 - z
    h0 = pl.multiple_of(c * half, 128)
    ho = pl.multiple_of((1 - c) * half, 128)
    q0 = pl.multiple_of(c * half + f * qtr, 16)
    e0 = pl.multiple_of(c * half + f * qtr + s * eig, 16)
    qo = pl.multiple_of(c * half + (1 - f) * qtr, 16)
    eo = pl.multiple_of(c * half + f * qtr + (1 - s) * eig, 16)
    shard = (z, z1, z2, z3)

    def shard_of(k):
        k0, kh = k % 2, k // 2
        return z0 + k0 - 2 * z0 * k0 + 2 * (zh + kh - 2 * zh * kh)

    def remote(src, dst, ssem, rsem, dev):
        return pltpu.make_async_remote_copy(
            src_ref=src, dst_ref=dst, send_sem=ssem, recv_sem=rsem, device_id=dev, device_id_type=MESH
        )

    pending = []

    def send(make):
        remote(*make()).start()
        pending.append(make)

    loads = [
        pltpu.make_async_copy(tok, xs.at[pl.ds(0, rows)], loc_sem.at[0]),
        pltpu.make_async_copy(wo, wbuf.at[ATT, z, pl.ds(3 * ml, ml)], loc_sem.at[1]),
        pltpu.make_async_copy(wi, wbuf.at[INN, z], loc_sem.at[2]),
        pltpu.make_async_copy(wout, wbuf.at[OUT, z], loc_sem.at[3]),
        pltpu.make_async_copy(cot, cots, loc_sem.at[4]),
    ] + [
        pltpu.make_async_copy(ref, wbuf.at[ATT, z, pl.ds(j * ml, ml)], loc_sem.at[8 + j])
        for j, ref in enumerate((wq, wk, wv))
    ]
    for cp in loads:
        cp.start()
    barrier = pltpu.get_barrier_semaphore()
    extra = [dp + (1 << b) * (1 - 2 * ((dp // (1 << b)) % 2)) for b in range(3, bits)]
    greet = [(p_c, z), (p_f, z), (p_s, z), (dp, z1), (dp, z2), (dp, z3)] + [(e, z) for e in extra]
    for dev in greet:
        pl.semaphore_signal(barrier, inc=1, device_id=dev, device_id_type=MESH)
    vin[...] = jnp.zeros_like(vin)
    vin[pl.ds(0, 1), pl.ds(0, ml)] = bq[...].astype(F32).reshape(1, ml)
    vin[pl.ds(0, 1), pl.ds(2 * ml, ml)] = bv[...].astype(F32).reshape(1, ml)
    for j, ref in enumerate((bi, bo, g1, s1, be, g2, s2)):
        vin[pl.ds(j + 1, 1), :] = ref[...].astype(F32).reshape(1, d)
    bias[z] = vin[...]
    for j in (1, 5, 6, 7):
        loads[j].wait()
    pl.semaphore_wait(barrier, len(greet))

    wide = {ATT: False, INN: False, OUT: True}

    def own(piece, off, n):
        if piece == ATT:
            return wbuf.at[ATT, z, pl.ds(off, n)]
        return (wi, wout)[piece - 1].at[pl.ds(off, n)]

    def reg(piece, k, off, n):
        return wbuf.at[piece, shard[k], pl.ds(off, n)]

    def ag_send(piece, slot, where, dev, mine=False):
        def make():
            region = reg(piece, *where)
            src = own(piece, *where[1:]) if mine else region
            return src, region, ag_s.at[piece, slot], ag_r.at[piece, slot], dev

        send(make)

    def ag_wait(piece, slot, where):
        region = reg(piece, *where)
        remote(region, region, ag_s.at[piece, slot], ag_r.at[piece, slot], (dp, z1)).wait_recv()

    def first(piece):
        return (q0, qtr) if wide[piece] else (e0, eig)

    def a_z(piece):
        off, n = first(piece)
        ag_send(piece, 1, (0, off, n), (dp, z1), True)
        ag_send(piece, 0, (0, off, n), (dp, z2), True)

    def a_zf(piece):
        off, n = first(piece)
        ag_wait(piece, 0, (2, off, n))
        ag_send(piece, 2, (2, off, n), (dp, z1))

    def a_arrive(piece, k):
        off, n = first(piece)
        if k != 2:
            ag_wait(piece, {1: 1, 3: 2}[k], (k, off, n))

    def a_s(piece, k):
        a_arrive(piece, k)
        ag_send(piece, 2 + k, (k, e0, eig), (p_s, z))

    def a_f(piece, k):
        if wide[piece]:
            a_arrive(piece, k)
        else:
            ag_wait(piece, 2 + k, (k, eo, eig))
        ag_send(piece, 5 + k, (k, q0, qtr), (p_f, z))

    def a_c(piece, k):
        ag_wait(piece, 5 + k, (k, qo, qtr))
        ag_send(piece, 8 + k, (k, h0, half), (p_c, z))

    def a_done(piece, k):
        ag_wait(piece, 8 + k, (k, ho, half))

    X_TOK, X_N, X_G, X_FG, X_A, X_DI, X_KA = 0, 1, 2, 3, 4, 8, 12

    def core_send(slot, pair):
        send(lambda: (*pair(), x_s.at[slot], x_r.at[slot], (p_c, z)))

    def core_wait(slot, dst):
        remote(dst, dst, x_s.at[slot], x_r.at[slot], (p_c, z)).wait_recv()

    for j, zz in enumerate((z1, z2, z3)):
        send(lambda j=j, zz=zz: (vin, bias.at[z], b_s.at[j], b_r.at[j], (dp, zz)))
    a_z(ATT)
    a_z(INN)
    a_z(OUT)
    core_send(X_TOK, lambda: (tok, xs.at[pl.ds(rows, rows)]))

    for r in range(rows):
        seg_row = seg[pl.ds(z * rows + r, 1), :]
        live_row = live[pl.ds(z * rows + r, 1), :]
        code = jnp.where(live_row == 1, seg_row, -1)
        ids = lax.broadcasted_iota(jnp.int32, (8, seq), 0)
        key_hot = (jnp.broadcast_to(code, (8, seq)) == ids).astype(F32).astype(BF)
        query_hot = (jnp.broadcast_to(seg_row, (8, seq)) == ids).astype(F32).astype(BF)
        mask[r] = jnp.where(dot(key_hot, query_hot, TN) > 0.5, 0.0, NEG_FILL)
    acc[...] = jnp.zeros_like(acc)
    first_row = (lax.broadcasted_iota(jnp.int32, (8, seq), 0) == 0).astype(F32).astype(BF)
    loads[0].wait()

    def attend(t):
        def row(r, carry):
            x_row = xs[r]
            bias_rows = bias[t].astype(BF)[:, : 3 * ml]
            qkv[t, r] = (
                dot(wbuf[ATT, t, pl.ds(0, 3 * ml), :], x_row, NT) + dot(bias_rows, first_row, TN)
            ).astype(BF)
            for h in range(hs):
                query = qkv[t, r, pl.ds(h * DH, DH), :]
                key = qkv[t, r, pl.ds(ml + h * DH, DH), :]
                value = qkv[t, r, pl.ds(2 * ml + h * DH, DH), :]
                scores = dot(key, query, TN) * scale + mask[r]
                top = jnp.max(scores, 0, keepdims=True)
                exponent = jnp.exp(scores - top)
                total = jnp.sum(exponent, 0, keepdims=True)
                prob_t = (exponent * (1.0 / total)).astype(BF)
                prob[t, r, h] = prob_t
                ka[t, r, pl.ds(3 * ml + h * DH, DH), :] = dot(value, prob_t, NN).astype(BF)
            part = dot(ka[t, r, pl.ds(3 * ml, ml), :], wbuf[ATT, t, pl.ds(3 * ml, ml), :], TN)
            sl = pl.ds(pl.multiple_of(r * seq, 16), seq)
            acc[sl, :] = acc[sl, :] + part
            return carry

        lax.fori_loop(0, rows, row, 0)

    def attend_loop(i, carry):
        @pl.when(i == 1)
        def _():
            remote(vin, bias.at[z1], b_s.at[0], b_r.at[0], (dp, z1)).wait_recv()
            remote(vin, bias.at[z2], b_s.at[1], b_r.at[1], (dp, z2)).wait_recv()
            remote(vin, bias.at[z3], b_s.at[2], b_r.at[2], (dp, z3)).wait_recv()
            a_s(ATT, 1)
            a_zf(ATT)
            a_s(ATT, 2)
            a_f(ATT, 1)
            a_s(INN, 1)
            a_s(ATT, 3)
            a_f(ATT, 2)
            a_c(ATT, 1)
            a_zf(INN)
            a_s(INN, 2)
            a_done(ATT, 1)

        @pl.when(i == 2)
        def _():
            a_f(ATT, 3)
            a_c(ATT, 2)
            a_s(INN, 3)
            a_f(INN, 1)
            a_done(ATT, 2)

        @pl.when(i == 3)
        def _():
            a_c(ATT, 3)
            a_f(INN, 2)
            a_c(INN, 1)
            a_done(ATT, 3)

        attend(shard_of(i))
        return carry

    lax.fori_loop(0, 4, attend_loop, 0)

    rb = 32

    def norm_rows(summed):
        mean = jnp.mean(summed, -1, keepdims=True)
        centred = summed - mean
        variance = jnp.mean(centred * centred, -1, keepdims=True)
        rs_ = lax.rsqrt(variance + EPSILON)
        return centred * rs_, rs_

    def norm_back(grad, hat, rs_):
        return rs_ * (grad - jnp.mean(grad, -1, keepdims=True) - hat * jnp.mean(grad * hat, -1, keepdims=True))

    def vrow(j):
        return vin[pl.ds(j, 1), :]

    a_f(INN, 3)
    a_c(INN, 2)
    a_zf(OUT)
    a_f(OUT, 1)

    def norm1(j, carry):
        sl = pl.ds(pl.multiple_of(j * rb, 16), rb)
        per = seq // rb
        x_blk = xs[j // per, pl.ds(pl.multiple_of((j % per) * rb, 16), rb), :].astype(F32)
        hat, rs_ = norm_rows(acc[sl, :] + vrow(2) + x_blk)
        nh1[sl, :] = hat
        r1[sl, :] = jnp.broadcast_to(rs_, (rb, 128))
        nb[sl, :] = (hat * vrow(3) + vrow(4)).astype(BF)
        acc[sl, :] = jnp.zeros((rb, d), F32)
        return carry

    lax.fori_loop(0, tl // rb, norm1, 0)
    core_send(X_N, lambda: (nb.at[:, pl.ds(ho, half)], nhalf.at[pl.ds(tl, tl)]))
    nhalf[pl.ds(0, tl), :] = nb[:, pl.ds(h0, half)]

    loads[2].wait()

    def up(i, carry):
        @pl.when(i == 1)
        def _():
            a_done(INN, 1)
            a_f(OUT, 2)
            a_c(INN, 3)

        @pl.when(i == 2)
        def _():
            a_done(INN, 2)
            a_c(OUT, 1)

        @pl.when(i == 3)
        def _():
            a_done(INN, 3)
            a_c(OUT, 2)

        t = shard_of(i)
        tmp[...] = dot(nb[...], wbuf[INN, t], NN)
        b_row = bias[t, pl.ds(1, 1), :]

        def act(j, carry):
            sl = pl.ds(pl.multiple_of(j * rb, 16), rb)
            u = tmp[sl, :] + b_row
            cdf = 0.5 * (1.0 + lax.erf(u * ROOT_HALF))
            af[t, sl, :] = (u * cdf).astype(BF)
            gp[t, sl, :] = (cdf + u * (PDF_SCALE * jnp.exp(-0.5 * u * u))).astype(BF)
            return carry

        lax.fori_loop(0, tl // rb, act, 0)
        remote(af.at[t, :, pl.ds(ho, half)], asib.at[t], x_s.at[X_A + i], x_r.at[X_A + i], (p_c, z)).start()
        return carry

    lax.fori_loop(0, 4, up, 0)
    loads[3].wait()
    loads[4].wait()

    def down(i, carry):
        @pl.when(i == 1)
        def _():
            a_f(OUT, 3)
            a_done(OUT, 1)

        @pl.when(i == 2)
        def _():
            a_done(OUT, 2)
            a_c(OUT, 3)

        @pl.when(i == 3)
        def _():
            a_done(OUT, 3)

        t = shard_of(i)
        acc[...] += dot(af[t], wbuf[OUT, t], NN)
        return carry

    lax.fori_loop(0, 4, down, 0)

    vec_ref[...] = jnp.zeros_like(vec_ref)

    def add_vec(row, value):
        vec_ref[pl.ds(row, 1), :] = vec_ref[pl.ds(row, 1), :] + value

    def norm2(j, carry):
        sl = pl.ds(pl.multiple_of(j * rb, 16), rb)
        normed = nh1[sl, :] * vrow(3) + vrow(4)
        hat, rs_ = norm_rows(acc[sl, :] + vrow(5) + normed)
        out_ref[sl, :] = (hat * vrow(6) + vrow(7)).astype(BF)
        c_blk = cots[sl, :].astype(F32)
        back = norm_back(c_blk * vrow(6), hat, rs_)
        sg[sl, :] = back
        g[sl, :] = back.astype(BF)
        acc[sl, :] = jnp.zeros((rb, d), F32)
        add_vec(V_G2, jnp.sum(c_blk * hat, 0, keepdims=True))
        add_vec(V_S2, jnp.sum(c_blk, 0, keepdims=True))
        add_vec(V_EB, jnp.sum(back, 0, keepdims=True))
        return carry

    lax.fori_loop(0, tl // rb, norm2, 0)
    core_send(X_G, lambda: (g.at[pl.ds(0, tl)], g.at[pl.ds(tl, tl)]))

    fq = pl.multiple_of(f * qtr, 16)
    fo = pl.multiple_of((1 - f) * qtr, 16)
    sq = pl.multiple_of(f * qtr + s * eig, 16)
    so = pl.multiple_of(f * qtr + (1 - s) * eig, 16)

    def g_sem(piece, slot):
        return gr_s.at[piece, slot], gr_r.at[piece, slot]

    def g_send(piece, slot, pair, dev):
        send(lambda: (*pair(), *g_sem(piece, slot), dev))

    def g_wait(piece, slot, dst):
        remote(dst, dst, *g_sem(piece, slot), (dp, z1)).wait_recv()

    def add_into(dst, src, n):
        def blk(j, carry):
            sl = pl.ds(pl.multiple_of(j * 48, 16), 48)
            dst[sl, :] = (dst[sl, :].astype(F32) + src[sl, :].astype(F32)).astype(BF)
            return carry

        lax.fori_loop(0, n // 48, blk, 0)

    def fs_dynamic(piece, k):
        ssem, rsem = g_sem(piece, k)
        remote(gr.at[piece, k, pl.ds(fo, qtr)], rf.at[piece, k], ssem, rsem, (p_f, z)).start()

    def fr(piece, k):
        g_wait(piece, k, rf.at[piece, k])
        add_into(gr.at[piece, k, pl.ds(fq, qtr)], rf.at[piece, k], qtr)
        if k == 3:
            g_send(piece, 4, lambda: (gr.at[piece, 3, pl.ds(fq, qtr)], rz1.at[piece, 0]), (dp, z1))
        if k == 1:
            g_send(piece, 5, lambda: (gr.at[piece, 1, pl.ds(fq, qtr)], rz1.at[piece, 1]), (dp, z1))

    def z1r2(piece):
        g_wait(piece, 4, rz1.at[piece, 0])
        add_into(gr.at[piece, 2, pl.ds(fq, qtr)], rz1.at[piece, 0], qtr)
        g_send(piece, 6, lambda: (gr.at[piece, 2, pl.ds(fq, qtr)], rz2.at[piece]), (dp, z2))

    def z1r0(piece):
        g_wait(piece, 5, rz1.at[piece, 1])
        add_into(gr.at[piece, 0, pl.ds(fq, qtr)], rz1.at[piece, 1], qtr)

    def z2r(piece):
        g_wait(piece, 6, rz2.at[piece])
        add_into(gr.at[piece, 0, pl.ds(fq, qtr)], rz2.at[piece], qtr)
        g_send(piece, 7, lambda: (gr.at[piece, 0, pl.ds(so, eig)], rs.at[piece]), (p_s, z))

    def sr(piece):
        g_wait(piece, 7, rs.at[piece])
        mine = gr.at[piece, 0, pl.ds(sq, eig)]
        add_into(mine, rs.at[piece], eig)
        for j, partner in enumerate(extra):
            cp = remote(mine, rx.at[piece, j], e_s.at[piece, j], e_r.at[piece, j], (partner, z))
            cp.start()
            cp.wait()
            add_into(mine, rx.at[piece, j], eig)
        g_send(
            piece, 8, lambda: (gr.at[piece, 0, pl.ds(sq, eig)], grad_ref.at[piece, pl.ds(e0, eig)]), (p_s, z)
        )
        cp = pltpu.make_async_copy(mine, grad_ref.at[piece, pl.ds(e0, eig)], loc_sem.at[5 + piece])
        cp.start()
        return cp

    local_out = {}

    def sr_(piece):
        local_out[piece] = sr(piece)

    def s2r(piece):
        g_wait(piece, 8, grad_ref.at[piece, pl.ds(eo, eig)])
        local_out[piece].wait()
        g_send(piece, 9, lambda: (grad_ref.at[piece, pl.ds(q0, qtr)],) * 2, (p_f, z))

    def f2r(piece):
        g_wait(piece, 9, grad_ref.at[piece, pl.ds(qo, qtr)])
        g_send(piece, 10, lambda: (grad_ref.at[piece, pl.ds(h0, half)],) * 2, (p_c, z))

    def c2r(piece):
        g_wait(piece, 10, grad_ref.at[piece, pl.ds(ho, half)])

    def order(i):
        return 3 - 2 * (i % 2) - i // 2

    def ffn_back(i, carry):
        @pl.when(i < 4)
        def _():
            k = order(i)
            t = shard_of(k)
            tmp[...] = dot(g[pl.ds(0, tl), :], wbuf[OUT, t], NT)

            def act(j, carry):
                sl = pl.ds(pl.multiple_of(j * rb, 16), rb)
                blk = (tmp[sl, :] * gp[t, sl, :].astype(F32)).astype(BF)
                di[t, sl, :] = blk
                return carry + jnp.sum(blk.astype(F32), 0, keepdims=True)

            vec_ref[pl.ds(4 + t, 1), :] = lax.fori_loop(0, tl // rb, act, jnp.zeros((1, d), F32))
            remote(
                di.at[t, pl.ds(0, tl)], di.at[t, pl.ds(tl, tl)], x_s.at[X_DI + k], x_r.at[X_DI + k], (p_c, z)
            ).start()

            @pl.when(i == 0)
            def _():
                core_wait(X_G, g.at[pl.ds(tl, tl)])
                core_wait(X_N, nhalf.at[pl.ds(tl, tl)])

            core_wait(X_A + k, asib.at[t])
            al[pl.ds(0, tl), :] = af[t, :, pl.ds(h0, half)]
            al[pl.ds(tl, tl), :] = asib[t]
            gr[OUT, k] = dot(al[...], g[...], TN).astype(BF)
            fs_dynamic(OUT, k)
            acc[...] += dot(di[t, pl.ds(0, tl), :], wbuf[INN, t], NT)

        @pl.when(i == 2)
        def _():
            fr(OUT, 3)

        @pl.when(i == 4)
        def _():
            fr(OUT, 1)

        @pl.when(i > 0)
        def _():
            k = order(i - 1)
            t = shard_of(k)
            core_wait(X_DI + k, di.at[t, pl.ds(tl, tl)])
            gr[INN, k] = dot(nhalf[...], di[t], TN).astype(BF)
            fs_dynamic(INN, k)

        return carry

    lax.fori_loop(0, 5, ffn_back, 0)

    def norm1_back(j, carry):
        sl = pl.ds(pl.multiple_of(j * rb, 16), rb)
        per = seq // rb
        hat = nh1[sl, :]
        total = acc[sl, :] + sg[sl, :]
        back = norm_back(total * vrow(3), hat, r1[sl, 0:1])
        fgf[sl, :] = back
        fg[j // per, pl.ds(pl.multiple_of((j % per) * rb, 16), rb), :] = back.astype(BF)
        acc[sl, :] = jnp.zeros((rb, d), F32)
        add_vec(V_G1, jnp.sum(total * hat, 0, keepdims=True))
        add_vec(V_S1, jnp.sum(total, 0, keepdims=True))
        add_vec(V_OB, jnp.sum(back, 0, keepdims=True))
        return carry

    lax.fori_loop(0, tl // rb, norm1_back, 0)
    core_send(X_FG, lambda: (fg.at[pl.ds(0, rows)], fg.at[pl.ds(rows, rows)]))
    ones = jnp.ones((8, seq), BF)

    def attend_back(t):
        def row(r, carry):
            dctx = dot(wbuf[ATT, t, pl.ds(3 * ml, ml), :], fg[r], NT).astype(BF)
            for h in range(hs):
                query = qkv[t, r, pl.ds(h * DH, DH), :]
                key = qkv[t, r, pl.ds(ml + h * DH, DH), :]
                value = qkv[t, r, pl.ds(2 * ml + h * DH, DH), :]
                prob_t = prob[t, r, h]
                grad = dctx[h * DH : (h + 1) * DH]
                ka[t, r, pl.ds(2 * ml + h * DH, DH), :] = dot(grad, prob_t, NT).astype(BF)
                prob_grad = dot(value, grad, TN)
                wide_prob = prob_t.astype(F32)
                inner = jnp.sum(wide_prob * prob_grad, 0, keepdims=True)
                score_grad = (wide_prob * (prob_grad - inner)).astype(BF)
                ka[t, r, pl.ds(h * DH, DH), :] = (dot(key, score_grad, NN) * scale).astype(BF)
                ka[t, r, pl.ds(ml + h * DH, DH), :] = (dot(query, score_grad, NT) * scale).astype(BF)
            grads = ka[t, r, pl.ds(0, 3 * ml), :]
            vec_ref[pl.ds(t, 1), pl.ds(0, 3 * ml)] += dot(ones, grads, NT)[0:1]
            sl = pl.ds(pl.multiple_of(r * seq, 16), seq)
            acc[sl, :] = acc[sl, :] + dot(grads, wbuf[ATT, t, pl.ds(0, 3 * ml), :], TN)
            return carry

        lax.fori_loop(0, rows, row, 0)

    def att_back(i, carry):
        @pl.when(i < 4)
        def _():
            k = order(i)
            t = shard_of(k)
            attend_back(t)
            remote(
                ka.at[t, :, pl.ds(ho, half)], ks.at[t], x_s.at[X_KA + k], x_r.at[X_KA + k], (p_c, z)
            ).start()

        @pl.when(i == 0)
        def _():
            core_wait(X_TOK, xs.at[pl.ds(rows, rows)])
            core_wait(X_FG, fg.at[pl.ds(rows, rows)])
            fr(OUT, 2)
            fr(OUT, 0)

        @pl.when(i == 1)
        def _():
            z1r2(OUT)
            fr(INN, 3)

        @pl.when(i == 2)
        def _():
            z1r0(OUT)
            fr(INN, 1)

        @pl.when(i == 3)
        def _():
            z2r(OUT)
            fr(INN, 2)

        @pl.when(i == 4)
        def _():
            fr(INN, 0)
            z1r2(INN)

        @pl.when(i > 0)
        def _():
            k = order(i - 1)
            t = shard_of(k)
            core_wait(X_KA + k, ks.at[t])
            for j in range(2):
                rowsel = pl.ds(pl.multiple_of(h0 + j * ml, 16), ml)
                use = c * j
                total = jnp.zeros((ml, d), F32)
                for r in range(rows):
                    right_own = xs[r] if j == 0 else jnp.where(use == 1, fg[r], xs[r])
                    right_sib = xs[rows + r] if j == 0 else jnp.where(use == 1, fg[rows + r], xs[rows + r])
                    total += dot(ka[t, r, rowsel, :], right_own, NN)
                    total += dot(ks[t, r, pl.ds(j * ml, ml), :], right_sib, NN)
                gr[ATT, k, pl.ds(j * ml, ml), :] = total.astype(BF)
            fs_dynamic(ATT, k)

        return carry

    lax.fori_loop(0, 5, att_back, 0)

    def finish(j, carry):
        sl = pl.ds(pl.multiple_of(j * rb, 16), rb)
        dx_ref[sl, :] = (fgf[sl, :] + acc[sl, :]).astype(BF)
        return carry

    lax.fori_loop(0, tl // rb, finish, 0)

    partners = [(p_c, z), (p_f, z), (p_s, z)] + [(e, z) for e in extra] + [(dp, z1), (dp, z2)]

    def v_step(j):
        cp = remote(vec_ref, vrecv.at[j], v_s.at[j], v_r.at[j], partners[j])
        cp.start()
        return cp

    def v_end(cp, j):
        cp.wait()
        vec_ref[...] += vrecv[j]

    v0 = v_step(0)
    sr_(OUT)
    z1r0(INN)
    v_end(v0, 0)
    v1 = v_step(1)
    fr(ATT, 3)
    z2r(INN)
    fr(ATT, 1)
    s2r(OUT)
    v_end(v1, 1)
    v2 = v_step(2)
    fr(ATT, 2)
    sr_(INN)
    f2r(OUT)
    fr(ATT, 0)
    v_end(v2, 2)
    v3 = v_step(3)
    z1r2(ATT)
    s2r(INN)
    z1r0(ATT)
    v_end(v3, 3)
    v4 = v_step(4)
    f2r(INN)
    z2r(ATT)
    v_end(v4, 4)
    for j in range(5, len(partners)):
        v_end(v_step(j), j)
    sr_(ATT)
    s2r(ATT)
    f2r(ATT)
    c2r(OUT)
    c2r(INN)
    c2r(ATT)

    for make in pending:
        remote(*make()).wait_send()

    def sent(k, carry):
        t = shard_of(k)
        remote(af.at[t, :, pl.ds(ho, half)], asib.at[t], x_s.at[X_A + k], x_r.at[X_A + k], (p_c, z)).wait_send()
        remote(
            di.at[t, pl.ds(0, tl)], di.at[t, pl.ds(tl, tl)], x_s.at[X_DI + k], x_r.at[X_DI + k], (p_c, z)
        ).wait_send()
        remote(ka.at[t, :, pl.ds(ho, half)], ks.at[t], x_s.at[X_KA + k], x_r.at[X_KA + k], (p_c, z)).wait_send()
        for piece in range(3):
            ssem, rsem = g_sem(piece, k)
            remote(gr.at[piece, k, pl.ds(fo, qtr)], rf.at[piece, k], ssem, rsem, (p_f, z)).wait_send()
        return carry

    lax.fori_loop(0, 4, sent, 0)


def spread_kernel(
    ml, grads, vec, out_in, dx_in,
    out_ref, dx_ref, gq, gk, gv, go, gi, ge, bq, bv, bo, g1, s1, bi, be, g2, s2,
    grads_v, vec_v, att_v, big_v, io_v, sem,
):
    z = lax.axis_index("mp")
    moves = [
        pltpu.make_async_copy(grads.at[1], grads_v.at[1], sem.at[0]),
        pltpu.make_async_copy(grads.at[2], grads_v.at[2], sem.at[1]),
        pltpu.make_async_copy(grads.at[0], grads_v.at[0], sem.at[2]),
        pltpu.make_async_copy(vec, vec_v, sem.at[3]),
        pltpu.make_async_copy(out_in, io_v.at[0], sem.at[4]),
        pltpu.make_async_copy(dx_in, io_v.at[1], sem.at[5]),
    ]
    for cp in moves:
        cp.start()
    outs = []
    for j, ref in enumerate((gi, ge)):
        moves[j].wait()
        big_v[j] = grads_v[j + 1].astype(F32)
        cp = pltpu.make_async_copy(big_v.at[j], ref, sem.at[6 + j])
        cp.start()
        outs.append(cp)
    moves[2].wait()
    att_v[...] = grads_v[0].astype(F32)
    for j, ref in enumerate((gq, gk, gv, go)):
        cp = pltpu.make_async_copy(att_v.at[pl.ds(j * ml, ml)], ref, sem.at[8 + j])
        cp.start()
        outs.append(cp)
    for j, ref in enumerate((out_ref, dx_ref)):
        moves[4 + j].wait()
        cp = pltpu.make_async_copy(io_v.at[j], ref, sem.at[12 + j])
        cp.start()
        outs.append(cp)
    moves[3].wait()
    bq[...] = vec_v[pl.ds(z, 1), pl.ds(0, ml)].reshape(ml)
    bv[...] = vec_v[pl.ds(z, 1), pl.ds(2 * ml, ml)].reshape(ml)
    bi[...] = vec_v[pl.ds(4 + z, 1), :].reshape(4 * ml)
    for row, ref in ((V_OB, bo), (V_G1, g1), (V_S1, s1), (V_EB, be), (V_G2, g2), (V_S2, s2)):
        ref[...] = vec_v[pl.ds(row, 1), :].reshape(4 * ml)
    for cp in outs:
        cp.wait()


def per_device(
    n_dp,
    tokens, segment_ids, live_mask, query_weight, key_weight, value_weight, query_bias, value_bias,
    output_weight, output_bias, first_gain, first_shift, inner_weight, inner_bias, outer_weight,
    outer_bias, second_gain, second_shift, cotangent,
):
    tl, d = tokens.shape
    seq_rows, seq = segment_ids.shape
    rows = tl // seq
    ml = query_weight.shape[1]
    half, qtr, eig = d // 2, d // 4, d // 8
    bits = n_dp.bit_length() - 1
    n_extra = max(bits - 3, 1)
    n_vec = bits + 2
    cfg = {"dp": n_dp, "d": d, "seq": seq, "rows": rows}
    vmem = pl.BlockSpec(memory_space=pltpu.VMEM)
    hbm = pl.BlockSpec(memory_space=pl.ANY)
    scratch = [
        pltpu.VMEM((3, 4, d, d), BF),
        pltpu.VMEM((4, 8, d), F32),
        pltpu.VMEM((2 * rows, seq, d), BF),
        pltpu.VMEM((tl, d), BF),
        pltpu.VMEM((4, rows, 3 * ml, seq), BF),
        pltpu.VMEM((4, rows, d, seq), BF),
        pltpu.VMEM((4, rows, half, seq), BF),
        pltpu.VMEM((4, rows, ml // DH, seq, seq), BF),
        pltpu.VMEM((rows, seq, seq), F32),
        pltpu.VMEM((tl, d), F32),
        pltpu.VMEM((tl, d), F32),
        pltpu.VMEM((tl, d), F32),
        pltpu.VMEM((tl, 128), F32),
        pltpu.VMEM((tl, d), BF),
        pltpu.VMEM((2 * tl, half), BF),
        pltpu.VMEM((4, tl, d), BF),
        pltpu.VMEM((4, tl, half), BF),
        pltpu.VMEM((2 * tl, half), BF),
        pltpu.VMEM((4, tl, d), BF),
        pltpu.VMEM((2 * tl, d), BF),
        pltpu.VMEM((tl, d), F32),
        pltpu.VMEM((4, 2 * tl, d), BF),
        pltpu.VMEM((2 * rows, seq, d), BF),
        pltpu.VMEM((tl, d), F32),
        pltpu.VMEM((3, 4, half, d), BF),
        pltpu.VMEM((3, 4, qtr, d), BF),
        pltpu.VMEM((3, 2, qtr, d), BF),
        pltpu.VMEM((3, qtr, d), BF),
        pltpu.VMEM((3, eig, d), BF),
        pltpu.VMEM((3, n_extra, eig, d), BF) if bits > 3 else pltpu.VMEM((1, 1, 16, 128), BF),
        pltpu.VMEM((n_vec, 16, d), F32),
        pltpu.VMEM((8, d), F32),
        pltpu.SemaphoreType.DMA((11,)),
        pltpu.SemaphoreType.DMA((3, 12)),
        pltpu.SemaphoreType.DMA((3, 12)),
        pltpu.SemaphoreType.DMA((3, 11)),
        pltpu.SemaphoreType.DMA((3, 11)),
        pltpu.SemaphoreType.DMA((16,)),
        pltpu.SemaphoreType.DMA((16,)),
        pltpu.SemaphoreType.DMA((3,)),
        pltpu.SemaphoreType.DMA((3,)),
        pltpu.SemaphoreType.DMA((n_vec,)),
        pltpu.SemaphoreType.DMA((n_vec,)),
        pltpu.SemaphoreType.DMA((3, n_extra)),
        pltpu.SemaphoreType.DMA((3, n_extra)),
    ]
    out, dx, grads, vec = pl.pallas_call(
        functools.partial(layer_kernel, cfg),
        out_shape=(
            jax.ShapeDtypeStruct((tl, d), BF),
            jax.ShapeDtypeStruct((tl, d), BF),
            jax.ShapeDtypeStruct((3, d, d), BF),
            jax.ShapeDtypeStruct((16, d), F32),
        ),
        in_specs=[hbm] * 8 + [vmem] * 11,
        out_specs=(vmem, vmem, hbm, vmem),
        scratch_shapes=scratch,
        compiler_params=pltpu.CompilerParams(
            collective_id=0, has_side_effects=True, vmem_limit_bytes=62 * 1024 * 1024
        ),
        name="layer",
    )(
        tokens.reshape(rows, seq, d), cotangent, query_weight.T, key_weight.T, value_weight.T, output_weight,
        inner_weight, outer_weight, query_bias, value_bias, inner_bias, output_bias, first_gain, first_shift,
        outer_bias, second_gain, second_shift, segment_ids, live_mask,
    )
    ff = inner_weight.shape[1]
    out, dx, gq, gk, gv, go, gi, ge, bq, bv, bo, g1, s1, bi, be, g2, s2 = pl.pallas_call(
        functools.partial(spread_kernel, ml),
        out_shape=tuple(
            jax.ShapeDtypeStruct(shape, dtype)
            for shape, dtype in [((tl, d), BF)] * 2
            + [((ml, d), F32)] * 4
            + [((d, ff), F32), ((ff, d), F32)]
            + [((ml,), F32)] * 2
            + [((d,), F32)] * 7
        ),
        in_specs=[hbm] * 4,
        out_specs=(hbm,) * 8 + (vmem,) * 9,
        scratch_shapes=[
            pltpu.VMEM((3, d, d), BF),
            pltpu.VMEM((16, d), F32),
            pltpu.VMEM((d, d), F32),
            pltpu.VMEM((2, d, d), F32),
            pltpu.VMEM((2, tl, d), BF),
            pltpu.SemaphoreType.DMA((14,)),
        ],
        compiler_params=pltpu.CompilerParams(vmem_limit_bytes=60 * 1024 * 1024),
        name="spread",
    )(grads, vec, out, dx)
    return out, dx, gq.T, gk.T, gv.T, bq, bv, go, bo, g1, s1, gi, bi, ge, be, g2, s2


def solution(mesh):
    tok, shared = P(("dp", "mp"), None), P()
    cols, rows, vec = P(None, "mp"), P("mp", None), P("mp")
    in_specs = (
        tok, P("dp", None), P("dp", None), cols, cols, cols, vec, vec, rows, shared, shared, shared,
        cols, vec, rows, shared, shared, shared, tok,
    )
    out_specs = (
        tok, tok, cols, cols, cols, vec, vec, rows, shared, shared, shared, cols, vec, rows,
        shared, shared, shared,
    )
    return jax.shard_map(
        functools.partial(per_device, mesh.shape["dp"]),
        mesh=mesh,
        in_specs=in_specs,
        out_specs=out_specs,
        check_vma=False,
    )
```

```python
import functools

import jax
import jax.numpy as jnp
from jax import lax
from jax.experimental import pallas as pl
from jax.experimental.pallas import tpu as pltpu
from jax.sharding import PartitionSpec as P

DH = 64
EPSILON = 1e-06
NEG_FILL = -1000000000.0
ROOT_HALF = 0.7071067811865476
PDF_SCALE = 0.3989422804014327
BF = jnp.bfloat16
F32 = jnp.float32
MESH = pl.DeviceIdType.MESH

NN = (((1,), (0,)), ((), ()))
NT = (((1,), (1,)), ((), ()))
TN = (((0,), (0,)), ((), ()))

ATT, INN, OUT = 0, 1, 2
WIDE = (False, False, True)
CHAIN = ("FS12", "F12S", "F12S")
PLAN = {
    "x0": {
        0: (("az2", 0, 0), ("az1", 0, 0),),
    },
    "att": {
        0: (("zf", 0, 0), ("s", 0, 2),),
        1: (("s", 0, 1), ("az1", 1, 0), ("f", 0, 2), ("az2", 1, 0),),
        2: (("f", 0, 1), ("az1", 2, 0), ("s", 1, 1), ("f", 1, 1), ("s", 0, 3), ("c", 0, 1), ("d", 0, 1), ("zf", 1, 0), ("c", 0, 2), ("s", 1, 2), ("az2", 2, 0), ("d", 0, 2), ("f", 2, 1),),
        3: (("f", 0, 3), ("c", 1, 1), ("f", 1, 2),),
        4: (("d", 1, 1),),
        5: (("s", 1, 3), ("c", 2, 1),),
        6: (("c", 0, 3), ("zf", 2, 0), ("c", 1, 2), ("d", 0, 3), ("f", 2, 2),),
        7: (("f", 1, 3),),
    },
    "n1": {
    },
    "up": {
        0: (("d", 2, 1), ("f", 2, 3),),
        2: (("c", 1, 3), ("d", 1, 2), ("c", 2, 2),),
        3: (("c", 2, 3), ("d", 1, 3),),
    },
    "dn": {
        1: (("d", 2, 2),),
        3: (("d", 2, 3),),
    },
    "l2": {
    },
    "da": {
    },
    "gwo": {
        2: (("gFr", 2, 3), ("g1s", 2, 3), ("gFs", 1, 3),),
    },
    "dn2": {
        0: (("gFs", 2, 3),),
        1: (("gFs", 2, 1),),
        3: (("gFr", 2, 1),),
    },
    "gwi": {
        1: (("gFs", 2, 2),),
        2: (("g1s", 2, 1),),
        3: (("gFs", 1, 2),),
    },
    "l1b": {
        0: (("gFs", 1, 0),),
    },
    "ab": {
        0: (("gFr", 1, 3), ("gFr", 2, 2), ("g1s", 1, 3), ("gFs", 2, 0), ("g1r", 2, 2), ("g2s", 2, 2), ("gFs", 1, 1),),
        4: (("gFs", 0, 3),),
        6: (("gFs", 0, 1), ("gFr", 1, 1), ("gFr", 2, 0), ("g1s", 1, 1), ("gFr", 1, 2),),
        7: (("g1r", 1, 2), ("gFr", 0, 3), ("g1r", 2, 0), ("gSs", 0, 3), ("g2s", 1, 2), ("g2r", 2, 0), ("gSs", 2, 0),),
    },
    "gwa": {
        3: (("gFr", 0, 1), ("gFs", 0, 2), ("gSs", 0, 1),),
    },
    "fin": {
    },
    "end": {
        0: (("gSr", 2, 0), ("vs", 0, 0), ("gSr", 0, 3), ("vr", 0, 0), ("gFr", 1, 0), ("gS2s", 2, 0), ("gFr", 0, 2), ("vs", 1, 0), ("gFs", 0, 0), ("gSs", 0, 2), ("g1s", 0, 3), ("g1r", 1, 0), ("vr", 1, 0), ("g2r", 1, 0), ("gS2r", 2, 0), ("gSr", 0, 2), ("gSs", 1, 0), ("g1r", 0, 2), ("gFr", 0, 0), ("gSr", 0, 1), ("g2s", 0, 2), ("gSs", 0, 0), ("g1s", 0, 1), ("vs", 2, 0), ("gSr", 1, 0), ("gF2r", 2, 0), ("gS2s", 1, 0), ("gSr", 0, 0), ("g1r", 0, 0), ("g2r", 0, 0), ("gS2s", 0, 0), ("gS2r", 1, 0), ("gC2r", 2, 0), ("gS2r", 0, 0), ("vr", 2, 0), ("vs", 3, 0), ("vr", 3, 0), ("gF2r", 1, 0), ("vs", 4, 0), ("gF2r", 0, 0), ("vr", 4, 0), ("gC2r", 0, 0), ("gC2r", 1, 0),),
    },
}
V_OB, V_G1, V_S1, V_EB, V_G2, V_S2 = 8, 9, 10, 11, 12, 13


def dot(left, right, dims):
    return lax.dot_general(left, right, dims, preferred_element_type=F32)


def layer_kernel(
    cfg,
    tok, cot, wq, wk, wv, wo, wi, wout, bq, bv, bi, bo, g1, s1, be, g2, s2, seg, live,
    out_ref, dx_ref, grad_ref, vec_ref,
    wbuf, bias, xs, cots, qkv, ka, ks, prob, mask, acc, tmp, nh1, r1,
    nb, nhalf, af, asib, al, gp, g, sg, di, fg, fgf,
    gr, rf, rz, rs, rx, vrecv, vin,
    loc_sem, ag_s, ag_r, gr_s, gr_r, x_s, x_r, b_s, b_r, v_s, v_r, e_s, e_r,
):
    n_dp, d, seq, rows = cfg["dp"], cfg["d"], cfg["seq"], cfg["rows"]
    tl = seq * rows
    ml = d // 4
    hs = ml // DH
    half, qtr, eig = d // 2, d // 4, d // 8
    scale = DH ** (-0.5)
    bits = n_dp.bit_length() - 1
    dp, z = lax.axis_index("dp"), lax.axis_index("mp")
    c = dp % 2
    df = 2 + 2 * c
    ds_ = 6 - df
    f, s = (dp // df) % 2, (dp // ds_) % 2
    p_f, p_s, p_c = dp + df * (1 - 2 * f), dp + ds_ * (1 - 2 * s), dp + 1 - 2 * c
    z0, zh = z % 2, z // 2
    z1, z2, z3 = z + 1 - 2 * z0, z + 2 - 4 * zh, 3 - z
    h0 = pl.multiple_of(c * half, 128)
    ho = pl.multiple_of((1 - c) * half, 128)
    q0 = pl.multiple_of(c * half + f * qtr, 16)
    e0 = pl.multiple_of(c * half + f * qtr + s * eig, 16)
    qo = pl.multiple_of(c * half + (1 - f) * qtr, 16)
    eo = pl.multiple_of(c * half + f * qtr + (1 - s) * eig, 16)
    shard = (z, z1, z2, z3)

    def shard_of(k):
        k0, kh = k % 2, k // 2
        return z0 + k0 - 2 * z0 * k0 + 2 * (zh + kh - 2 * zh * kh)

    def remote(src, dst, ssem, rsem, dev):
        return pltpu.make_async_remote_copy(
            src_ref=src, dst_ref=dst, send_sem=ssem, recv_sem=rsem, device_id=dev, device_id_type=MESH
        )

    pending = []

    def send(make):
        remote(*make()).start()
        pending.append(make)

    loads = [
        pltpu.make_async_copy(tok, xs.at[pl.ds(0, rows)], loc_sem.at[0]),
        pltpu.make_async_copy(wo, wbuf.at[ATT, z, pl.ds(3 * ml, ml)], loc_sem.at[1]),
        pltpu.make_async_copy(wi, wbuf.at[INN, z], loc_sem.at[2]),
        pltpu.make_async_copy(wout, wbuf.at[OUT, z], loc_sem.at[3]),
        pltpu.make_async_copy(cot, cots, loc_sem.at[4]),
    ] + [
        pltpu.make_async_copy(ref, wbuf.at[ATT, z, pl.ds(j * ml, ml)], loc_sem.at[8 + j])
        for j, ref in enumerate((wq, wk, wv))
    ]
    for cp in loads:
        cp.start()
    barrier = pltpu.get_barrier_semaphore()
    extra = [dp + (1 << b) * (1 - 2 * ((dp // (1 << b)) % 2)) for b in range(3, bits)]
    greet = [(p_c, z), (p_f, z), (p_s, z), (dp, z1), (dp, z2), (dp, z3)] + [(e, z) for e in extra]
    for dev in greet:
        pl.semaphore_signal(barrier, inc=1, device_id=dev, device_id_type=MESH)
    vin[...] = jnp.zeros_like(vin)
    vin[pl.ds(0, 1), pl.ds(0, ml)] = bq[...].astype(F32).reshape(1, ml)
    vin[pl.ds(0, 1), pl.ds(2 * ml, ml)] = bv[...].astype(F32).reshape(1, ml)
    for j, ref in enumerate((bi, bo, g1, s1, be, g2, s2)):
        vin[pl.ds(j + 1, 1), :] = ref[...].astype(F32).reshape(1, d)
    bias[z] = vin[...]
    for j in (1, 5, 6, 7):
        loads[j].wait()
    pl.semaphore_wait(barrier, len(greet))

    def own(piece, off, n):
        if piece == ATT:
            return wbuf.at[ATT, z, pl.ds(off, n)]
        return (wi, wout)[piece - 1].at[pl.ds(off, n)]

    def reg(piece, k, off, n):
        return wbuf.at[piece, shard[k], pl.ds(off, n)]

    def ag_send(piece, slot, where, dev, mine=False):
        def make():
            region = reg(piece, *where)
            src = own(piece, *where[1:]) if mine else region
            return src, region, ag_s.at[piece, slot], ag_r.at[piece, slot], dev

        send(make)

    def ag_wait(piece, slot, where):
        region = reg(piece, *where)
        remote(region, region, ag_s.at[piece, slot], ag_r.at[piece, slot], (dp, z1)).wait_recv()

    def first(piece):
        return (q0, qtr) if WIDE[piece] else (e0, eig)

    def a_z1(piece, _):
        ag_send(piece, 1, (0, *first(piece)), (dp, z1), True)

    def a_z2(piece, _):
        ag_send(piece, 0, (0, *first(piece)), (dp, z2), True)

    def a_zf(piece, _):
        ag_wait(piece, 0, (2, *first(piece)))
        ag_send(piece, 2, (2, *first(piece)), (dp, z1))

    def a_arrive(piece, k):
        if k != 2:
            ag_wait(piece, {1: 1, 3: 2}[k], (k, *first(piece)))

    def a_s(piece, k):
        a_arrive(piece, k)
        ag_send(piece, 2 + k, (k, e0, eig), (p_s, z))

    def a_f(piece, k):
        if WIDE[piece]:
            a_arrive(piece, k)
        else:
            ag_wait(piece, 2 + k, (k, eo, eig))
        ag_send(piece, 5 + k, (k, q0, qtr), (p_f, z))

    def a_c(piece, k):
        ag_wait(piece, 5 + k, (k, qo, qtr))
        ag_send(piece, 8 + k, (k, h0, half), (p_c, z))

    def a_d(piece, k):
        ag_wait(piece, 8 + k, (k, ho, half))

    X_TOK, X_N, X_G, X_FG, X_A, X_DI, X_KA = 0, 1, 2, 3, 4, 8, 12

    def core_send(slot, pair):
        send(lambda: (*pair(), x_s.at[slot], x_r.at[slot], (p_c, z)))

    def core_wait(slot, dst):
        remote(dst, dst, x_s.at[slot], x_r.at[slot], (p_c, z)).wait_recv()

    fq = pl.multiple_of(f * qtr, 16)
    fo = pl.multiple_of((1 - f) * qtr, 16)
    sq = pl.multiple_of(f * qtr + s * eig, 16)
    so = pl.multiple_of(f * qtr + (1 - s) * eig, 16)

    def g_sem(piece, slot):
        return gr_s.at[piece, slot], gr_r.at[piece, slot]

    def g_send(piece, slot, pair, dev):
        send(lambda: (*pair(), *g_sem(piece, slot), dev))

    def g_wait(piece, slot, dst):
        remote(dst, dst, *g_sem(piece, slot), (dp, z1)).wait_recv()

    def add_into(dst, src, n):
        def blk(j, carry):
            sl = pl.ds(pl.multiple_of(j * 48, 16), 48)
            dst[sl, :] = (dst[sl, :].astype(F32) + src[sl, :].astype(F32)).astype(BF)
            return carry

        lax.fori_loop(0, n // 48, blk, 0)

    def part(piece, stage):
        chain = CHAIN[piece]
        return (sq, eig) if chain.index("S") < chain.index(stage) else (fq, qtr)

    def g_fs(piece, k):
        g_send(piece, k, lambda: (gr.at[piece, k, pl.ds(fo, qtr)], rf.at[piece, k]), (p_f, z))

    def g_fr(piece, k):
        g_wait(piece, k, rf.at[piece, k])
        add_into(gr.at[piece, k, pl.ds(fq, qtr)], rf.at[piece, k], qtr)

    def g_ss(piece, k):
        g_send(piece, 4 + k, lambda: (gr.at[piece, k, pl.ds(so, eig)], rs.at[piece, k]), (p_s, z))

    def g_sr(piece, k):
        g_wait(piece, 4 + k, rs.at[piece, k])
        add_into(gr.at[piece, k, pl.ds(sq, eig)], rs.at[piece, k], eig)

    def g_1s(piece, k):
        off, n = part(piece, "1")
        slot = 0 if k == 3 else 1
        g_send(
            piece, 8 + slot, lambda: (gr.at[piece, k, pl.ds(off, n)], rz.at[piece, slot, pl.ds(0, n)]), (dp, z1)
        )

    def g_zr(piece, k, slot, stage):
        off, n = part(piece, stage)
        g_wait(piece, 8 + slot, rz.at[piece, slot, pl.ds(0, n)])
        add_into(gr.at[piece, k, pl.ds(off, n)], rz.at[piece, slot, pl.ds(0, n)], n)

    def g_1r(piece, k):
        g_zr(piece, k, 0 if k == 2 else 1, "1")

    def g_2s(piece, k):
        off, n = part(piece, "2")
        g_send(piece, 10, lambda: (gr.at[piece, 2, pl.ds(off, n)], rz.at[piece, 2, pl.ds(0, n)]), (dp, z2))

    def g_2r(piece, k):
        g_zr(piece, 0, 2, "2")

    def local_out(piece):
        return pltpu.make_async_copy(
            gr.at[piece, 0, pl.ds(sq, eig)], grad_ref.at[piece, pl.ds(e0, eig)], loc_sem.at[5 + piece]
        )

    def g_s2s(piece, _):
        for j, partner in enumerate(extra):
            cp = remote(
                gr.at[piece, 0, pl.ds(sq, eig)], rx.at[piece, j], e_s.at[piece, j], e_r.at[piece, j], (partner, z)
            )
            cp.start()
            cp.wait()
            add_into(gr.at[piece, 0, pl.ds(sq, eig)], rx.at[piece, j], eig)
        g_send(
            piece, 11, lambda: (gr.at[piece, 0, pl.ds(sq, eig)], grad_ref.at[piece, pl.ds(e0, eig)]), (p_s, z)
        )
        local_out(piece).start()

    def g_s2r(piece, _):
        g_wait(piece, 11, grad_ref.at[piece, pl.ds(eo, eig)])
        local_out(piece).wait()
        g_send(piece, 12, lambda: (grad_ref.at[piece, pl.ds(q0, qtr)],) * 2, (p_f, z))

    def g_f2r(piece, _):
        g_wait(piece, 12, grad_ref.at[piece, pl.ds(qo, qtr)])
        g_send(piece, 13, lambda: (grad_ref.at[piece, pl.ds(h0, half)],) * 2, (p_c, z))

    def g_c2r(piece, _):
        g_wait(piece, 13, grad_ref.at[piece, pl.ds(ho, half)])

    partners = [(p_c, z), (p_f, z), (p_s, z), (dp, z1), (dp, z2)] + [(e, z) for e in extra]

    def v_copy(j):
        return remote(vec_ref, vrecv.at[j], v_s.at[j], v_r.at[j], partners[j])

    def v_send(j, _):
        v_copy(j).start()

    def v_recv(j, _):
        v_copy(j).wait()
        vec_ref[...] += vrecv[j]

    events = {
        "az1": a_z1, "az2": a_z2, "zf": a_zf, "s": a_s, "f": a_f, "c": a_c, "d": a_d,
        "gFs": g_fs, "gFr": g_fr, "gSs": g_ss, "gSr": g_sr, "g1s": g_1s, "g1r": g_1r, "g2s": g_2s, "g2r": g_2r,
        "gS2s": g_s2s, "gS2r": g_s2r, "gF2r": g_f2r, "gC2r": g_c2r, "vs": v_send, "vr": v_recv,
    }

    def do(listed):
        for kind, piece, k in listed:
            events[kind](piece, k)

    def at(place, index):
        for n, listed in PLAN.get(place, {}).items():
            pl.when(index == n)(functools.partial(do, listed))

    def once(place):
        do(PLAN.get(place, {}).get(0, ()))

    for j, zz in enumerate((z1, z2, z3)):
        send(lambda j=j, zz=zz: (vin, bias.at[z], b_s.at[j], b_r.at[j], (dp, zz)))
    once("x0")
    core_send(X_TOK, lambda: (tok, xs.at[pl.ds(rows, rows)]))

    for r in range(rows):
        seg_row = seg[pl.ds(z * rows + r, 1), :]
        live_row = live[pl.ds(z * rows + r, 1), :]
        code = jnp.where(live_row == 1, seg_row, -1)
        ids = lax.broadcasted_iota(jnp.int32, (8, seq), 0)
        key_hot = (jnp.broadcast_to(code, (8, seq)) == ids).astype(F32).astype(BF)
        query_hot = (jnp.broadcast_to(seg_row, (8, seq)) == ids).astype(F32).astype(BF)
        mask[r] = jnp.where(dot(key_hot, query_hot, TN) > 0.5, 0.0, NEG_FILL)
    acc[...] = jnp.zeros_like(acc)
    first_row = (lax.broadcasted_iota(jnp.int32, (8, seq), 0) == 0).astype(F32).astype(BF)
    loads[0].wait()

    def attend(i, carry):
        t = shard_of(i)

        def row(r, inner_carry):
            at("att", i * rows + r)

            @pl.when((i == 1) & (r == 0))
            def _():
                for j, zz in enumerate((z1, z2, z3)):
                    remote(vin, bias.at[zz], b_s.at[j], b_r.at[j], (dp, zz)).wait_recv()

            x_row = xs[r]
            bias_rows = bias[t].astype(BF)[:, : 3 * ml]
            qkv[t, r] = (
                dot(wbuf[ATT, t, pl.ds(0, 3 * ml), :], x_row, NT) + dot(bias_rows, first_row, TN)
            ).astype(BF)
            for h in range(hs):
                query = qkv[t, r, pl.ds(h * DH, DH), :]
                key = qkv[t, r, pl.ds(ml + h * DH, DH), :]
                value = qkv[t, r, pl.ds(2 * ml + h * DH, DH), :]
                scores = dot(key, query, TN) * scale + mask[r]
                top = jnp.max(scores, 0, keepdims=True)
                exponent = jnp.exp(scores - top)
                total = jnp.sum(exponent, 0, keepdims=True)
                prob_t = (exponent * (1.0 / total)).astype(BF)
                prob[t, r, h] = prob_t
                ka[t, r, pl.ds(3 * ml + h * DH, DH), :] = dot(value, prob_t, NN).astype(BF)
            part_sum = dot(ka[t, r, pl.ds(3 * ml, ml), :], wbuf[ATT, t, pl.ds(3 * ml, ml), :], TN)
            sl = pl.ds(pl.multiple_of(r * seq, 16), seq)
            acc[sl, :] = acc[sl, :] + part_sum
            return inner_carry

        lax.fori_loop(0, rows, row, 0)
        return carry

    lax.fori_loop(0, 4, attend, 0)

    rb = 32

    def norm_rows(summed):
        mean = jnp.mean(summed, -1, keepdims=True)
        centred = summed - mean
        variance = jnp.mean(centred * centred, -1, keepdims=True)
        rs_ = lax.rsqrt(variance + EPSILON)
        return centred * rs_, rs_

    def norm_back(grad, hat, rs_):
        return rs_ * (grad - jnp.mean(grad, -1, keepdims=True) - hat * jnp.mean(grad * hat, -1, keepdims=True))

    def vrow(j):
        return vin[pl.ds(j, 1), :]

    once("n1")

    def norm1(j, carry):
        sl = pl.ds(pl.multiple_of(j * rb, 16), rb)
        per = seq // rb
        x_blk = xs[j // per, pl.ds(pl.multiple_of((j % per) * rb, 16), rb), :].astype(F32)
        hat, rs_ = norm_rows(acc[sl, :] + vrow(2) + x_blk)
        nh1[sl, :] = hat
        r1[sl, :] = jnp.broadcast_to(rs_, (rb, 128))
        nb[sl, :] = (hat * vrow(3) + vrow(4)).astype(BF)
        acc[sl, :] = jnp.zeros((rb, d), F32)
        return carry

    lax.fori_loop(0, tl // rb, norm1, 0)
    core_send(X_N, lambda: (nb.at[:, pl.ds(ho, half)], nhalf.at[pl.ds(tl, tl)]))
    nhalf[pl.ds(0, tl), :] = nb[:, pl.ds(h0, half)]

    loads[2].wait()

    def up(i, carry):
        at("up", i)
        t = shard_of(i)
        tmp[...] = dot(nb[...], wbuf[INN, t], NN)
        b_row = bias[t, pl.ds(1, 1), :]

        def act(j, carry):
            sl = pl.ds(pl.multiple_of(j * rb, 16), rb)
            u = tmp[sl, :] + b_row
            cdf = 0.5 * (1.0 + lax.erf(u * ROOT_HALF))
            af[t, sl, :] = (u * cdf).astype(BF)
            gp[t, sl, :] = (cdf + u * (PDF_SCALE * jnp.exp(-0.5 * u * u))).astype(BF)
            return carry

        lax.fori_loop(0, tl // rb, act, 0)
        remote(af.at[t, :, pl.ds(ho, half)], asib.at[t], x_s.at[X_A + i], x_r.at[X_A + i], (p_c, z)).start()
        return carry

    lax.fori_loop(0, 4, up, 0)
    loads[3].wait()
    loads[4].wait()

    def down(i, carry):
        at("dn", i)
        t = shard_of(i)
        acc[...] += dot(af[t], wbuf[OUT, t], NN)
        return carry

    lax.fori_loop(0, 4, down, 0)

    once("l2")
    vec_ref[...] = jnp.zeros_like(vec_ref)

    def add_vec(row, value):
        vec_ref[pl.ds(row, 1), :] = vec_ref[pl.ds(row, 1), :] + value

    def norm2(j, carry):
        sl = pl.ds(pl.multiple_of(j * rb, 16), rb)
        normed = nh1[sl, :] * vrow(3) + vrow(4)
        hat, rs_ = norm_rows(acc[sl, :] + vrow(5) + normed)
        out_ref[sl, :] = (hat * vrow(6) + vrow(7)).astype(BF)
        c_blk = cots[sl, :].astype(F32)
        back = norm_back(c_blk * vrow(6), hat, rs_)
        sg[sl, :] = back
        g[sl, :] = back.astype(BF)
        acc[sl, :] = jnp.zeros((rb, d), F32)
        add_vec(V_G2, jnp.sum(c_blk * hat, 0, keepdims=True))
        add_vec(V_S2, jnp.sum(c_blk, 0, keepdims=True))
        add_vec(V_EB, jnp.sum(back, 0, keepdims=True))
        return carry

    lax.fori_loop(0, tl // rb, norm2, 0)
    core_send(X_G, lambda: (g.at[pl.ds(0, tl)], g.at[pl.ds(tl, tl)]))

    def order(i):
        return 3 - 2 * (i % 2) - i // 2

    def ffn_back(i, carry):
        @pl.when(i < 4)
        def _():
            at("da", i)
            k = order(i)
            t = shard_of(k)
            tmp[...] = dot(g[pl.ds(0, tl), :], wbuf[OUT, t], NT)

            def act(j, total):
                sl = pl.ds(pl.multiple_of(j * rb, 16), rb)
                blk = (tmp[sl, :] * gp[t, sl, :].astype(F32)).astype(BF)
                di[t, sl, :] = blk
                return total + jnp.sum(blk.astype(F32), 0, keepdims=True)

            vec_ref[pl.ds(4 + t, 1), :] = lax.fori_loop(0, tl // rb, act, jnp.zeros((1, d), F32))
            remote(
                di.at[t, pl.ds(0, tl)], di.at[t, pl.ds(tl, tl)], x_s.at[X_DI + k], x_r.at[X_DI + k], (p_c, z)
            ).start()
            at("gwo", i)

            @pl.when(i == 0)
            def _():
                core_wait(X_G, g.at[pl.ds(tl, tl)])
                core_wait(X_N, nhalf.at[pl.ds(tl, tl)])

            core_wait(X_A + k, asib.at[t])
            al[pl.ds(0, tl), :] = af[t, :, pl.ds(h0, half)]
            al[pl.ds(tl, tl), :] = asib[t]
            gr[OUT, k] = dot(al[...], g[...], TN).astype(BF)
            at("dn2", i)
            acc[...] += dot(di[t, pl.ds(0, tl), :], wbuf[INN, t], NT)

        @pl.when(i > 0)
        def _():
            at("gwi", i - 1)
            k = order(i - 1)
            t = shard_of(k)
            core_wait(X_DI + k, di.at[t, pl.ds(tl, tl)])
            gr[INN, k] = dot(nhalf[...], di[t], TN).astype(BF)

        return carry

    lax.fori_loop(0, 5, ffn_back, 0)
    once("l1b")

    def norm1_back(j, carry):
        sl = pl.ds(pl.multiple_of(j * rb, 16), rb)
        per = seq // rb
        hat = nh1[sl, :]
        total = acc[sl, :] + sg[sl, :]
        back = norm_back(total * vrow(3), hat, r1[sl, 0:1])
        fgf[sl, :] = back
        fg[j // per, pl.ds(pl.multiple_of((j % per) * rb, 16), rb), :] = back.astype(BF)
        acc[sl, :] = jnp.zeros((rb, d), F32)
        add_vec(V_G1, jnp.sum(total * hat, 0, keepdims=True))
        add_vec(V_S1, jnp.sum(total, 0, keepdims=True))
        add_vec(V_OB, jnp.sum(back, 0, keepdims=True))
        return carry

    lax.fori_loop(0, tl // rb, norm1_back, 0)
    core_send(X_FG, lambda: (fg.at[pl.ds(0, rows)], fg.at[pl.ds(rows, rows)]))
    ones = jnp.ones((8, seq), BF)

    def att_back(i, carry):
        @pl.when(i < 4)
        def _():
            k = order(i)
            t = shard_of(k)

            def row(r, inner_carry):
                at("ab", i * rows + r)
                dctx = dot(wbuf[ATT, t, pl.ds(3 * ml, ml), :], fg[r], NT).astype(BF)
                for h in range(hs):
                    query = qkv[t, r, pl.ds(h * DH, DH), :]
                    key = qkv[t, r, pl.ds(ml + h * DH, DH), :]
                    value = qkv[t, r, pl.ds(2 * ml + h * DH, DH), :]
                    prob_t = prob[t, r, h]
                    grad = dctx[h * DH : (h + 1) * DH]
                    ka[t, r, pl.ds(2 * ml + h * DH, DH), :] = dot(grad, prob_t, NT).astype(BF)
                    prob_grad = dot(value, grad, TN)
                    wide_prob = prob_t.astype(F32)
                    inner = jnp.sum(wide_prob * prob_grad, 0, keepdims=True)
                    score_grad = (wide_prob * (prob_grad - inner)).astype(BF)
                    ka[t, r, pl.ds(h * DH, DH), :] = (dot(key, score_grad, NN) * scale).astype(BF)
                    ka[t, r, pl.ds(ml + h * DH, DH), :] = (dot(query, score_grad, NT) * scale).astype(BF)
                grads = ka[t, r, pl.ds(0, 3 * ml), :]
                vec_ref[pl.ds(t, 1), pl.ds(0, 3 * ml)] += dot(ones, grads, NT)[0:1]
                sl = pl.ds(pl.multiple_of(r * seq, 16), seq)
                acc[sl, :] = acc[sl, :] + dot(grads, wbuf[ATT, t, pl.ds(0, 3 * ml), :], TN)
                return inner_carry

            lax.fori_loop(0, rows, row, 0)
            remote(
                ka.at[t, :, pl.ds(ho, half)], ks.at[t], x_s.at[X_KA + k], x_r.at[X_KA + k], (p_c, z)
            ).start()

        @pl.when(i == 0)
        def _():
            core_wait(X_TOK, xs.at[pl.ds(rows, rows)])
            core_wait(X_FG, fg.at[pl.ds(rows, rows)])

        @pl.when(i > 0)
        def _():
            at("gwa", i - 1)
            k = order(i - 1)
            t = shard_of(k)
            core_wait(X_KA + k, ks.at[t])
            for j in range(2):
                rowsel = pl.ds(pl.multiple_of(h0 + j * ml, 16), ml)
                use = c * j
                total = jnp.zeros((ml, d), F32)
                for r in range(rows):
                    right_own = xs[r] if j == 0 else jnp.where(use == 1, fg[r], xs[r])
                    right_sib = xs[rows + r] if j == 0 else jnp.where(use == 1, fg[rows + r], xs[rows + r])
                    total += dot(ka[t, r, rowsel, :], right_own, NN)
                    total += dot(ks[t, r, pl.ds(j * ml, ml), :], right_sib, NN)
                gr[ATT, k, pl.ds(j * ml, ml), :] = total.astype(BF)

        return carry

    lax.fori_loop(0, 5, att_back, 0)
    once("fin")

    def finish(j, carry):
        sl = pl.ds(pl.multiple_of(j * rb, 16), rb)
        dx_ref[sl, :] = (fgf[sl, :] + acc[sl, :]).astype(BF)
        return carry

    lax.fori_loop(0, tl // rb, finish, 0)

    once("end")
    for j in range(5, len(partners)):
        v_send(j, 0)
        v_recv(j, 0)

    for make in pending:
        remote(*make()).wait_send()

    def sent(k, carry):
        t = shard_of(k)
        remote(af.at[t, :, pl.ds(ho, half)], asib.at[t], x_s.at[X_A + k], x_r.at[X_A + k], (p_c, z)).wait_send()
        remote(
            di.at[t, pl.ds(0, tl)], di.at[t, pl.ds(tl, tl)], x_s.at[X_DI + k], x_r.at[X_DI + k], (p_c, z)
        ).wait_send()
        remote(ka.at[t, :, pl.ds(ho, half)], ks.at[t], x_s.at[X_KA + k], x_r.at[X_KA + k], (p_c, z)).wait_send()
        return carry

    lax.fori_loop(0, 4, sent, 0)


def spread_kernel(
    ml, grads, vec, out_in, dx_in,
    out_ref, dx_ref, gq, gk, gv, go, gi, ge, bq, bv, bo, g1, s1, bi, be, g2, s2,
    grads_v, vec_v, att_v, big_v, io_v, sem,
):
    z = lax.axis_index("mp")
    moves = [
        pltpu.make_async_copy(grads.at[1], grads_v.at[1], sem.at[0]),
        pltpu.make_async_copy(grads.at[2], grads_v.at[2], sem.at[1]),
        pltpu.make_async_copy(grads.at[0], grads_v.at[0], sem.at[2]),
        pltpu.make_async_copy(vec, vec_v, sem.at[3]),
        pltpu.make_async_copy(out_in, io_v.at[0], sem.at[4]),
        pltpu.make_async_copy(dx_in, io_v.at[1], sem.at[5]),
    ]
    for cp in moves:
        cp.start()
    outs = []
    for j, ref in enumerate((gi, ge)):
        moves[j].wait()
        big_v[j] = grads_v[j + 1].astype(F32)
        cp = pltpu.make_async_copy(big_v.at[j], ref, sem.at[6 + j])
        cp.start()
        outs.append(cp)
    moves[2].wait()
    att_v[...] = grads_v[0].astype(F32)
    for j, ref in enumerate((gq, gk, gv, go)):
        cp = pltpu.make_async_copy(att_v.at[pl.ds(j * ml, ml)], ref, sem.at[8 + j])
        cp.start()
        outs.append(cp)
    for j, ref in enumerate((out_ref, dx_ref)):
        moves[4 + j].wait()
        cp = pltpu.make_async_copy(io_v.at[j], ref, sem.at[12 + j])
        cp.start()
        outs.append(cp)
    moves[3].wait()
    bq[...] = vec_v[pl.ds(z, 1), pl.ds(0, ml)].reshape(ml)
    bv[...] = vec_v[pl.ds(z, 1), pl.ds(2 * ml, ml)].reshape(ml)
    bi[...] = vec_v[pl.ds(4 + z, 1), :].reshape(4 * ml)
    for row, ref in ((V_OB, bo), (V_G1, g1), (V_S1, s1), (V_EB, be), (V_G2, g2), (V_S2, s2)):
        ref[...] = vec_v[pl.ds(row, 1), :].reshape(4 * ml)
    for cp in outs:
        cp.wait()


def per_device(
    n_dp,
    tokens, segment_ids, live_mask, query_weight, key_weight, value_weight, query_bias, value_bias,
    output_weight, output_bias, first_gain, first_shift, inner_weight, inner_bias, outer_weight,
    outer_bias, second_gain, second_shift, cotangent,
):
    tl, d = tokens.shape
    seq_rows, seq = segment_ids.shape
    rows = tl // seq
    ml = query_weight.shape[1]
    half, qtr, eig = d // 2, d // 4, d // 8
    bits = n_dp.bit_length() - 1
    n_extra = max(bits - 3, 1)
    n_vec = bits + 2
    cfg = {"dp": n_dp, "d": d, "seq": seq, "rows": rows}
    vmem = pl.BlockSpec(memory_space=pltpu.VMEM)
    hbm = pl.BlockSpec(memory_space=pl.ANY)
    scratch = [
        pltpu.VMEM((3, 4, d, d), BF),
        pltpu.VMEM((4, 8, d), F32),
        pltpu.VMEM((2 * rows, seq, d), BF),
        pltpu.VMEM((tl, d), BF),
        pltpu.VMEM((4, rows, 3 * ml, seq), BF),
        pltpu.VMEM((4, rows, d, seq), BF),
        pltpu.VMEM((4, rows, half, seq), BF),
        pltpu.VMEM((4, rows, ml // DH, seq, seq), BF),
        pltpu.VMEM((rows, seq, seq), F32),
        pltpu.VMEM((tl, d), F32),
        pltpu.VMEM((tl, d), F32),
        pltpu.VMEM((tl, d), F32),
        pltpu.VMEM((tl, 128), F32),
        pltpu.VMEM((tl, d), BF),
        pltpu.VMEM((2 * tl, half), BF),
        pltpu.VMEM((4, tl, d), BF),
        pltpu.VMEM((4, tl, half), BF),
        pltpu.VMEM((2 * tl, half), BF),
        pltpu.VMEM((4, tl, d), BF),
        pltpu.VMEM((2 * tl, d), BF),
        pltpu.VMEM((tl, d), F32),
        pltpu.VMEM((4, 2 * tl, d), BF),
        pltpu.VMEM((2 * rows, seq, d), BF),
        pltpu.VMEM((tl, d), F32),
        pltpu.VMEM((3, 4, half, d), BF),
        pltpu.VMEM((3, 4, qtr, d), BF),
        pltpu.VMEM((3, 3, qtr, d), BF),
        pltpu.VMEM((3, 4, eig, d), BF),
        pltpu.VMEM((3, n_extra, eig, d), BF) if bits > 3 else pltpu.VMEM((1, 1, 16, 128), BF),
        pltpu.VMEM((n_vec, 16, d), F32),
        pltpu.VMEM((8, d), F32),
        pltpu.SemaphoreType.DMA((11,)),
        pltpu.SemaphoreType.DMA((3, 12)),
        pltpu.SemaphoreType.DMA((3, 12)),
        pltpu.SemaphoreType.DMA((3, 14)),
        pltpu.SemaphoreType.DMA((3, 14)),
        pltpu.SemaphoreType.DMA((16,)),
        pltpu.SemaphoreType.DMA((16,)),
        pltpu.SemaphoreType.DMA((3,)),
        pltpu.SemaphoreType.DMA((3,)),
        pltpu.SemaphoreType.DMA((n_vec,)),
        pltpu.SemaphoreType.DMA((n_vec,)),
        pltpu.SemaphoreType.DMA((3, n_extra)),
        pltpu.SemaphoreType.DMA((3, n_extra)),
    ]
    out, dx, grads, vec = pl.pallas_call(
        functools.partial(layer_kernel, cfg),
        out_shape=(
            jax.ShapeDtypeStruct((tl, d), BF),
            jax.ShapeDtypeStruct((tl, d), BF),
            jax.ShapeDtypeStruct((3, d, d), BF),
            jax.ShapeDtypeStruct((16, d), F32),
        ),
        in_specs=[hbm] * 8 + [vmem] * 11,
        out_specs=(vmem, vmem, hbm, vmem),
        scratch_shapes=scratch,
        compiler_params=pltpu.CompilerParams(
            collective_id=0, has_side_effects=True, vmem_limit_bytes=62 * 1024 * 1024
        ),
        name="layer",
    )(
        tokens.reshape(rows, seq, d), cotangent, query_weight.T, key_weight.T, value_weight.T, output_weight,
        inner_weight, outer_weight, query_bias, value_bias, inner_bias, output_bias, first_gain, first_shift,
        outer_bias, second_gain, second_shift, segment_ids, live_mask,
    )
    ff = inner_weight.shape[1]
    out, dx, gq, gk, gv, go, gi, ge, bq, bv, bo, g1, s1, bi, be, g2, s2 = pl.pallas_call(
        functools.partial(spread_kernel, ml),
        out_shape=tuple(
            jax.ShapeDtypeStruct(shape, dtype)
            for shape, dtype in [((tl, d), BF)] * 2
            + [((ml, d), F32)] * 4
            + [((d, ff), F32), ((ff, d), F32)]
            + [((ml,), F32)] * 2
            + [((d,), F32)] * 7
        ),
        in_specs=[hbm] * 4,
        out_specs=(hbm,) * 8 + (vmem,) * 9,
        scratch_shapes=[
            pltpu.VMEM((3, d, d), BF),
            pltpu.VMEM((16, d), F32),
            pltpu.VMEM((d, d), F32),
            pltpu.VMEM((2, d, d), F32),
            pltpu.VMEM((2, tl, d), BF),
            pltpu.SemaphoreType.DMA((14,)),
        ],
        compiler_params=pltpu.CompilerParams(vmem_limit_bytes=60 * 1024 * 1024),
        name="spread",
    )(grads, vec, out, dx)
    return out, dx, gq.T, gk.T, gv.T, bq, bv, go, bo, g1, s1, gi, bi, ge, be, g2, s2


def solution(mesh):
    tok, shared = P(("dp", "mp"), None), P()
    cols, rows, vec = P(None, "mp"), P("mp", None), P("mp")
    in_specs = (
        tok, P("dp", None), P("dp", None), cols, cols, cols, vec, vec, rows, shared, shared, shared,
        cols, vec, rows, shared, shared, shared, tok,
    )
    out_specs = (
        tok, tok, cols, cols, cols, vec, vec, rows, shared, shared, shared, cols, vec, rows,
        shared, shared, shared,
    )
    return jax.shard_map(
        functools.partial(per_device, mesh.shape["dp"]),
        mesh=mesh,
        in_specs=in_specs,
        out_specs=out_specs,
        check_vma=False,
    )
```

```python
import functools

import jax
import jax.numpy as jnp
from jax import lax
from jax.experimental import pallas as pl
from jax.experimental.pallas import tpu as pltpu
from jax.sharding import PartitionSpec as P

DH = 64
EPSILON = 1e-06
NEG_FILL = -1000000000.0
ROOT_HALF = 0.7071067811865476
PDF_SCALE = 0.3989422804014327
BF = jnp.bfloat16
F32 = jnp.float32
MESH = pl.DeviceIdType.MESH

NN = (((1,), (0,)), ((), ()))
NT = (((1,), (1,)), ((), ()))
TN = (((0,), (0,)), ((), ()))

ATT, INN, OUT = 0, 1, 2
GATHERED = (
    (0, 0, 384, False),
    (0, 384, 384, False),
    (1, 0, 384, False),
    (1, 384, 384, True),
    (2, 0, 384, False),
    (2, 384, 384, True),
)
SUMMED = (
    (0, 0, 192, "FS12"),
    (0, 192, 192, "FS12"),
    (1, 0, 192, "F12S"),
    (1, 192, 192, "F12S"),
    (2, 0, 192, "F12S"),
    (2, 192, 192, "F12S"),
)
PLAN = {
    "x0": {
        0: (("az1", 0, 0), ("az2", 0, 0), ("az1", 1, 0), ("az2", 1, 0), ("s", 0, 1), ("zf", 0, 0), ("s", 0, 2), ("s", 1, 1), ("az2", 2, 0), ("az1", 2, 0), ("f", 0, 1), ("zf", 1, 0), ("f", 1, 1),),
    },
    "att": {
        0: (("s", 1, 2), ("az1", 3, 0), ("c", 0, 1), ("f", 0, 2), ("az2", 3, 0),),
        1: (("s", 2, 1), ("f", 1, 2), ("c", 1, 1), ("zf", 2, 0), ("s", 2, 2), ("s", 0, 3), ("az2", 4, 0), ("az1", 4, 0), ("c", 0, 2),),
        2: (("f", 2, 1), ("d", 1, 1), ("d", 0, 1),),
        3: (("f", 3, 1), ("f", 0, 3), ("d", 0, 2), ("s", 1, 3), ("az2", 5, 0), ("az1", 5, 0), ("f", 1, 3), ("s", 4, 1), ("c", 1, 2), ("zf", 4, 0), ("s", 2, 3), ("zf", 3, 0), ("f", 2, 2),),
        4: (("d", 1, 2), ("s", 4, 2), ("c", 0, 3), ("f", 3, 2),),
        5: (("f", 4, 1), ("f", 5, 1), ("d", 0, 3), ("c", 1, 3), ("f", 2, 3), ("zf", 5, 0), ("c", 2, 2), ("f", 5, 2),),
        6: (("c", 2, 1), ("c", 4, 1), ("c", 3, 1), ("c", 3, 2), ("d", 1, 3), ("s", 4, 3), ("f", 3, 3), ("c", 5, 1),),
        7: (("f", 4, 2), ("d", 3, 1), ("d", 2, 1), ("d", 3, 2), ("c", 2, 3),),
    },
    "n1": {
        0: (("f", 4, 3), ("c", 5, 2), ("c", 3, 3), ("d", 2, 3), ("d", 2, 2), ("f", 5, 3),),
    },
    "up": {
        2: (("c", 4, 2),),
        3: (("d", 3, 3), ("c", 4, 3),),
    },
    "dn": {
        1: (("d", 5, 1), ("d", 4, 2), ("d", 4, 1), ("c", 5, 3),),
        2: (("d", 5, 2),),
        3: (("d", 4, 3), ("d", 5, 3),),
    },
    "l2": {
    },
    "da": {
        2: (("gFr", 5, 3), ("gFs", 2, 3), ("g1s", 5, 3), ("gFs", 4, 1),),
    },
    "gwo": {
        3: (("g1s", 5, 1),),
    },
    "dn2": {
        0: (("gFs", 5, 3), ("gFs", 4, 3),),
        1: (("gFs", 5, 1),),
        3: (("gFs", 2, 1),),
    },
    "gwi": {
        1: (("gFr", 4, 3), ("gFs", 4, 2), ("g1s", 4, 3), ("gFs", 3, 3), ("gFr", 5, 1), ("gFs", 5, 2),),
        3: (("gFs", 3, 2), ("gFs", 4, 0),),
    },
    "l1b": {
        0: (("gFr", 4, 1), ("gFr", 4, 2),),
    },
    "ab": {
        0: (("g1r", 4, 2), ("gFs", 5, 0), ("g1s", 4, 1),),
        1: (("gFs", 2, 2),),
        2: (("gFs", 2, 0), ("gFs", 3, 0), ("g2s", 4, 2),),
        3: (("gFr", 2, 3), ("gFr", 2, 1), ("gFr", 5, 2), ("gFr", 3, 3), ("g1s", 2, 3),),
        4: (("gFr", 4, 0),),
        5: (("g1s", 3, 3), ("gFs", 0, 3), ("g1r", 5, 2), ("gFr", 5, 0), ("g1r", 4, 0), ("gFs", 1, 3),),
        6: (("g2s", 5, 2),),
        7: (("gFs", 0, 1), ("g2r", 4, 0), ("gSs", 4, 0),),
    },
    "gwa": {
        0: (("gFs", 3, 1),),
        2: (("gFr", 3, 2), ("gFr", 3, 1), ("gFr", 0, 3), ("gFs", 1, 1), ("gFr", 2, 2), ("g1s", 2, 1), ("gFr", 3, 0), ("gFr", 1, 3),),
        3: (("gFs", 1, 2), ("g1r", 2, 2), ("gFr", 0, 1), ("gSr", 4, 0), ("gSs", 1, 3), ("g2s", 2, 2), ("gSs", 0, 1),),
    },
    "fin": {
        0: (("g1s", 3, 1), ("gFr", 2, 0), ("gFs", 1, 0),),
    },
    "end": {
        0: (("g1r", 3, 2), ("gFs", 0, 2), ("gFs", 0, 0), ("g2s", 3, 2), ("gSs", 0, 3), ("gSr", 0, 1), ("g1r", 2, 0), ("gFr", 1, 2), ("gSs", 1, 2), ("gSr", 1, 3), ("gFr", 0, 2), ("g1r", 5, 0), ("vs", 0, 0), ("gSs", 0, 2), ("vr", 0, 0), ("gS2s", 4, 0), ("g2r", 5, 0), ("gSr", 0, 3), ("vs", 1, 0), ("g1s", 0, 3), ("g2r", 2, 0), ("g1r", 3, 0), ("gFr", 1, 1), ("gFr", 1, 0), ("gFr", 0, 0), ("gSs", 1, 1), ("g1s", 1, 3), ("gSs", 5, 0), ("gSr", 0, 2), ("gSs", 2, 0), ("vr", 1, 0), ("gS2r", 4, 0), ("gSr", 5, 0), ("gSs", 1, 0), ("gSr", 1, 1), ("gS2s", 5, 0), ("g1r", 0, 2), ("gSs", 0, 0), ("gSr", 1, 2), ("g2s", 0, 2), ("g1s", 1, 1), ("g2r", 3, 0), ("g1r", 1, 2), ("gSs", 3, 0), ("gSr", 2, 0), ("gS2r", 5, 0), ("g1s", 0, 1), ("gSr", 1, 0), ("gS2s", 2, 0), ("vs", 2, 0), ("g2s", 1, 2), ("gSr", 0, 0), ("gSr", 3, 0), ("gS2s", 3, 0), ("g1r", 1, 0), ("gS2r", 2, 0), ("g1r", 0, 0), ("g2r", 0, 0), ("gF2r", 4, 0), ("gS2s", 0, 0), ("vr", 2, 0), ("g2r", 1, 0), ("gS2s", 1, 0), ("vs", 3, 0), ("gS2r", 3, 0), ("gS2r", 0, 0), ("gS2r", 1, 0), ("vr", 3, 0), ("gC2r", 4, 0), ("gF2r", 5, 0), ("gF2r", 2, 0), ("vs", 4, 0), ("gC2r", 2, 0), ("gF2r", 0, 0), ("vr", 4, 0), ("gF2r", 3, 0), ("gC2r", 0, 0), ("gF2r", 1, 0), ("gC2r", 5, 0), ("gC2r", 1, 0), ("gC2r", 3, 0),),
    },
}
V_OB, V_G1, V_S1, V_EB, V_G2, V_S2 = 8, 9, 10, 11, 12, 13


def dot(left, right, dims):
    return lax.dot_general(left, right, dims, preferred_element_type=F32)


def depth_at(p, stage):
    done = SUMMED[p][3].split(stage)[0]
    return ("F" in done) + ("S" in done)


def z_rows(p, slot):
    sizes = {(q, t): SUMMED[q][2] >> depth_at(q, "2" if t == 2 else "1") for q in range(len(SUMMED)) for t in range(3)}
    return sum(n for key, n in sizes.items() if key < (p, slot)), sizes[p, slot]


def layer_kernel(
    cfg,
    tok, cot, wq, wk, wv, wo, wi, wout, bq, bv, bi, bo, g1, s1, be, g2, s2, seg_in, live_in,
    out_hbm, dx_hbm, grad_ref, vec_hbm,
    wbuf, bias, xs, cots, qkv, ka, ks, prob, mask, acc, tmp, nh1, r1,
    nb, nhalf, af, asib, al, gp, g, sg, di, fg, whole,
    gr, rf, rz, rs, rx, vrecv, vin,
    dx_ref, vec_ref, seg, live, *rest,
):
    n_dp, d, seq, rows = cfg["dp"], cfg["d"], cfg["seq"], cfg["rows"]
    tl = seq * rows
    ml = d // 4
    hs = ml // DH
    half, qtr, eig = d // 2, d // 4, d // 8
    scale = DH ** (-0.5)
    bits = n_dp.bit_length() - 1
    dp, z = lax.axis_index("dp"), lax.axis_index("mp")
    c = dp % 2
    df = 2 + 2 * c
    ds_ = 6 - df
    f, s = (dp // df) % 2, (dp // ds_) % 2
    p_f, p_s, p_c = dp + df * (1 - 2 * f), dp + ds_ * (1 - 2 * s), dp + 1 - 2 * c
    z0, zh = z % 2, z // 2
    z1, z2, z3 = z + 1 - 2 * z0, z + 2 - 4 * zh, 3 - z
    h0 = pl.multiple_of(c * half, 128)
    ho = pl.multiple_of((1 - c) * half, 128)

    def sub(base, n, depth, other=False):
        off = base
        for level, bit in enumerate((c, f, s)[:depth]):
            n //= 2
            off = off + n * (1 - bit if other and level == depth - 1 else bit)
        return (pl.multiple_of(off, 16) if depth else off), n

    def cut(base, n, depth, other=False):
        off = base
        for level, bit in enumerate((f, s)[:depth]):
            n //= 2
            off = off + n * (1 - bit if other and level == depth - 1 else bit)
        return (pl.multiple_of(off, 16) if depth else off), n

    gathered = {}
    for a, (piece, base, n, wide) in enumerate(GATHERED):
        for depth in (1, 2, 3):
            for other in (False, True):
                gathered[a, depth, other] = sub(base, n, depth, other)
    summed = {}
    for p, (piece, base, n, chain) in enumerate(SUMMED):
        for depth in (0, 1, 2):
            for other in (False, True):
                summed[p, depth, other] = cut(base, n, depth, other)

    finals = {}
    for p, (piece, base, n, chain) in enumerate(SUMMED):
        for depth in (0, 1, 2):
            for other in (False, True):
                off, m = summed[p, depth, other]
                finals[p, depth, other] = (pl.multiple_of(c * half + off, 16), m)
        finals[p, "core", True] = (pl.multiple_of((1 - c) * half + base, 16), n)
    shard = (z, z1, z2, z3)

    def shard_of(k):
        k0, kh = k % 2, k // 2
        return z0 + k0 - 2 * z0 * k0 + 2 * (zh + kh - 2 * zh * kh)

    def remote(src, dst, ssem, rsem, dev):
        return pltpu.make_async_remote_copy(
            src_ref=src, dst_ref=dst, send_sem=ssem, recv_sem=rsem, device_id=dev, device_id_type=MESH
        )

    pending = []

    def send(make):
        remote(*make()).start()
        pending.append(make)

    small = rest[:9]
    loc_sem, ag_s, ag_r, gr_s, gr_r, x_s, x_r, b_s, b_r, v_s, v_r, e_s, e_r, out_sem = rest[9:]
    barrier = pltpu.get_barrier_semaphore()
    extra = [dp + (1 << b) * (1 - 2 * ((dp // (1 << b)) % 2)) for b in range(3, bits)]
    greet = [(p_c, z), (p_f, z), (p_s, z), (dp, z1), (dp, z2), (dp, z3)] + [(e, z) for e in extra]
    for dev in greet:
        pl.semaphore_signal(barrier, inc=1, device_id=dev, device_id_type=MESH)
    att_loads = [
        pltpu.make_async_copy(ref, wbuf.at[ATT, z, pl.ds(j * ml, ml)], loc_sem.at[j])
        for j, ref in enumerate((wq, wk, wv, wo))
    ]
    vec_loads = [
        pltpu.make_async_copy(ref, dst, loc_sem.at[4 + j])
        for j, (ref, dst) in enumerate(zip((bq, bv, bi, bo, g1, s1, be, g2, s2), small))
    ]
    seg_loads = [
        pltpu.make_async_copy(seg_in, seg, loc_sem.at[13]),
        pltpu.make_async_copy(live_in, live, loc_sem.at[14]),
        pltpu.make_async_copy(tok, xs.at[pl.ds(0, rows)], loc_sem.at[15]),
    ]
    late_loads = [
        pltpu.make_async_copy(wi, wbuf.at[INN, z], loc_sem.at[16]),
        pltpu.make_async_copy(wout, wbuf.at[OUT, z], loc_sem.at[17]),
        pltpu.make_async_copy(cot, cots, loc_sem.at[18]),
    ]
    for cp in att_loads + vec_loads + seg_loads + late_loads:
        cp.start()
    for cp in att_loads:
        cp.wait()
    pl.semaphore_wait(barrier, len(greet))

    def own(piece, off, n):
        if piece == ATT:
            return wbuf.at[ATT, z, pl.ds(off, n)]
        return (wi, wout)[piece - 1].at[pl.ds(off, n)]

    def reg(piece, k, off, n):
        return wbuf.at[piece, shard[k], pl.ds(off, n)]

    def ag_send(a, slot, k, rows_of, dev, mine=False):
        piece = GATHERED[a][0]

        def make():
            region = reg(piece, k, *rows_of)
            return own(piece, *rows_of) if mine else region, region, ag_s.at[a, slot], ag_r.at[a, slot], dev

        send(make)

    def ag_wait(a, slot, k, rows_of):
        region = reg(GATHERED[a][0], k, *rows_of)
        remote(region, region, ag_s.at[a, slot], ag_r.at[a, slot], (dp, z1)).wait_recv()

    def first(a):
        return gathered[a, 2 if GATHERED[a][3] else 3, False]

    def a_z1(a, _):
        ag_send(a, 1, 0, first(a), (dp, z1), True)

    def a_z2(a, _):
        ag_send(a, 0, 0, first(a), (dp, z2), True)

    def a_zf(a, _):
        ag_wait(a, 0, 2, first(a))
        ag_send(a, 2, 2, first(a), (dp, z1))

    def a_arrive(a, k):
        if k != 2:
            ag_wait(a, {1: 1, 3: 2}[k], k, first(a))

    def a_s(a, k):
        a_arrive(a, k)
        ag_send(a, 2 + k, k, gathered[a, 3, False], (p_s, z))

    def a_f(a, k):
        if GATHERED[a][3]:
            a_arrive(a, k)
        else:
            ag_wait(a, 2 + k, k, gathered[a, 3, True])
        ag_send(a, 5 + k, k, gathered[a, 2, False], (p_f, z))

    def a_c(a, k):
        ag_wait(a, 5 + k, k, gathered[a, 2, True])
        ag_send(a, 8 + k, k, gathered[a, 1, False], (p_c, z))

    def a_d(a, k):
        ag_wait(a, 8 + k, k, gathered[a, 1, True])

    X_TOK, X_N, X_G, X_FG, X_A, X_DI, X_KA = 0, 1, 2, 3, 4, 8, 12

    def core_send(slot, pair):
        send(lambda: (*pair(), x_s.at[slot], x_r.at[slot], (p_c, z)))

    def core_wait(slot, dst):
        remote(dst, dst, x_s.at[slot], x_r.at[slot], (p_c, z)).wait_recv()

    def g_sem(p, slot):
        return gr_s.at[p, slot], gr_r.at[p, slot]

    def g_send(p, slot, pair, dev):
        send(lambda: (*pair(), *g_sem(p, slot), dev))

    def g_wait(p, slot, dst):
        remote(dst, dst, *g_sem(p, slot), (dp, z1)).wait_recv()

    def add_into(dst, src, n):
        def blk(j, carry):
            sl = pl.ds(pl.multiple_of(j * 48, 16), 48)
            dst[sl, :] = (dst[sl, :].astype(F32) + src[sl, :].astype(F32)).astype(BF)
            return carry

        lax.fori_loop(0, n // 48, blk, 0)

    def chunk(p, k, depth, other=False):
        off, n = summed[p, depth, other]
        return gr.at[SUMMED[p][0], k, pl.ds(off, n)]

    def final(p, depth, other=False):
        off, n = finals[p, depth, other]
        return whole.at[SUMMED[p][0], pl.ds(off, n)]

    def f_slot(p, k):
        piece, base, n, _ = SUMMED[p]
        return rf.at[piece, k, pl.ds(base // 2, n // 2)]

    def s_slot(p, k):
        piece, base, n, _ = SUMMED[p]
        return rs.at[piece, k, pl.ds(base // 4, n // 4)]

    def z_slot(p, slot):
        return rz.at[pl.ds(*z_rows(p, slot))]

    def g_fs(p, k):
        g_send(p, k, lambda: (chunk(p, k, 1, True), f_slot(p, k)), (p_f, z))

    def g_fr(p, k):
        g_wait(p, k, f_slot(p, k))
        add_into(chunk(p, k, 1), f_slot(p, k), SUMMED[p][2] // 2)

    def g_ss(p, k):
        g_send(p, 4 + k, lambda: (chunk(p, k, 2, True), s_slot(p, k)), (p_s, z))

    def g_sr(p, k):
        g_wait(p, 4 + k, s_slot(p, k))
        add_into(chunk(p, k, 2), s_slot(p, k), SUMMED[p][2] // 4)

    def g_1s(p, k):
        slot = 0 if k == 3 else 1
        g_send(p, 8 + slot, lambda: (chunk(p, k, depth_at(p, "1")), z_slot(p, slot)), (dp, z1))

    def g_1r(p, k):
        slot = 0 if k == 2 else 1
        g_wait(p, 8 + slot, z_slot(p, slot))
        depth = depth_at(p, "1")
        add_into(chunk(p, k, depth), z_slot(p, slot), SUMMED[p][2] >> depth)

    def g_2s(p, k):
        g_send(p, 10, lambda: (chunk(p, 2, depth_at(p, "2")), z_slot(p, 2)), (dp, z2))

    def g_2r(p, k):
        g_wait(p, 10, z_slot(p, 2))
        depth = depth_at(p, "2")
        add_into(chunk(p, 0, depth), z_slot(p, 2), SUMMED[p][2] >> depth)

    def write_out(p):
        piece, base, n, _ = SUMMED[p]
        return [
            pltpu.make_async_copy(
                whole.at[piece, pl.ds(side * half + base, n)],
                grad_ref.at[piece, pl.ds(side * half + base, n)],
                out_sem.at[p, side],
            )
            for side in range(2)
        ]

    def g_s2s(p, _):
        piece, base, n, _ = SUMMED[p]
        for j, partner in enumerate(extra):
            slot = rx.at[piece, j, pl.ds(base // 4, n // 4)]
            cp = remote(chunk(p, 0, 2), slot, e_s.at[p, j], e_r.at[p, j], (partner, z))
            cp.start()
            cp.wait()
            add_into(chunk(p, 0, 2), slot, n // 4)
        mine, target = chunk(p, 0, 2), final(p, 2)
        for lo in range(0, n // 4, 48):
            target[pl.ds(lo, 48), :] = mine[pl.ds(lo, 48), :]
        g_send(p, 11, lambda: (final(p, 2),) * 2, (p_s, z))

    def g_s2r(p, _):
        g_wait(p, 11, final(p, 2, True))
        g_send(p, 12, lambda: (final(p, 1),) * 2, (p_f, z))

    def g_f2r(p, _):
        g_wait(p, 12, final(p, 1, True))
        g_send(p, 13, lambda: (final(p, 0),) * 2, (p_c, z))

    def g_c2r(p, _):
        g_wait(p, 13, final(p, "core", True))
        for cp in write_out(p):
            cp.start()

    partners = [(p_c, z), (p_f, z), (p_s, z), (dp, z1), (dp, z2)] + [(e, z) for e in extra]

    def v_copy(j):
        return remote(vec_ref, vrecv.at[j], v_s.at[j], v_r.at[j], partners[j])

    def v_send(j, _):
        v_copy(j).start()

    def v_recv(j, _):
        v_copy(j).wait()
        vec_ref[...] += vrecv[j]

    events = {
        "az1": a_z1, "az2": a_z2, "zf": a_zf, "s": a_s, "f": a_f, "c": a_c, "d": a_d,
        "gFs": g_fs, "gFr": g_fr, "gSs": g_ss, "gSr": g_sr, "g1s": g_1s, "g1r": g_1r, "g2s": g_2s, "g2r": g_2r,
        "gS2s": g_s2s, "gS2r": g_s2r, "gF2r": g_f2r, "gC2r": g_c2r, "vs": v_send, "vr": v_recv,
    }

    def do(listed):
        for kind, piece, k in listed:
            events[kind](piece, k)

    def at(place, index):
        for n, listed in PLAN.get(place, {}).items():
            pl.when(index == n)(functools.partial(do, listed))

    def once(place):
        do(PLAN.get(place, {}).get(0, ()))

    once("x0")
    for cp in vec_loads:
        cp.wait()
    vin[...] = jnp.zeros_like(vin)
    vin[pl.ds(0, 1), pl.ds(0, ml)] = small[0][...].astype(F32).reshape(1, ml)
    vin[pl.ds(0, 1), pl.ds(2 * ml, ml)] = small[1][...].astype(F32).reshape(1, ml)
    for j, ref in enumerate(small[2:]):
        vin[pl.ds(j + 1, 1), :] = ref[...].astype(F32).reshape(1, d)
    bias[z] = vin[...]
    for j, zz in enumerate((z1, z2, z3)):
        send(lambda j=j, zz=zz: (vin, bias.at[z], b_s.at[j], b_r.at[j], (dp, zz)))
    core_send(X_TOK, lambda: (tok, xs.at[pl.ds(rows, rows)]))
    for cp in seg_loads:
        cp.wait()

    for r in range(rows):
        seg_row = seg[pl.ds(z * rows + r, 1), :]
        live_row = live[pl.ds(z * rows + r, 1), :]
        code = jnp.where(live_row == 1, seg_row, -1)
        ids = lax.broadcasted_iota(jnp.int32, (8, seq), 0)
        key_hot = (jnp.broadcast_to(code, (8, seq)) == ids).astype(F32).astype(BF)
        query_hot = (jnp.broadcast_to(seg_row, (8, seq)) == ids).astype(F32).astype(BF)
        mask[r] = jnp.where(dot(key_hot, query_hot, TN) > 0.5, 0.0, NEG_FILL)
    acc[...] = jnp.zeros_like(acc)
    first_row = (lax.broadcasted_iota(jnp.int32, (8, seq), 0) == 0).astype(F32).astype(BF)

    def attend(i, carry):
        t = shard_of(i)

        def row(r, inner_carry):
            at("att", i * rows + r)

            @pl.when((i == 1) & (r == 0))
            def _():
                for j, zz in enumerate((z1, z2, z3)):
                    remote(vin, bias.at[zz], b_s.at[j], b_r.at[j], (dp, zz)).wait_recv()

            x_row = xs[r]
            bias_rows = bias[t].astype(BF)[:, : 3 * ml]
            qkv[t, r] = (
                dot(wbuf[ATT, t, pl.ds(0, 3 * ml), :], x_row, NT) + dot(bias_rows, first_row, TN)
            ).astype(BF)
            for h in range(hs):
                query = qkv[t, r, pl.ds(h * DH, DH), :]
                key = qkv[t, r, pl.ds(ml + h * DH, DH), :]
                value = qkv[t, r, pl.ds(2 * ml + h * DH, DH), :]
                scores = dot(key, query, TN) * scale + mask[r]
                top = jnp.max(scores, 0, keepdims=True)
                exponent = jnp.exp(scores - top)
                total = jnp.sum(exponent, 0, keepdims=True)
                prob_t = (exponent * (1.0 / total)).astype(BF)
                prob[t, r, h] = prob_t
                ka[t, r, pl.ds(3 * ml + h * DH, DH), :] = dot(value, prob_t, NN).astype(BF)
            part_sum = dot(ka[t, r, pl.ds(3 * ml, ml), :], wbuf[ATT, t, pl.ds(3 * ml, ml), :], TN)
            sl = pl.ds(pl.multiple_of(r * seq, 16), seq)
            acc[sl, :] = acc[sl, :] + part_sum
            return inner_carry

        lax.fori_loop(0, rows, row, 0)
        return carry

    lax.fori_loop(0, 4, attend, 0)

    rb = seq

    def norm_rows(summed):
        mean = jnp.mean(summed, -1, keepdims=True)
        centred = summed - mean
        variance = jnp.mean(centred * centred, -1, keepdims=True)
        rs_ = lax.rsqrt(variance + EPSILON)
        return centred * rs_, rs_

    def norm_back(grad, hat, rs_):
        return rs_ * (grad - jnp.mean(grad, -1, keepdims=True) - hat * jnp.mean(grad * hat, -1, keepdims=True))

    def vrow(j):
        return vin[pl.ds(j, 1), :]

    once("n1")

    def norm1(j, carry):
        sl = pl.ds(pl.multiple_of(j * rb, 16), rb)
        per = seq // rb
        x_blk = xs[j // per, pl.ds(pl.multiple_of((j % per) * rb, 16), rb), :].astype(F32)
        hat, rs_ = norm_rows(acc[sl, :] + vrow(2) + x_blk)
        nh1[sl, :] = hat
        r1[sl, :] = jnp.broadcast_to(rs_, (rb, 128))
        nb[sl, :] = (hat * vrow(3) + vrow(4)).astype(BF)
        acc[sl, :] = jnp.zeros((rb, d), F32)
        return carry

    lax.fori_loop(0, tl // rb, norm1, 0)
    core_send(X_N, lambda: (nb.at[:, pl.ds(ho, half)], nhalf.at[pl.ds(tl, tl)]))
    nhalf[pl.ds(0, tl), :] = nb[:, pl.ds(h0, half)]

    late_loads[0].wait()

    def up(i, carry):
        at("up", i)
        t = shard_of(i)
        tmp[...] = dot(nb[...], wbuf[INN, t], NN)
        b_row = bias[t, pl.ds(1, 1), :]

        def act(j, carry):
            sl = pl.ds(pl.multiple_of(j * rb, 16), rb)
            u = tmp[sl, :] + b_row
            cdf = 0.5 * (1.0 + lax.erf(u * ROOT_HALF))
            af[t, sl, :] = (u * cdf).astype(BF)
            gp[t, sl, :] = (cdf + u * (PDF_SCALE * jnp.exp(-0.5 * u * u))).astype(BF)
            return carry

        lax.fori_loop(0, tl // rb, act, 0)
        remote(af.at[t, :, pl.ds(ho, half)], asib.at[t], x_s.at[X_A + i], x_r.at[X_A + i], (p_c, z)).start()
        return carry

    lax.fori_loop(0, 4, up, 0)
    late_loads[1].wait()
    late_loads[2].wait()

    def down(i, carry):
        at("dn", i)
        t = shard_of(i)
        acc[...] += dot(af[t], wbuf[OUT, t], NN)
        return carry

    lax.fori_loop(0, 4, down, 0)

    once("l2")
    vec_ref[...] = jnp.zeros_like(vec_ref)

    def add_vec(row, value):
        vec_ref[pl.ds(row, 1), :] = vec_ref[pl.ds(row, 1), :] + value

    def norm2(j, carry):
        sl = pl.ds(pl.multiple_of(j * rb, 16), rb)
        normed = nh1[sl, :] * vrow(3) + vrow(4)
        hat, rs_ = norm_rows(acc[sl, :] + vrow(5) + normed)
        c_blk = cots[sl, :].astype(F32)
        cots[sl, :] = (hat * vrow(6) + vrow(7)).astype(BF)
        back = norm_back(c_blk * vrow(6), hat, rs_)
        sg[sl, :] = back
        g[sl, :] = back.astype(BF)
        acc[sl, :] = jnp.zeros((rb, d), F32)
        add_vec(V_G2, jnp.sum(c_blk * hat, 0, keepdims=True))
        add_vec(V_S2, jnp.sum(c_blk, 0, keepdims=True))
        add_vec(V_EB, jnp.sum(back, 0, keepdims=True))
        return carry

    lax.fori_loop(0, tl // rb, norm2, 0)
    out_copy = pltpu.make_async_copy(cots, out_hbm, loc_sem.at[19])
    core_send(X_G, lambda: (g.at[pl.ds(0, tl)], g.at[pl.ds(tl, tl)]))

    def order(i):
        return 3 - 2 * (i % 2) - i // 2

    def ffn_back(i, carry):
        @pl.when(i < 4)
        def _():
            at("da", i)
            k = order(i)
            t = shard_of(k)
            tmp[...] = dot(g[pl.ds(0, tl), :], wbuf[OUT, t], NT)

            def act(j, total):
                sl = pl.ds(pl.multiple_of(j * rb, 16), rb)
                blk = (tmp[sl, :] * gp[t, sl, :].astype(F32)).astype(BF)
                di[t, sl, :] = blk
                return total + jnp.sum(blk.astype(F32), 0, keepdims=True)

            vec_ref[pl.ds(4 + t, 1), :] = lax.fori_loop(0, tl // rb, act, jnp.zeros((1, d), F32))
            remote(
                di.at[t, pl.ds(0, tl)], di.at[t, pl.ds(tl, tl)], x_s.at[X_DI + k], x_r.at[X_DI + k], (p_c, z)
            ).start()
            at("gwo", i)

            @pl.when(i == 0)
            def _():
                core_wait(X_G, g.at[pl.ds(tl, tl)])
                core_wait(X_N, nhalf.at[pl.ds(tl, tl)])

            core_wait(X_A + k, asib.at[t])
            al[pl.ds(0, tl), :] = af[t, :, pl.ds(h0, half)]
            al[pl.ds(tl, tl), :] = asib[t]
            gr[OUT, k] = dot(al[...], g[...], TN).astype(BF)
            at("dn2", i)
            acc[...] += dot(di[t, pl.ds(0, tl), :], wbuf[INN, t], NT)

        @pl.when(i > 0)
        def _():
            at("gwi", i - 1)
            k = order(i - 1)
            t = shard_of(k)
            core_wait(X_DI + k, di.at[t, pl.ds(tl, tl)])
            gr[INN, k] = dot(nhalf[...], di[t], TN).astype(BF)

        return carry

    out_copy.start()
    lax.fori_loop(0, 5, ffn_back, 0)
    once("l1b")

    def norm1_back(j, carry):
        sl = pl.ds(pl.multiple_of(j * rb, 16), rb)
        per = seq // rb
        hat = nh1[sl, :]
        total = acc[sl, :] + sg[sl, :]
        back = norm_back(total * vrow(3), hat, r1[sl, 0:1])
        sg[sl, :] = back
        fg[j // per, pl.ds(pl.multiple_of((j % per) * rb, 16), rb), :] = back.astype(BF)
        acc[sl, :] = jnp.zeros((rb, d), F32)
        add_vec(V_G1, jnp.sum(total * hat, 0, keepdims=True))
        add_vec(V_S1, jnp.sum(total, 0, keepdims=True))
        add_vec(V_OB, jnp.sum(back, 0, keepdims=True))
        return carry

    lax.fori_loop(0, tl // rb, norm1_back, 0)
    core_send(X_FG, lambda: (fg.at[pl.ds(0, rows)], fg.at[pl.ds(rows, rows)]))
    ones = jnp.ones((8, seq), BF)

    def att_back(i, carry):
        @pl.when(i < 4)
        def _():
            k = order(i)
            t = shard_of(k)

            def row(r, inner_carry):
                at("ab", i * rows + r)
                dctx = dot(wbuf[ATT, t, pl.ds(3 * ml, ml), :], fg[r], NT).astype(BF)
                for h in range(hs):
                    query = qkv[t, r, pl.ds(h * DH, DH), :]
                    key = qkv[t, r, pl.ds(ml + h * DH, DH), :]
                    value = qkv[t, r, pl.ds(2 * ml + h * DH, DH), :]
                    prob_t = prob[t, r, h]
                    grad = dctx[h * DH : (h + 1) * DH]
                    ka[t, r, pl.ds(2 * ml + h * DH, DH), :] = dot(grad, prob_t, NT).astype(BF)
                    prob_grad = dot(value, grad, TN)
                    wide_prob = prob_t.astype(F32)
                    inner = jnp.sum(wide_prob * prob_grad, 0, keepdims=True)
                    score_grad = (wide_prob * (prob_grad - inner)).astype(BF)
                    ka[t, r, pl.ds(h * DH, DH), :] = (dot(key, score_grad, NN) * scale).astype(BF)
                    ka[t, r, pl.ds(ml + h * DH, DH), :] = (dot(query, score_grad, NT) * scale).astype(BF)
                grads = ka[t, r, pl.ds(0, 3 * ml), :]
                vec_ref[pl.ds(t, 1), pl.ds(0, 3 * ml)] += dot(ones, grads, NT)[0:1]
                sl = pl.ds(pl.multiple_of(r * seq, 16), seq)
                acc[sl, :] = acc[sl, :] + dot(grads, wbuf[ATT, t, pl.ds(0, 3 * ml), :], TN)
                return inner_carry

            lax.fori_loop(0, rows, row, 0)
            remote(
                ka.at[t, :, pl.ds(ho, half)], ks.at[t], x_s.at[X_KA + k], x_r.at[X_KA + k], (p_c, z)
            ).start()

        @pl.when(i == 0)
        def _():
            core_wait(X_TOK, xs.at[pl.ds(rows, rows)])
            core_wait(X_FG, fg.at[pl.ds(rows, rows)])

        @pl.when(i > 0)
        def _():
            at("gwa", i - 1)
            k = order(i - 1)
            t = shard_of(k)
            core_wait(X_KA + k, ks.at[t])
            for j in range(2):
                rowsel = pl.ds(pl.multiple_of(h0 + j * ml, 16), ml)
                use = c * j
                total = jnp.zeros((ml, d), F32)
                for r in range(rows):
                    right_own = xs[r] if j == 0 else jnp.where(use == 1, fg[r], xs[r])
                    right_sib = xs[rows + r] if j == 0 else jnp.where(use == 1, fg[rows + r], xs[rows + r])
                    total += dot(ka[t, r, rowsel, :], right_own, NN)
                    total += dot(ks[t, r, pl.ds(j * ml, ml), :], right_sib, NN)
                gr[ATT, k, pl.ds(j * ml, ml), :] = total.astype(BF)

        return carry

    lax.fori_loop(0, 5, att_back, 0)
    once("fin")

    def finish(j, carry):
        sl = pl.ds(pl.multiple_of(j * rb, 16), rb)
        dx_ref[sl, :] = (sg[sl, :] + acc[sl, :]).astype(BF)
        return carry

    lax.fori_loop(0, tl // rb, finish, 0)

    dx_copy = pltpu.make_async_copy(dx_ref, dx_hbm, loc_sem.at[20])
    dx_copy.start()

    once("end")
    for j in range(5, len(partners)):
        v_send(j, 0)
        v_recv(j, 0)
    vec_copy = pltpu.make_async_copy(vec_ref, vec_hbm, loc_sem.at[21])
    vec_copy.start()

    for make in pending:
        remote(*make()).wait_send()

    def sent(k, carry):
        t = shard_of(k)
        remote(af.at[t, :, pl.ds(ho, half)], asib.at[t], x_s.at[X_A + k], x_r.at[X_A + k], (p_c, z)).wait_send()
        remote(
            di.at[t, pl.ds(0, tl)], di.at[t, pl.ds(tl, tl)], x_s.at[X_DI + k], x_r.at[X_DI + k], (p_c, z)
        ).wait_send()
        remote(ka.at[t, :, pl.ds(ho, half)], ks.at[t], x_s.at[X_KA + k], x_r.at[X_KA + k], (p_c, z)).wait_send()
        return carry

    lax.fori_loop(0, 4, sent, 0)
    for p in range(len(SUMMED)):
        for cp in write_out(p):
            cp.wait()
    out_copy.wait()
    dx_copy.wait()
    vec_copy.wait()


def spread_kernel(
    ml, grads, vec, out_in, dx_in,
    out_ref, dx_ref, gq, gk, gv, go, gi, ge, bq, bv, bo, g1, s1, bi, be, g2, s2,
    grads_v, vec_v, wide_v, io_v, in_sem, out_sem,
):
    z = lax.axis_index("mp")
    n = 2 * ml
    steps = [(piece, lo, [(ref, lo, n)]) for piece, ref in ((1, gi), (2, ge)) for lo in (0, n)]
    steps += [(0, 0, [(gq, 0, ml), (gk, 0, ml)]), (0, n, [(gv, 0, ml), (go, 0, ml)])]
    moves = [
        pltpu.make_async_copy(grads.at[piece, pl.ds(lo, n)], grads_v.at[piece, pl.ds(lo, n)], in_sem.at[j])
        for j, (piece, lo, _) in enumerate(steps)
    ]
    ins = [
        pltpu.make_async_copy(vec, vec_v, in_sem.at[6]),
        pltpu.make_async_copy(out_in, io_v.at[0], in_sem.at[7]),
        pltpu.make_async_copy(dx_in, io_v.at[1], in_sem.at[8]),
    ]
    for cp in moves + ins:
        cp.start()
    outs = []

    def put(src, dst):
        cp = pltpu.make_async_copy(src, dst, out_sem.at[len(outs)])
        cp.start()
        outs.append(cp)

    for j, (piece, lo, refs) in enumerate(steps):
        moves[j].wait()
        wide_v[piece, pl.ds(lo, n), :] = grads_v[piece, pl.ds(lo, n), :].astype(F32)
        at = lo
        for ref, row, m in refs:
            put(wide_v.at[piece, pl.ds(at, m)], ref.at[pl.ds(row, m)])
            at += m
    ins[0].wait()
    bq[...] = vec_v[pl.ds(z, 1), pl.ds(0, ml)].reshape(ml)
    bv[...] = vec_v[pl.ds(z, 1), pl.ds(2 * ml, ml)].reshape(ml)
    bi[...] = vec_v[pl.ds(4 + z, 1), :].reshape(4 * ml)
    for row, ref in ((V_OB, bo), (V_G1, g1), (V_S1, s1), (V_EB, be), (V_G2, g2), (V_S2, s2)):
        ref[...] = vec_v[pl.ds(row, 1), :].reshape(4 * ml)
    for j, ref in enumerate((out_ref, dx_ref)):
        ins[1 + j].wait()
        put(io_v.at[j], ref)
    for cp in outs:
        cp.wait()


def per_device(
    n_dp,
    tokens, segment_ids, live_mask, query_weight, key_weight, value_weight, query_bias, value_bias,
    output_weight, output_bias, first_gain, first_shift, inner_weight, inner_bias, outer_weight,
    outer_bias, second_gain, second_shift, cotangent,
):
    tl, d = tokens.shape
    seq_rows, seq = segment_ids.shape
    rows = tl // seq
    ml = query_weight.shape[1]
    ff = inner_weight.shape[1]
    half, qtr, eig = d // 2, d // 4, d // 8
    bits = n_dp.bit_length() - 1
    n_extra = max(bits - 3, 1)
    n_vec = bits + 2
    cfg = {"dp": n_dp, "d": d, "seq": seq, "rows": rows}
    vmem = pl.BlockSpec(memory_space=pltpu.VMEM)
    hbm = pl.BlockSpec(memory_space=pl.ANY)
    scratch = [
        pltpu.VMEM((3, 4, d, d), BF),
        pltpu.VMEM((4, 8, d), F32),
        pltpu.VMEM((2 * rows, seq, d), BF),
        pltpu.VMEM((tl, d), BF),
        pltpu.VMEM((4, rows, 3 * ml, seq), BF),
        pltpu.VMEM((4, rows, d, seq), BF),
        pltpu.VMEM((4, rows, half, seq), BF),
        pltpu.VMEM((4, rows, ml // DH, seq, seq), BF),
        pltpu.VMEM((rows, seq, seq), F32),
        pltpu.VMEM((tl, d), F32),
        pltpu.VMEM((tl, d), F32),
        pltpu.VMEM((tl, d), F32),
        pltpu.VMEM((tl, 128), F32),
        pltpu.VMEM((tl, d), BF),
        pltpu.VMEM((2 * tl, half), BF),
        pltpu.VMEM((4, tl, d), BF),
        pltpu.VMEM((4, tl, half), BF),
        pltpu.VMEM((2 * tl, half), BF),
        pltpu.VMEM((4, tl, d), BF),
        pltpu.VMEM((2 * tl, d), BF),
        pltpu.VMEM((tl, d), F32),
        pltpu.VMEM((4, 2 * tl, d), BF),
        pltpu.VMEM((2 * rows, seq, d), BF),
        pltpu.VMEM((3, d, d), BF),
        pltpu.VMEM((3, 4, half, d), BF),
        pltpu.VMEM((3, 4, qtr, d), BF),
        pltpu.VMEM((sum(z_rows(len(SUMMED) - 1, 2)), d), BF),
        pltpu.VMEM((3, 4, eig, d), BF),
        pltpu.VMEM((3, n_extra, eig, d), BF) if bits > 3 else pltpu.VMEM((1, 1, 16, 128), BF),
        pltpu.VMEM((n_vec, 16, d), F32),
        pltpu.VMEM((8, d), F32),
        pltpu.VMEM((tl, d), BF),
        pltpu.VMEM((16, d), F32),
        pltpu.VMEM((seq_rows, seq), jnp.int32),
        pltpu.VMEM((seq_rows, seq), jnp.int32),
    ]
    scratch += [pltpu.VMEM((n,), BF) for n in (ml, ml, ff, d, d, d, d, d, d)]
    scratch += [
        pltpu.SemaphoreType.DMA(shape)
        for shape in [(24,)] + [(len(GATHERED), 12)] * 2 + [(len(SUMMED), 14)] * 2 + [(16,)] * 2 + [(3,)] * 2
        + [(n_vec,)] * 2 + [(len(SUMMED), n_extra)] * 2 + [(len(SUMMED), 2)]
    ]
    out, dx, grads, vec = pl.pallas_call(
        functools.partial(layer_kernel, cfg),
        out_shape=(
            jax.ShapeDtypeStruct((tl, d), BF),
            jax.ShapeDtypeStruct((tl, d), BF),
            jax.ShapeDtypeStruct((3, d, d), BF),
            jax.ShapeDtypeStruct((16, d), F32),
        ),
        in_specs=[hbm] * 19,
        out_specs=(hbm,) * 4,
        scratch_shapes=scratch,
        compiler_params=pltpu.CompilerParams(
            collective_id=0, has_side_effects=True, vmem_limit_bytes=62 * 1024 * 1024
        ),
        name="layer",
    )(
        tokens.reshape(rows, seq, d), cotangent, query_weight.T, key_weight.T, value_weight.T, output_weight,
        inner_weight, outer_weight, query_bias, value_bias, inner_bias, output_bias, first_gain, first_shift,
        outer_bias, second_gain, second_shift, segment_ids, live_mask,
    )
    out, dx, gq, gk, gv, go, gi, ge, bq, bv, bo, g1, s1, bi, be, g2, s2 = pl.pallas_call(
        functools.partial(spread_kernel, ml),
        out_shape=tuple(
            jax.ShapeDtypeStruct(shape, dtype)
            for shape, dtype in [((tl, d), BF)] * 2
            + [((ml, d), F32)] * 4
            + [((d, ff), F32), ((ff, d), F32)]
            + [((ml,), F32)] * 2
            + [((d,), F32)] * 7
        ),
        in_specs=[hbm] * 4,
        out_specs=(hbm,) * 8 + (vmem,) * 9,
        scratch_shapes=[
            pltpu.VMEM((3, d, d), BF),
            pltpu.VMEM((16, d), F32),
            pltpu.VMEM((3, d, d), F32),
            pltpu.VMEM((2, tl, d), BF),
            pltpu.SemaphoreType.DMA((9,)),
            pltpu.SemaphoreType.DMA((10,)),
        ],
        compiler_params=pltpu.CompilerParams(vmem_limit_bytes=60 * 1024 * 1024),
        name="spread",
    )(grads, vec, out, dx)
    return out, dx, gq.T, gk.T, gv.T, bq, bv, go, bo, g1, s1, gi, bi, ge, be, g2, s2


def solution(mesh):
    tok, shared = P(("dp", "mp"), None), P()
    cols, rows, vec = P(None, "mp"), P("mp", None), P("mp")
    in_specs = (
        tok, P("dp", None), P("dp", None), cols, cols, cols, vec, vec, rows, shared, shared, shared,
        cols, vec, rows, shared, shared, shared, tok,
    )
    out_specs = (
        tok, tok, cols, cols, cols, vec, vec, rows, shared, shared, shared, cols, vec, rows,
        shared, shared, shared,
    )
    return jax.shard_map(
        functools.partial(per_device, mesh.shape["dp"]),
        mesh=mesh,
        in_specs=in_specs,
        out_specs=out_specs,
        check_vma=False,
    )
```

```python
import functools

import jax
import jax.numpy as jnp
from jax import lax
from jax.experimental import pallas as pl
from jax.experimental.pallas import tpu as pltpu
from jax.sharding import PartitionSpec as P

DH = 64
EPSILON = 1e-06
NEG_FILL = -1000000000.0
ROOT_HALF = 0.7071067811865476
PDF_SCALE = 0.3989422804014327
BF = jnp.bfloat16
F32 = jnp.float32
MESH = pl.DeviceIdType.MESH
LIMIT = 59 * 1024 * 1024

NN = (((1,), (0,)), ((), ()))
NT = (((1,), (1,)), ((), ()))
TN = (((0,), (0,)), ((), ()))

ATT, INN, OUT = 0, 1, 2
GATHERED = (
    (0, 0, 384, 3),
    (0, 384, 384, 3),
    (1, 0, 384, 3),
    (1, 384, 384, 2),
    (2, 0, 384, 3),
    (2, 384, 256, 2),
    (2, 640, 128, 1),
)
SUMMED = (
    (0, 0, 192, "FS12"),
    (0, 192, 128, "FSZd"),
    (0, 320, 64, "FSZd"),
    (1, 0, 192, "F12S"),
    (1, 192, 192, "F12S"),
    (2, 0, 192, "1F2S"),
    (2, 192, 192, "F12S"),
)
PLAN = {
    "x0": {
        0: (("az1", 0, 0), ("az1", 1, 0), ("s", 0, 1), ("az2", 1, 0), ("az1", 4, 0), ("az2", 0, 0), ("az1", 2, 0), ("s", 1, 1), ("f", 0, 1), ("s", 4, 1), ("f", 1, 1), ("az2", 4, 0), ("zf", 0, 0), ("az2", 2, 0), ("zf", 1, 0), ("s", 0, 2), ("s", 1, 2),),
    },
    "att": {
        0: (("f", 4, 1), ("s", 2, 1),),
        1: (("f", 1, 2), ("az1", 5, 0), ("s", 0, 3), ("s", 1, 3), ("f", 0, 2), ("az2", 3, 0), ("c", 1, 1), ("zf", 4, 0), ("s", 4, 2), ("d", 1, 1), ("c", 4, 1), ("c", 0, 1), ("zf", 2, 0), ("f", 2, 1),),
        2: (("s", 2, 2), ("f", 1, 3), ("d", 0, 1), ("f", 0, 3), ("az2", 5, 0),),
        3: (("c", 1, 2), ("c", 2, 1), ("c", 0, 2), ("az1", 3, 0), ("zf", 3, 0), ("f", 3, 2), ("s", 2, 3), ("az2", 6, 0), ("d", 4, 1),),
        4: (("f", 2, 2), ("s", 4, 3), ("d", 1, 2), ("d", 0, 2), ("f", 4, 2), ("c", 1, 3),),
        5: (("zf", 5, 0), ("c", 0, 3), ("d", 1, 3), ("f", 2, 3),),
        6: (("f", 3, 1), ("d", 0, 3),),
        7: (("f", 3, 3), ("c", 2, 2), ("c", 3, 2), ("f", 5, 1), ("az1", 6, 0), ("f", 5, 2),),
    },
    "n1": {
        0: (("d", 2, 1), ("f", 4, 3), ("c", 3, 1), ("c", 2, 3), ("c", 4, 2),),
    },
    "up": {
        0: (("zf", 6, 0), ("d", 3, 2),),
        1: (("c", 6, 2), ("d", 3, 1), ("d", 2, 2), ("f", 5, 3), ("c", 3, 3),),
        2: (("c", 5, 1),),
        3: (("c", 6, 1), ("d", 3, 3), ("c", 5, 2), ("d", 2, 3), ("d", 4, 2),),
    },
    "dn": {
        0: (("c", 4, 3),),
        1: (("d", 5, 1), ("d", 6, 1), ("d", 6, 2), ("c", 6, 3), ("c", 5, 3),),
        2: (("d", 5, 2),),
        3: (("d", 6, 3), ("d", 5, 3), ("d", 4, 3),),
    },
    "l2": {
    },
    "da": {
        2: (("gFs", 4, 3), ("gFr", 6, 3), ("gFs", 3, 3),),
        3: (("gFs", 3, 1),),
    },
    "gwo": {
        2: (("g1s", 6, 3),),
        3: (("gFs", 4, 1),),
    },
    "dn2": {
        0: (("gFs", 6, 3), ("g1s", 5, 3),),
        1: (("gFs", 6, 1),),
        2: (("gFs", 6, 2),),
    },
    "gwi": {
        1: (("g1s", 5, 1),),
        2: (("gFr", 6, 1),),
        3: (("g1s", 6, 1), ("gFr", 4, 3), ("gFs", 6, 0), ("g1r", 5, 2), ("gFr", 6, 2),),
    },
    "l1b": {
        0: (("gFs", 4, 2), ("g1r", 6, 2), ("gFs", 3, 0),),
    },
    "ab": {
        1: (("gFr", 3, 3), ("gFs", 5, 2),),
        2: (("gFs", 3, 2), ("g2s", 6, 2), ("gFs", 4, 0),),
        4: (("gFs", 0, 3), ("g1s", 3, 3), ("gFs", 1, 3), ("g1r", 5, 0), ("gFs", 2, 3), ("g1s", 4, 3), ("gFs", 5, 0),),
        6: (("gFs", 0, 1), ("gFs", 1, 1), ("gFr", 5, 2), ("g2s", 5, 2), ("gFr", 6, 0),),
        7: (("gFr", 0, 3), ("gFr", 4, 1), ("g1r", 6, 0), ("gFs", 2, 1), ("gFr", 2, 3), ("gFr", 1, 3), ("gSs", 1, 3), ("g1s", 4, 1), ("gSs", 0, 3), ("g2r", 6, 0), ("gSs", 6, 0),),
    },
    "gwa": {
        2: (("gFr", 0, 1), ("gFr", 3, 1), ("gFr", 4, 2), ("gSs", 0, 1),),
        3: (("gSs", 2, 3), ("gFs", 1, 2), ("g1r", 4, 2), ("g2s", 4, 2), ("gFr", 1, 1), ("gFs", 0, 2), ("gFs", 2, 2),),
    },
    "fin": {
    },
    "end": {
        0: (("gFs", 2, 0), ("g1s", 3, 1), ("gFr", 4, 0), ("gFr", 3, 2), ("gSs", 1, 1), ("gFr", 1, 2), ("gFr", 5, 0), ("g2r", 5, 0), ("gSr", 6, 0), ("g1r", 3, 2), ("gSs", 5, 0), ("gSs", 1, 2), ("gFs", 1, 0), ("gFr", 2, 2), ("g2s", 3, 2), ("gFr", 3, 0), ("gSr", 1, 3), ("gFr", 0, 2), ("gSr", 0, 1), ("gFr", 2, 1), ("gFs", 0, 0), ("gSr", 0, 3), ("g1s", 0, 3), ("vs", 0, 0), ("vr", 0, 0), ("gS2s", 6, 0), ("vs", 1, 0), ("gSs", 2, 1), ("gSr", 5, 0), ("gSr", 1, 2), ("gS2s", 5, 0), ("gSr", 1, 1), ("gFr", 1, 0), ("gSs", 2, 2), ("g1r", 4, 0), ("gSr", 2, 3), ("gSs", 0, 2), ("gZs", 1, 2), ("g1s", 0, 1), ("g2r", 4, 0), ("gFr", 0, 0), ("gSs", 4, 0), ("g1r", 3, 0), ("gSs", 1, 0), ("gSs", 0, 0), ("gFr", 2, 0), ("gS2r", 5, 0), ("g2r", 3, 0), ("gSr", 0, 2), ("gSs", 3, 0), ("g1r", 0, 2), ("vr", 1, 0), ("vs", 2, 0), ("g2s", 0, 2), ("gSr", 2, 1), ("gZs", 1, 1), ("gSr", 4, 0), ("gS2s", 4, 0), ("gSr", 0, 0), ("gZs", 2, 1), ("gS2r", 6, 0), ("gSr", 3, 0), ("gS2s", 3, 0), ("gZs", 1, 3), ("g1r", 0, 0), ("gSs", 2, 0), ("gS2r", 4, 0), ("gSr", 1, 0), ("g2r", 0, 0), ("gZr", 1, 1), ("gZr", 1, 2), ("gS2s", 0, 0), ("gF2r", 5, 0), ("gSr", 2, 2), ("gZs", 2, 3), ("gS2r", 3, 0), ("gSr", 2, 0), ("gZr", 1, 3), ("vr", 2, 0), ("gC2r", 5, 0), ("gZs", 2, 2), ("vs", 3, 0), ("gZr", 2, 1), ("gS2s", 1, 0), ("gS2r", 0, 0), ("gF2r", 3, 0), ("vr", 3, 0), ("gF2r", 4, 0), ("gZr", 2, 2), ("gZr", 2, 3), ("gS2s", 2, 0), ("vs", 4, 0), ("gF2r", 6, 0), ("gd2Fr", 1, 0), ("gC2r", 6, 0), ("gd2Sr", 1, 0), ("gF2r", 1, 0), ("gF2r", 0, 0), ("gd2Fr", 2, 0), ("gC2r", 4, 0), ("gd2Sr", 2, 0), ("gF2r", 2, 0), ("gC2r", 0, 0), ("vr", 4, 0), ("gC2r", 3, 0), ("gC2r", 1, 0), ("gC2r", 2, 0),),
    },
}
V_OB, V_G1, V_S1, V_EB, V_G2, V_S2 = 8, 9, 10, 11, 12, 13


def dot(left, right, dims):
    return lax.dot_general(left, right, dims, preferred_element_type=F32)


def depth_at(p, stage):
    done = SUMMED[p][3].split(stage)[0]
    return ("F" in done) + ("S" in done)


def z_rows(p, slot):
    sizes = {}
    for q, (_, _, n, chain) in enumerate(SUMMED):
        for t in range(3):
            sizes[q, t] = n >> depth_at(q, "Z" if "Z" in chain else "112"[t])
    return sum(n for key, n in sizes.items() if key < (p, slot)), sizes[p, slot]


def layer_kernel(
    cfg,
    tok, cot, wq, wk, wv, wo, wi, wout, bq, bv, bi, bo, g1, s1, be, g2, s2, seg_in, live_in,
    out_ref, dx_ref, whole, vec_ref,
    wbuf, bias, xs, cots, qkv, ka, ks, prob, mask, acc, tmp, nh1, r1,
    nb, nhalf, af, asib, al, gp, g, sg, di, fg,
    gr, rf, rz, rs, rx, vrecv, vin,
    seg, live, *rest,
):
    n_dp, d, seq, rows = cfg["dp"], cfg["d"], cfg["seq"], cfg["rows"]
    tl = seq * rows
    ml = d // 4
    hs = ml // DH
    half, qtr, eig = d // 2, d // 4, d // 8
    scale = DH ** (-0.5)
    bits = n_dp.bit_length() - 1
    dp, z = lax.axis_index("dp"), lax.axis_index("mp")
    c = dp % 2
    df = 2 + 2 * c
    ds_ = 6 - df
    f, s = (dp // df) % 2, (dp // ds_) % 2
    p_x = dp + df * (1 - 2 * f) + ds_ * (1 - 2 * s)
    p_f, p_s, p_c = dp + df * (1 - 2 * f), dp + ds_ * (1 - 2 * s), dp + 1 - 2 * c
    z0, zh = z % 2, z // 2
    z1, z2, z3 = z + 1 - 2 * z0, z + 2 - 4 * zh, 3 - z
    h0 = pl.multiple_of(c * half, 128)
    ho = pl.multiple_of((1 - c) * half, 128)

    def sub(base, n, depth, other=False):
        off = base
        for level, bit in enumerate((c, f, s)[:depth]):
            n //= 2
            off = off + n * (1 - bit if other and level == depth - 1 else bit)
        return (pl.multiple_of(off, 16) if depth else off), n

    def cut(base, n, depth, other=False):
        off = base
        for level, bit in enumerate((f, s)[:depth]):
            n //= 2
            off = off + n * (1 - bit if other and level == depth - 1 else bit)
        return (pl.multiple_of(off, 16) if depth else off), n

    gathered = {}
    for a, (piece, base, n, cuts) in enumerate(GATHERED):
        for depth in (1, 2, 3):
            for other in (False, True):
                gathered[a, depth, other] = sub(base, n, depth, other)
    summed = {}
    for p, (piece, base, n, chain) in enumerate(SUMMED):
        for depth in (0, 1, 2):
            for other in (False, True):
                summed[p, depth, other] = cut(base, n, depth, other)

    finals = {}
    for p, (piece, base, n, chain) in enumerate(SUMMED):
        for depth in (0, 1, 2):
            for other in (False, True):
                off, m = summed[p, depth, other]
                finals[p, depth, other] = (pl.multiple_of(c * half + off, 16), m)
        finals[p, "core", True] = (pl.multiple_of((1 - c) * half + base, 16), n)
    shard = (z, z1, z2, z3)

    def shard_of(k):
        k0, kh = k % 2, k // 2
        return z0 + k0 - 2 * z0 * k0 + 2 * (zh + kh - 2 * zh * kh)

    def remote(src, dst, ssem, rsem, dev):
        return pltpu.make_async_remote_copy(
            src_ref=src, dst_ref=dst, send_sem=ssem, recv_sem=rsem, device_id=dev, device_id_type=MESH
        )

    pending = []

    def send(make):
        remote(*make()).start()
        pending.append(make)

    small = rest[:9]
    loc_sem, ag_s, ag_r, gr_s, gr_r, x_s, x_r, b_s, b_r, v_s, v_r, e_s, e_r = rest[9:]
    barrier = pltpu.get_barrier_semaphore()
    extra = [dp + (1 << b) * (1 - 2 * ((dp // (1 << b)) % 2)) for b in range(3, bits)]
    greet = [(p_c, z), (p_f, z), (p_s, z), (p_x, z), (dp, z1), (dp, z2), (dp, z3)] + [(e, z) for e in extra]
    for dev in greet:
        pl.semaphore_signal(barrier, inc=1, device_id=dev, device_id_type=MESH)
    att_loads = [
        pltpu.make_async_copy(ref, wbuf.at[ATT, z, pl.ds(j * ml, ml)], loc_sem.at[j])
        for j, ref in enumerate((wq, wk, wv, wo))
    ]
    vec_loads = [
        pltpu.make_async_copy(ref, dst, loc_sem.at[4 + j])
        for j, (ref, dst) in enumerate(zip((bq, bv, bi, bo, g1, s1, be, g2, s2), small))
    ]
    seg_loads = [
        pltpu.make_async_copy(seg_in, seg, loc_sem.at[13]),
        pltpu.make_async_copy(live_in, live, loc_sem.at[14]),
        pltpu.make_async_copy(tok, xs.at[pl.ds(0, rows)], loc_sem.at[15]),
    ]
    late_loads = [
        pltpu.make_async_copy(wi, wbuf.at[INN, z], loc_sem.at[16]),
        pltpu.make_async_copy(wout, wbuf.at[OUT, z], loc_sem.at[17]),
        pltpu.make_async_copy(cot, cots, loc_sem.at[18]),
    ]
    for cp in att_loads + vec_loads + seg_loads + late_loads:
        cp.start()
    for cp in att_loads:
        cp.wait()
    pl.semaphore_wait(barrier, len(greet))

    def own(piece, off, n):
        if piece == ATT:
            return wbuf.at[ATT, z, pl.ds(off, n)]
        return (wi, wout)[piece - 1].at[pl.ds(off, n)]

    def reg(piece, k, off, n):
        return wbuf.at[piece, shard[k], pl.ds(off, n)]

    def ag_send(a, slot, k, rows_of, dev, mine=False):
        piece = GATHERED[a][0]

        def make():
            region = reg(piece, k, *rows_of)
            return own(piece, *rows_of) if mine else region, region, ag_s.at[a, slot], ag_r.at[a, slot], dev

        send(make)

    def ag_wait(a, slot, k, rows_of):
        region = reg(GATHERED[a][0], k, *rows_of)
        remote(region, region, ag_s.at[a, slot], ag_r.at[a, slot], (dp, z1)).wait_recv()

    def first(a):
        return gathered[a, GATHERED[a][3], False]

    def a_z1(a, _):
        ag_send(a, 1, 0, first(a), (dp, z1), True)

    def a_z2(a, _):
        ag_send(a, 0, 0, first(a), (dp, z2), True)

    def a_zf(a, _):
        ag_wait(a, 0, 2, first(a))
        ag_send(a, 2, 2, first(a), (dp, z1))

    def a_arrive(a, k):
        if k != 2:
            ag_wait(a, {1: 1, 3: 2}[k], k, first(a))

    def a_s(a, k):
        a_arrive(a, k)
        ag_send(a, 2 + k, k, gathered[a, 3, False], (p_s, z))

    def a_f(a, k):
        if GATHERED[a][3] < 3:
            a_arrive(a, k)
        else:
            ag_wait(a, 2 + k, k, gathered[a, 3, True])
        ag_send(a, 5 + k, k, gathered[a, 2, False], (p_f, z))

    def a_c(a, k):
        if GATHERED[a][3] < 2:
            a_arrive(a, k)
        else:
            ag_wait(a, 5 + k, k, gathered[a, 2, True])
        ag_send(a, 8 + k, k, gathered[a, 1, False], (p_c, z))

    def a_d(a, k):
        ag_wait(a, 8 + k, k, gathered[a, 1, True])

    X_TOK, X_N, X_FG, X_A, X_DI, X_KA, X_G = 0, 1, 2, 4, 8, 12, 16

    def core_send(slot, pair):
        send(lambda: (*pair(), x_s.at[slot], x_r.at[slot], (p_c, z)))

    def core_wait(slot, dst):
        remote(dst, dst, x_s.at[slot], x_r.at[slot], (p_c, z)).wait_recv()

    def g_sem(p, slot):
        return gr_s.at[p, slot], gr_r.at[p, slot]

    def g_send(p, slot, pair, dev):
        send(lambda: (*pair(), *g_sem(p, slot), dev))

    def g_wait(p, slot, dst):
        remote(dst, dst, *g_sem(p, slot), (dp, z1)).wait_recv()

    def add_into(dst, src, n):
        m = 48 if n % 48 == 0 else (32 if n % 32 == 0 else 16)

        def blk(j, carry):
            sl = pl.ds(pl.multiple_of(j * m, 16), m)
            dst[sl, :] = (dst[sl, :].astype(F32) + src[sl, :].astype(F32)).astype(BF)
            return carry

        lax.fori_loop(0, n // m, blk, 0)

    def chunk(p, k, depth, other=False):
        off, n = summed[p, depth, other]
        return gr.at[SUMMED[p][0], k, pl.ds(off, n)]

    def final(p, depth, other=False):
        off, n = finals[p, depth, other]
        return whole.at[SUMMED[p][0], pl.ds(off, n)]

    def final_across(p, side):
        _, base, n, _ = SUMMED[p]
        off = pl.multiple_of(c * half + base + (1 - f) * (n // 2) + side * (n // 4), 16)
        return whole.at[SUMMED[p][0], pl.ds(off, n // 4)]

    def f_slot(p, k):
        piece, base, n, _ = SUMMED[p]
        return rf.at[piece, k, pl.ds(base // 2, n // 2)]

    def s_slot(p, k):
        piece, base, n, _ = SUMMED[p]
        return rs.at[piece, k, pl.ds(base // 4, n // 4)]

    def z_slot(p, slot):
        return rz.at[pl.ds(*z_rows(p, slot))]

    def g_fs(p, k):
        g_send(p, k, lambda: (chunk(p, k, 1, True), f_slot(p, k)), (p_f, z))

    def g_fr(p, k):
        g_wait(p, k, f_slot(p, k))
        add_into(chunk(p, k, 1), f_slot(p, k), SUMMED[p][2] // 2)

    def g_ss(p, k):
        g_send(p, 4 + k, lambda: (chunk(p, k, 2, True), s_slot(p, k)), (p_s, z))

    def g_sr(p, k):
        g_wait(p, 4 + k, s_slot(p, k))
        add_into(chunk(p, k, 2), s_slot(p, k), SUMMED[p][2] // 4)

    def g_1s(p, k):
        slot = 0 if k == 3 else 1
        g_send(p, 8 + slot, lambda: (chunk(p, k, depth_at(p, "1")), z_slot(p, slot)), (dp, z1))

    def g_1r(p, k):
        slot = 0 if k == 2 else 1
        g_wait(p, 8 + slot, z_slot(p, slot))
        depth = depth_at(p, "1")
        add_into(chunk(p, k, depth), z_slot(p, slot), SUMMED[p][2] >> depth)

    def g_2s(p, k):
        g_send(p, 10, lambda: (chunk(p, 2, depth_at(p, "2")), z_slot(p, 2)), (dp, z2))

    def g_2r(p, k):
        g_wait(p, 10, z_slot(p, 2))
        depth = depth_at(p, "2")
        add_into(chunk(p, 0, depth), z_slot(p, 2), SUMMED[p][2] >> depth)

    def g_zs(p, k):
        depth = depth_at(p, "Z")
        g_send(p, 7 + k, lambda: (chunk(p, k, depth), z_slot(p, k - 1)), (dp, shard[k]))

    def g_zr(p, k):
        depth = depth_at(p, "Z")
        g_wait(p, 7 + k, z_slot(p, k - 1))
        add_into(chunk(p, 0, depth), z_slot(p, k - 1), SUMMED[p][2] >> depth)

    def g_s2s(p, _):
        piece, base, n, _ = SUMMED[p]
        for j, partner in enumerate(extra):
            slot = rx.at[piece, j, pl.ds(base // 4, n // 4)]
            cp = remote(chunk(p, 0, 2), slot, e_s.at[p, j], e_r.at[p, j], (partner, z))
            cp.start()
            cp.wait()
            add_into(chunk(p, 0, 2), slot, n // 4)
        mine, target = chunk(p, 0, 2), final(p, 2)
        for lo in range(0, n // 4, 16):
            target[pl.ds(lo, 16), :] = mine[pl.ds(lo, 16), :]
        g_send(p, 11, lambda: (final(p, 2),) * 2, (p_s, z))
        if SUMMED[p][3].endswith("d"):
            g_send(p, 12, lambda: (final(p, 2),) * 2, (p_f, z))
            g_send(p, 14, lambda: (final(p, 2),) * 2, (p_x, z))

    def g_s2r(p, _):
        g_wait(p, 11, final(p, 2, True))
        g_send(p, 12, lambda: (final(p, 1),) * 2, (p_f, z))

    def g_d2sr(p, _):
        g_wait(p, 11, final(p, 2, True))

    def g_d2fr(p, _):
        g_wait(p, 12, final_across(p, s))

    def g_f2r(p, _):
        if SUMMED[p][3].endswith("d"):
            g_wait(p, 14, final_across(p, 1 - s))
        else:
            g_wait(p, 12, final(p, 1, True))
        g_send(p, 13, lambda: (final(p, 0),) * 2, (p_c, z))

    def g_c2r(p, _):
        g_wait(p, 13, final(p, "core", True))

    partners = [(p_c, z), (p_f, z), (p_s, z), (dp, z1), (dp, z2)] + [(e, z) for e in extra]

    def v_copy(j):
        return remote(vec_ref, vrecv.at[j], v_s.at[j], v_r.at[j], partners[j])

    def v_send(j, _):
        v_copy(j).start()

    def v_recv(j, _):
        v_copy(j).wait()
        vec_ref[...] += vrecv[j]

    events = {
        "az1": a_z1, "az2": a_z2, "zf": a_zf, "s": a_s, "f": a_f, "c": a_c, "d": a_d,
        "gFs": g_fs, "gFr": g_fr, "gSs": g_ss, "gSr": g_sr, "g1s": g_1s, "g1r": g_1r, "g2s": g_2s, "g2r": g_2r,
        "gZs": g_zs, "gZr": g_zr, "gd2Fr": g_d2fr, "gd2Sr": g_d2sr, "gS2s": g_s2s, "gS2r": g_s2r, "gF2r": g_f2r, "gC2r": g_c2r, "vs": v_send, "vr": v_recv,
    }

    def do(listed):
        for kind, piece, k in listed:
            events[kind](piece, k)

    def at(place, index):
        for n, listed in PLAN.get(place, {}).items():
            pl.when(index == n)(functools.partial(do, listed))

    def once(place):
        do(PLAN.get(place, {}).get(0, ()))

    once("x0")
    for cp in vec_loads:
        cp.wait()
    vin[...] = jnp.zeros_like(vin)
    vin[pl.ds(0, 1), pl.ds(0, ml)] = small[0][...].astype(F32).reshape(1, ml)
    vin[pl.ds(0, 1), pl.ds(2 * ml, ml)] = small[1][...].astype(F32).reshape(1, ml)
    for j, ref in enumerate(small[2:]):
        vin[pl.ds(j + 1, 1), :] = ref[...].astype(F32).reshape(1, d)
    bias[z] = vin[...]
    for j, zz in enumerate((z1, z2, z3)):
        send(lambda j=j, zz=zz: (vin, bias.at[z], b_s.at[j], b_r.at[j], (dp, zz)))
    core_send(X_TOK, lambda: (tok, xs.at[pl.ds(rows, rows)]))
    for cp in seg_loads:
        cp.wait()

    for r in range(rows):
        seg_row = seg[pl.ds(z * rows + r, 1), :]
        live_row = live[pl.ds(z * rows + r, 1), :]
        code = jnp.where(live_row == 1, seg_row, -1)
        ids = lax.broadcasted_iota(jnp.int32, (8, seq), 0)
        key_hot = (jnp.broadcast_to(code, (8, seq)) == ids).astype(F32).astype(BF)
        query_hot = (jnp.broadcast_to(seg_row, (8, seq)) == ids).astype(F32).astype(BF)
        mask[r] = jnp.where(dot(key_hot, query_hot, TN) > 0.5, 0.0, NEG_FILL)
    acc[...] = jnp.zeros_like(acc)
    first_row = (lax.broadcasted_iota(jnp.int32, (8, seq), 0) == 0).astype(F32).astype(BF)

    def attend(i, carry):
        t = shard_of(i)

        def row(r, inner_carry):
            at("att", i * rows + r)

            @pl.when((i == 1) & (r == 0))
            def _():
                for j, zz in enumerate((z1, z2, z3)):
                    remote(vin, bias.at[zz], b_s.at[j], b_r.at[j], (dp, zz)).wait_recv()

            x_row = xs[r]
            bias_rows = bias[t].astype(BF)[:, : 3 * ml]
            qkv[t, r] = (
                dot(wbuf[ATT, t, pl.ds(0, 3 * ml), :], x_row, NT) + dot(bias_rows, first_row, TN)
            ).astype(BF)
            for h in range(hs):
                query = qkv[t, r, pl.ds(h * DH, DH), :]
                key = qkv[t, r, pl.ds(ml + h * DH, DH), :]
                value = qkv[t, r, pl.ds(2 * ml + h * DH, DH), :]
                scores = dot(key, query, TN) * scale + mask[r]
                top = jnp.max(scores, 0, keepdims=True)
                exponent = jnp.exp(scores - top)
                total = jnp.sum(exponent, 0, keepdims=True)
                prob_t = (exponent * (1.0 / total)).astype(BF)
                prob[t, r, h] = prob_t
                ka[t, r, pl.ds(3 * ml + h * DH, DH), :] = dot(value, prob_t, NN).astype(BF)
            part_sum = dot(ka[t, r, pl.ds(3 * ml, ml), :], wbuf[ATT, t, pl.ds(3 * ml, ml), :], TN)
            sl = pl.ds(pl.multiple_of(r * seq, 16), seq)
            acc[sl, :] = acc[sl, :] + part_sum
            return inner_carry

        lax.fori_loop(0, rows, row, 0)
        return carry

    lax.fori_loop(0, 4, attend, 0)

    rb = seq

    def norm_rows(summed):
        mean = jnp.mean(summed, -1, keepdims=True)
        centred = summed - mean
        variance = jnp.mean(centred * centred, -1, keepdims=True)
        rs_ = lax.rsqrt(variance + EPSILON)
        return centred * rs_, rs_

    def norm_back(grad, hat, rs_):
        return rs_ * (grad - jnp.mean(grad, -1, keepdims=True) - hat * jnp.mean(grad * hat, -1, keepdims=True))

    def vrow(j):
        return vin[pl.ds(j, 1), :]

    once("n1")

    def norm1(j, carry):
        sl = pl.ds(pl.multiple_of(j * rb, 16), rb)
        per = seq // rb
        x_blk = xs[j // per, pl.ds(pl.multiple_of((j % per) * rb, 16), rb), :].astype(F32)
        hat, rs_ = norm_rows(acc[sl, :] + vrow(2) + x_blk)
        nh1[sl, :] = hat
        r1[sl, :] = jnp.broadcast_to(rs_, (rb, 128))
        nb[sl, :] = (hat * vrow(3) + vrow(4)).astype(BF)
        acc[sl, :] = jnp.zeros((rb, d), F32)
        return carry

    lax.fori_loop(0, tl // rb, norm1, 0)
    core_send(X_N, lambda: (nb.at[:, pl.ds(ho, half)], nhalf.at[pl.ds(tl, tl)]))
    nhalf[pl.ds(0, tl), :] = nb[:, pl.ds(h0, half)]

    late_loads[0].wait()

    def up(i, carry):
        at("up", i)
        t = shard_of(i)
        tmp[...] = dot(nb[...], wbuf[INN, t], NN)
        b_row = bias[t, pl.ds(1, 1), :]

        def act(j, carry):
            sl = pl.ds(pl.multiple_of(j * rb, 16), rb)
            u = tmp[sl, :] + b_row
            cdf = 0.5 * (1.0 + lax.erf(u * ROOT_HALF))
            af[t, sl, :] = (u * cdf).astype(BF)
            gp[t, sl, :] = (cdf + u * (PDF_SCALE * jnp.exp(-0.5 * u * u))).astype(BF)
            return carry

        lax.fori_loop(0, tl // rb, act, 0)
        remote(af.at[t, :, pl.ds(ho, half)], asib.at[t], x_s.at[X_A + i], x_r.at[X_A + i], (p_c, z)).start()
        return carry

    lax.fori_loop(0, 4, up, 0)
    late_loads[1].wait()
    late_loads[2].wait()

    def down(i, carry):
        at("dn", i)
        t = shard_of(i)
        acc[...] += dot(af[t], wbuf[OUT, t], NN)
        return carry

    lax.fori_loop(0, 4, down, 0)

    once("l2")
    vec_ref[...] = jnp.zeros_like(vec_ref)

    def add_vec(row, value):
        vec_ref[pl.ds(row, 1), :] = vec_ref[pl.ds(row, 1), :] + value

    def norm2(j, carry):
        sl = pl.ds(pl.multiple_of(j * rb, 16), rb)
        normed = nh1[sl, :] * vrow(3) + vrow(4)
        hat, rs_ = norm_rows(acc[sl, :] + vrow(5) + normed)
        c_blk = cots[sl, :].astype(F32)
        out_ref[sl, :] = (hat * vrow(6) + vrow(7)).astype(BF)
        back = norm_back(c_blk * vrow(6), hat, rs_)
        sg[sl, :] = back
        g[sl, :] = back.astype(BF)
        acc[sl, :] = jnp.zeros((rb, d), F32)
        add_vec(V_G2, jnp.sum(c_blk * hat, 0, keepdims=True))
        add_vec(V_S2, jnp.sum(c_blk, 0, keepdims=True))
        add_vec(V_EB, jnp.sum(back, 0, keepdims=True))
        return carry

    def g_copy(j):
        src = g.at[pl.ds(pl.multiple_of(j * rb, 16), rb)]
        dst = g.at[pl.ds(pl.multiple_of(tl + j * rb, 16), rb)]
        return remote(src, dst, x_s.at[X_G + j], x_r.at[X_G + j], (p_c, z))

    for j in range(tl // rb):
        norm2(j, 0)
        g_copy(j).start()
    def order(i):
        return 3 - 2 * (i % 2) - i // 2

    def ffn_back(i, carry):
        @pl.when(i < 4)
        def _():
            at("da", i)
            k = order(i)
            t = shard_of(k)
            tmp[...] = dot(g[pl.ds(0, tl), :], wbuf[OUT, t], NT)

            def act(j, total):
                sl = pl.ds(pl.multiple_of(j * rb, 16), rb)
                blk = (tmp[sl, :] * gp[t, sl, :].astype(F32)).astype(BF)
                di[t, sl, :] = blk
                return total + jnp.sum(blk.astype(F32), 0, keepdims=True)

            vec_ref[pl.ds(4 + t, 1), :] = lax.fori_loop(0, tl // rb, act, jnp.zeros((1, d), F32))
            remote(
                di.at[t, pl.ds(0, tl)], di.at[t, pl.ds(tl, tl)], x_s.at[X_DI + k], x_r.at[X_DI + k], (p_c, z)
            ).start()
            at("gwo", i)

            @pl.when(i == 0)
            def _():
                for j in range(tl // rb):
                    g_copy(j).wait_recv()
                core_wait(X_N, nhalf.at[pl.ds(tl, tl)])

            core_wait(X_A + k, asib.at[t])
            al[pl.ds(0, tl), :] = af[t, :, pl.ds(h0, half)]
            al[pl.ds(tl, tl), :] = asib[t]
            gr[OUT, k] = dot(al[...], g[...], TN).astype(BF)
            at("dn2", i)
            acc[...] += dot(di[t, pl.ds(0, tl), :], wbuf[INN, t], NT)

        @pl.when(i > 0)
        def _():
            at("gwi", i - 1)
            k = order(i - 1)
            t = shard_of(k)
            core_wait(X_DI + k, di.at[t, pl.ds(tl, tl)])
            gr[INN, k] = dot(nhalf[...], di[t], TN).astype(BF)

        return carry

    lax.fori_loop(0, 5, ffn_back, 0)
    once("l1b")

    def norm1_back(j, carry):
        sl = pl.ds(pl.multiple_of(j * rb, 16), rb)
        per = seq // rb
        hat = nh1[sl, :]
        total = acc[sl, :] + sg[sl, :]
        back = norm_back(total * vrow(3), hat, r1[sl, 0:1])
        sg[sl, :] = back
        fg[j // per, pl.ds(pl.multiple_of((j % per) * rb, 16), rb), :] = back.astype(BF)
        acc[sl, :] = jnp.zeros((rb, d), F32)
        add_vec(V_G1, jnp.sum(total * hat, 0, keepdims=True))
        add_vec(V_S1, jnp.sum(total, 0, keepdims=True))
        add_vec(V_OB, jnp.sum(back, 0, keepdims=True))
        return carry

    lax.fori_loop(0, tl // rb, norm1_back, 0)
    core_send(X_FG, lambda: (fg.at[pl.ds(0, rows)], fg.at[pl.ds(rows, rows)]))
    ones = jnp.ones((8, seq), BF)

    def att_back(i, carry):
        @pl.when(i < 4)
        def _():
            k = order(i)
            t = shard_of(k)

            def row(r, inner_carry):
                at("ab", i * rows + r)
                dctx = dot(wbuf[ATT, t, pl.ds(3 * ml, ml), :], fg[r], NT).astype(BF)
                for h in range(hs):
                    query = qkv[t, r, pl.ds(h * DH, DH), :]
                    key = qkv[t, r, pl.ds(ml + h * DH, DH), :]
                    value = qkv[t, r, pl.ds(2 * ml + h * DH, DH), :]
                    prob_t = prob[t, r, h]
                    grad = dctx[h * DH : (h + 1) * DH]
                    ka[t, r, pl.ds(2 * ml + h * DH, DH), :] = dot(grad, prob_t, NT).astype(BF)
                    prob_grad = dot(value, grad, TN)
                    wide_prob = prob_t.astype(F32)
                    inner = jnp.sum(wide_prob * prob_grad, 0, keepdims=True)
                    score_grad = (wide_prob * (prob_grad - inner)).astype(BF)
                    ka[t, r, pl.ds(h * DH, DH), :] = (dot(key, score_grad, NN) * scale).astype(BF)
                    ka[t, r, pl.ds(ml + h * DH, DH), :] = (dot(query, score_grad, NT) * scale).astype(BF)
                grads = ka[t, r, pl.ds(0, 3 * ml), :]
                vec_ref[pl.ds(t, 1), pl.ds(0, 3 * ml)] += dot(ones, grads, NT)[0:1]
                sl = pl.ds(pl.multiple_of(r * seq, 16), seq)
                acc[sl, :] = acc[sl, :] + dot(grads, wbuf[ATT, t, pl.ds(0, 3 * ml), :], TN)
                return inner_carry

            lax.fori_loop(0, rows, row, 0)
            remote(
                ka.at[t, :, pl.ds(ho, half)], ks.at[t], x_s.at[X_KA + k], x_r.at[X_KA + k], (p_c, z)
            ).start()

        @pl.when(i == 0)
        def _():
            core_wait(X_TOK, xs.at[pl.ds(rows, rows)])
            core_wait(X_FG, fg.at[pl.ds(rows, rows)])

        @pl.when(i > 0)
        def _():
            at("gwa", i - 1)
            k = order(i - 1)
            t = shard_of(k)
            core_wait(X_KA + k, ks.at[t])
            for j in range(2):
                rowsel = pl.ds(pl.multiple_of(h0 + j * ml, 16), ml)
                use = c * j
                total = jnp.zeros((ml, d), F32)
                for r in range(rows):
                    right_own = xs[r] if j == 0 else jnp.where(use == 1, fg[r], xs[r])
                    right_sib = xs[rows + r] if j == 0 else jnp.where(use == 1, fg[rows + r], xs[rows + r])
                    total += dot(ka[t, r, rowsel, :], right_own, NN)
                    total += dot(ks[t, r, pl.ds(j * ml, ml), :], right_sib, NN)
                gr[ATT, k, pl.ds(j * ml, ml), :] = total.astype(BF)

        return carry

    lax.fori_loop(0, 5, att_back, 0)
    once("fin")

    def finish(j, carry):
        sl = pl.ds(pl.multiple_of(j * rb, 16), rb)
        dx_ref[sl, :] = (sg[sl, :] + acc[sl, :]).astype(BF)
        return carry

    lax.fori_loop(0, tl // rb, finish, 0)


    once("end")
    for j in range(5, len(partners)):
        v_send(j, 0)
        v_recv(j, 0)

    for make in pending:
        remote(*make()).wait_send()

    def sent(k, carry):
        t = shard_of(k)
        remote(af.at[t, :, pl.ds(ho, half)], asib.at[t], x_s.at[X_A + k], x_r.at[X_A + k], (p_c, z)).wait_send()
        remote(
            di.at[t, pl.ds(0, tl)], di.at[t, pl.ds(tl, tl)], x_s.at[X_DI + k], x_r.at[X_DI + k], (p_c, z)
        ).wait_send()
        remote(ka.at[t, :, pl.ds(ho, half)], ks.at[t], x_s.at[X_KA + k], x_r.at[X_KA + k], (p_c, z)).wait_send()
        return carry

    lax.fori_loop(0, 4, sent, 0)
    for j in range(tl // rb):
        g_copy(j).wait_send()


def spread_kernel(
    ml, grads, vec, out_in, dx_in,
    out_ref, dx_ref, gq, gk, gv, go, gi, ge, bq, bv, bo, g1, s1, bi, be, g2, s2,
    wide_v, sem,
):
    z = lax.axis_index("mp")
    n = 2 * ml
    outs = []

    def put(src, dst):
        cp = pltpu.make_async_copy(src, dst, sem.at[len(outs)])
        cp.start()
        outs.append(cp)

    put(out_in, out_ref)
    put(dx_in, dx_ref)
    steps = [(piece, lo, [(ref, lo, n)]) for piece, ref in ((1, gi), (2, ge)) for lo in (0, n)]
    steps += [(0, 0, [(gq, 0, ml), (gk, 0, ml)]), (0, n, [(gv, 0, ml), (go, 0, ml)])]
    for piece, lo, refs in steps:
        wide_v[piece, pl.ds(lo, n), :] = grads[piece, pl.ds(lo, n), :].astype(F32)
        at = lo
        for ref, row, m in refs:
            put(wide_v.at[piece, pl.ds(at, m)], ref.at[pl.ds(row, m)])
            at += m
    bq[...] = vec[pl.ds(z, 1), pl.ds(0, ml)].reshape(ml)
    bv[...] = vec[pl.ds(z, 1), pl.ds(2 * ml, ml)].reshape(ml)
    bi[...] = vec[pl.ds(4 + z, 1), :].reshape(4 * ml)
    for row, ref in ((V_OB, bo), (V_G1, g1), (V_S1, s1), (V_EB, be), (V_G2, g2), (V_S2, s2)):
        ref[...] = vec[pl.ds(row, 1), :].reshape(4 * ml)
    for cp in outs:
        cp.wait()


def per_device(
    n_dp,
    tokens, segment_ids, live_mask, query_weight, key_weight, value_weight, query_bias, value_bias,
    output_weight, output_bias, first_gain, first_shift, inner_weight, inner_bias, outer_weight,
    outer_bias, second_gain, second_shift, cotangent,
):
    tl, d = tokens.shape
    seq_rows, seq = segment_ids.shape
    rows = tl // seq
    ml = query_weight.shape[1]
    ff = inner_weight.shape[1]
    half, qtr, eig = d // 2, d // 4, d // 8
    bits = n_dp.bit_length() - 1
    n_extra = max(bits - 3, 1)
    n_vec = bits + 2
    cfg = {"dp": n_dp, "d": d, "seq": seq, "rows": rows}
    vmem = pl.BlockSpec(memory_space=pltpu.VMEM)
    hbm = pl.BlockSpec(memory_space=pl.ANY)
    scratch = [
        pltpu.VMEM((3, 4, d, d), BF),
        pltpu.VMEM((4, 8, d), F32),
        pltpu.VMEM((2 * rows, seq, d), BF),
        pltpu.VMEM((tl, d), BF),
        pltpu.VMEM((4, rows, 3 * ml, seq), BF),
        pltpu.VMEM((4, rows, d, seq), BF),
        pltpu.VMEM((4, rows, half, seq), BF),
        pltpu.VMEM((4, rows, ml // DH, seq, seq), BF),
        pltpu.VMEM((rows, seq, seq), F32),
        pltpu.VMEM((tl, d), F32),
        pltpu.VMEM((tl, d), F32),
        pltpu.VMEM((tl, d), F32),
        pltpu.VMEM((tl, 128), F32),
        pltpu.VMEM((tl, d), BF),
        pltpu.VMEM((2 * tl, half), BF),
        pltpu.VMEM((4, tl, d), BF),
        pltpu.VMEM((4, tl, half), BF),
        pltpu.VMEM((2 * tl, half), BF),
        pltpu.VMEM((4, tl, d), BF),
        pltpu.VMEM((2 * tl, d), BF),
        pltpu.VMEM((tl, d), F32),
        pltpu.VMEM((4, 2 * tl, d), BF),
        pltpu.VMEM((2 * rows, seq, d), BF),
        pltpu.VMEM((3, 4, half, d), BF),
        pltpu.VMEM((3, 4, qtr, d), BF),
        pltpu.VMEM((sum(z_rows(len(SUMMED) - 1, 2)), d), BF),
        pltpu.VMEM((3, 4, eig, d), BF),
        pltpu.VMEM((3, n_extra, eig, d), BF) if bits > 3 else pltpu.VMEM((1, 1, 16, 128), BF),
        pltpu.VMEM((n_vec, 16, d), F32),
        pltpu.VMEM((8, d), F32),
        pltpu.VMEM((seq_rows, seq), jnp.int32),
        pltpu.VMEM((seq_rows, seq), jnp.int32),
    ]
    scratch += [pltpu.VMEM((n,), BF) for n in (ml, ml, ff, d, d, d, d, d, d)]
    scratch += [
        pltpu.SemaphoreType.DMA(shape)
        for shape in [(24,)] + [(len(GATHERED), 12)] * 2 + [(len(SUMMED), 15)] * 2 + [(16 + rows,)] * 2 + [(3,)] * 2
        + [(n_vec,)] * 2 + [(len(SUMMED), n_extra)] * 2
    ]
    out, dx, grads, vec = pl.pallas_call(
        functools.partial(layer_kernel, cfg),
        out_shape=(
            pltpu.VMEM((tl, d), BF),
            pltpu.VMEM((tl, d), BF),
            pltpu.VMEM((3, d, d), BF),
            pltpu.VMEM((16, d), F32),
        ),
        in_specs=[hbm] * 19,
        out_specs=(vmem,) * 4,
        scratch_shapes=scratch,
        compiler_params=pltpu.CompilerParams(
            collective_id=0, has_side_effects=True, vmem_limit_bytes=LIMIT
        ),
        name="layer",
    )(
        tokens.reshape(rows, seq, d), cotangent, query_weight.T, key_weight.T, value_weight.T, output_weight,
        inner_weight, outer_weight, query_bias, value_bias, inner_bias, output_bias, first_gain, first_shift,
        outer_bias, second_gain, second_shift, segment_ids, live_mask,
    )
    out, dx, gq, gk, gv, go, gi, ge, bq, bv, bo, g1, s1, bi, be, g2, s2 = pl.pallas_call(
        functools.partial(spread_kernel, ml),
        out_shape=tuple(
            jax.ShapeDtypeStruct(shape, dtype)
            for shape, dtype in [((tl, d), BF)] * 2
            + [((ml, d), F32)] * 4
            + [((d, ff), F32), ((ff, d), F32)]
            + [((ml,), F32)] * 2
            + [((d,), F32)] * 7
        ),
        in_specs=[vmem] * 4,
        out_specs=(hbm,) * 8 + (vmem,) * 9,
        scratch_shapes=[pltpu.VMEM((3, d, d), F32), pltpu.SemaphoreType.DMA((10,))],
        compiler_params=pltpu.CompilerParams(vmem_limit_bytes=24 * 1024 * 1024),
        name="spread",
    )(*(pltpu.with_memory_space_constraint(x, pltpu.VMEM) for x in (grads, vec, out, dx)))
    return out, dx, gq.T, gk.T, gv.T, bq, bv, go, bo, g1, s1, gi, bi, ge, be, g2, s2


def solution(mesh):
    tok, shared = P(("dp", "mp"), None), P()
    cols, rows, vec = P(None, "mp"), P("mp", None), P("mp")
    in_specs = (
        tok, P("dp", None), P("dp", None), cols, cols, cols, vec, vec, rows, shared, shared, shared,
        cols, vec, rows, shared, shared, shared, tok,
    )
    out_specs = (
        tok, tok, cols, cols, cols, vec, vec, rows, shared, shared, shared, cols, vec, rows,
        shared, shared, shared,
    )
    return jax.shard_map(
        functools.partial(per_device, mesh.shape["dp"]),
        mesh=mesh,
        in_specs=in_specs,
        out_specs=out_specs,
        check_vma=False,
    )
```

```python
import functools

import jax
import jax.numpy as jnp
from jax import lax
from jax.experimental import pallas as pl
from jax.experimental.pallas import tpu as pltpu
from jax.sharding import PartitionSpec as P

DH = 64
EPSILON = 1e-06
NEG_FILL = -1000000000.0
ROOT_HALF = 0.7071067811865476
PDF_SCALE = 0.3989422804014327
BF = jnp.bfloat16
F32 = jnp.float32
MESH = pl.DeviceIdType.MESH
LIMIT = 59 * 1024 * 1024

NN = (((1,), (0,)), ((), ()))
NT = (((1,), (1,)), ((), ()))
TN = (((0,), (0,)), ((), ()))

ATT, INN, OUT = 0, 1, 2
GATHERED = (
    (0, 0, 384, 3),
    (0, 384, 384, 3),
    (1, 0, 384, 3),
    (1, 384, 384, 2),
    (2, 0, 384, 3),
    (2, 384, 256, 2),
    (2, 640, 128, 1),
)
SUMMED = (
    (0, 0, 192, "FS12"),
    (0, 192, 192, "FSZd"),
    (1, 0, 192, "F12S"),
    (1, 192, 192, "F12S"),
    (2, 0, 192, "1F2S"),
    (2, 192, 192, "F12S"),
)
PLAN = {
    "x0": {
        0: (("az2", 0, 0), ("az1", 0, 0), ("az1", 1, 0), ("az2", 1, 0), ("zf", 0, 0), ("s", 0, 2), ("az1", 4, 0),),
    },
    "att": {
        0: (("s", 0, 1), ("az2", 2, 0), ("s", 1, 1), ("f", 0, 2), ("zf", 1, 0), ("s", 1, 2), ("s", 0, 3), ("az2", 4, 0), ("f", 0, 1), ("s", 4, 1), ("f", 1, 2), ("az1", 2, 0),),
        1: (("f", 1, 1), ("az1", 3, 0), ("s", 1, 3), ("az2", 3, 0), ("zf", 2, 0), ("f", 0, 3), ("c", 0, 1),),
        2: (("d", 0, 1), ("s", 2, 2), ("s", 2, 1), ("f", 4, 1), ("zf", 4, 0), ("c", 1, 1), ("c", 0, 2), ("az2", 5, 0), ("d", 1, 1), ("f", 1, 3),),
        3: (("s", 4, 2), ("c", 0, 3), ("f", 2, 2), ("d", 0, 2), ("c", 1, 2), ("f", 2, 1),),
        4: (("c", 1, 3), ("zf", 3, 0), ("s", 2, 3), ("s", 4, 3), ("d", 1, 2), ("f", 3, 1), ("az1", 5, 0),),
        5: (("f", 4, 2), ("c", 2, 1), ("d", 1, 3), ("az2", 6, 0), ("f", 3, 2), ("c", 4, 1), ("c", 2, 2), ("d", 0, 3),),
        6: (("zf", 5, 0), ("d", 4, 1), ("f", 2, 3), ("f", 3, 3),),
        7: (("az1", 6, 0), ("d", 2, 1), ("c", 3, 1), ("f", 5, 2),),
    },
    "n1": {
        0: (("d", 2, 2), ("f", 5, 1),),
    },
    "up": {
        0: (("c", 4, 2), ("d", 3, 1), ("f", 4, 3), ("c", 2, 3), ("c", 3, 2), ("zf", 6, 0),),
        1: (("f", 5, 3), ("c", 3, 3), ("c", 6, 2),),
        2: (("d", 3, 2),),
        3: (("c", 5, 1), ("d", 2, 3), ("d", 3, 3), ("c", 5, 2),),
    },
    "dn": {
        0: (("c", 6, 1), ("d", 6, 2), ("c", 4, 3),),
        1: (("d", 5, 1), ("c", 6, 3), ("c", 5, 3), ("d", 5, 2), ("d", 6, 1), ("d", 4, 2),),
        3: (("d", 4, 3), ("d", 5, 3), ("d", 6, 3),),
    },
    "l2": {
    },
    "da": {
        1: (("gFs", 5, 3),),
        2: (("gFs", 3, 3),),
        3: (("gFs", 3, 1),),
    },
    "gwo": {
        2: (("gFs", 2, 3),),
        3: (("g1s", 5, 3),),
    },
    "dn2": {
        0: (("g1s", 4, 3),),
        1: (("gFs", 5, 1), ("g1s", 4, 1),),
        3: (("gFs", 5, 0), ("gFs", 2, 1),),
    },
    "gwi": {
        1: (("gFr", 5, 3), ("gFs", 5, 2),),
        2: (("g1r", 4, 2), ("gFr", 3, 3), ("gFs", 4, 2), ("g1s", 3, 3),),
        3: (("gFs", 2, 2), ("gFs", 3, 2),),
    },
    "l1b": {
    },
    "ab": {
        0: (("gFr", 3, 1), ("gFs", 2, 0), ("gFr", 2, 3),),
        2: (("gFr", 4, 2), ("gFs", 3, 0), ("g2s", 4, 2),),
        4: (("gFs", 0, 3),),
        5: (("gFs", 1, 3), ("gFr", 5, 2), ("g1r", 5, 2), ("g2s", 5, 2),),
        6: (("gFs", 1, 1), ("gFr", 4, 0), ("gFr", 5, 1), ("g2r", 4, 0), ("gFs", 0, 1), ("g1s", 2, 3),),
        7: (("gSs", 4, 0), ("gFr", 0, 3), ("gFr", 1, 3), ("gSs", 0, 3),),
    },
    "gwa": {
        0: (("g1s", 3, 1), ("g1r", 4, 0), ("gFs", 4, 0),),
        2: (("gSs", 1, 3), ("gFr", 2, 1), ("g1s", 2, 1),),
        3: (("gFs", 0, 2), ("gFr", 3, 2), ("g1r", 3, 2), ("g2s", 3, 2), ("gFr", 1, 1), ("gFr", 2, 0), ("gSr", 4, 0), ("gFr", 2, 2), ("gFs", 1, 2),),
    },
    "fin": {
        0: (("gS2s", 4, 0),),
    },
    "end": {
        0: (("gFr", 3, 0), ("gFs", 0, 0), ("g1r", 2, 2), ("gFr", 0, 1), ("g1s", 5, 1), ("gFs", 1, 0), ("vs", 0, 0), ("gSs", 0, 1), ("g1r", 3, 0), ("gFr", 5, 0), ("gFr", 1, 2), ("g2s", 2, 2), ("gSs", 1, 2), ("gSr", 0, 3), ("gS2r", 4, 0), ("gFr", 0, 2), ("g2r", 3, 0), ("vr", 0, 0), ("gSs", 3, 0), ("gFr", 0, 0), ("g1r", 5, 0), ("gSr", 0, 1), ("gSs", 0, 0), ("gSs", 0, 2), ("g2r", 5, 0), ("vs", 1, 0), ("gSr", 1, 2), ("gFr", 1, 0), ("g1s", 0, 3), ("gSs", 5, 0), ("gSr", 3, 0), ("gSr", 1, 3), ("gZs", 1, 2), ("g1r", 2, 0), ("gSs", 1, 1), ("g2r", 2, 0), ("gSs", 2, 0), ("g1s", 0, 1), ("gS2s", 3, 0), ("gSs", 1, 0), ("gSr", 0, 2), ("vr", 1, 0), ("g1r", 0, 2), ("gSr", 5, 0), ("gSr", 0, 0), ("gS2s", 5, 0), ("vs", 2, 0), ("g2s", 0, 2), ("gSr", 1, 1), ("gSr", 2, 0), ("gZs", 1, 1), ("gS2s", 2, 0), ("gF2r", 4, 0), ("g1r", 0, 0), ("gS2r", 3, 0), ("gZs", 1, 3), ("gSr", 1, 0), ("gS2r", 5, 0), ("gZr", 1, 1), ("g2r", 0, 0), ("gZr", 1, 2), ("gS2s", 0, 0), ("gS2r", 2, 0), ("gF2r", 3, 0), ("gZr", 1, 3), ("gS2s", 1, 0), ("gF2r", 5, 0), ("vr", 2, 0), ("vs", 3, 0), ("gS2r", 0, 0), ("vr", 3, 0), ("vs", 4, 0), ("gd2Fr", 1, 0), ("gF2r", 2, 0), ("gC2r", 5, 0), ("gd2Sr", 1, 0), ("gF2r", 1, 0), ("gF2r", 0, 0), ("gC2r", 2, 0), ("gC2r", 4, 0), ("vr", 4, 0), ("gC2r", 3, 0), ("gC2r", 1, 0), ("gC2r", 0, 0),),
    },
}
V_OB, V_G1, V_S1, V_EB, V_G2, V_S2 = 8, 9, 10, 11, 12, 13


def dot(left, right, dims):
    return lax.dot_general(left, right, dims, preferred_element_type=F32)


def depth_at(p, stage):
    done = SUMMED[p][3].split(stage)[0]
    return ("F" in done) + ("S" in done)


def z_rows(p, slot):
    sizes = {}
    for q, (_, _, n, chain) in enumerate(SUMMED):
        for t in range(3):
            sizes[q, t] = n >> depth_at(q, "Z" if "Z" in chain else "112"[t])
    return sum(n for key, n in sizes.items() if key < (p, slot)), sizes[p, slot]


def layer_kernel(
    cfg,
    tok, cot, wq, wk, wv, wo, wi, wout, bq, bv, bi, bo, g1, s1, be, g2, s2, seg_in, live_in,
    out_ref, dx_ref, whole, vec_ref,
    wbuf, bias, xs, cots, qkv, ka, ks, prob, mask, acc, tmp, nh1, r1,
    nb, nhalf, af, asib, al, gp, g, sg, di, fg,
    gr, rf, rz, rs, rx, vrecv, vin, short,
    seg, live, *rest,
):
    n_dp, d, seq, rows = cfg["dp"], cfg["d"], cfg["seq"], cfg["rows"]
    tl = seq * rows
    ml = d // 4
    hs = ml // DH
    half, qtr, eig = d // 2, d // 4, d // 8
    scale = DH ** (-0.5)
    bits = n_dp.bit_length() - 1
    dp, z = lax.axis_index("dp"), lax.axis_index("mp")
    c = dp % 2
    df = 2 + 2 * c
    ds_ = 6 - df
    f, s = (dp // df) % 2, (dp // ds_) % 2
    p_x = dp + df * (1 - 2 * f) + ds_ * (1 - 2 * s)
    p_f, p_s, p_c = dp + df * (1 - 2 * f), dp + ds_ * (1 - 2 * s), dp + 1 - 2 * c
    z0, zh = z % 2, z // 2
    z1, z2, z3 = z + 1 - 2 * z0, z + 2 - 4 * zh, 3 - z
    h0 = pl.multiple_of(c * half, 128)
    ho = pl.multiple_of((1 - c) * half, 128)

    def sub(base, n, depth, other=False):
        off = base
        for level, bit in enumerate((c, f, s)[:depth]):
            n //= 2
            off = off + n * (1 - bit if other and level == depth - 1 else bit)
        return (pl.multiple_of(off, 16) if depth else off), n

    def cut(base, n, depth, other=False):
        off = base
        for level, bit in enumerate((f, s)[:depth]):
            n //= 2
            off = off + n * (1 - bit if other and level == depth - 1 else bit)
        return (pl.multiple_of(off, 16) if depth else off), n

    gathered = {}
    for a, (piece, base, n, cuts) in enumerate(GATHERED):
        for depth in (1, 2, 3):
            for other in (False, True):
                gathered[a, depth, other] = sub(base, n, depth, other)
    summed = {}
    for p, (piece, base, n, chain) in enumerate(SUMMED):
        for depth in (0, 1, 2):
            for other in (False, True):
                summed[p, depth, other] = cut(base, n, depth, other)

    finals = {}
    for p, (piece, base, n, chain) in enumerate(SUMMED):
        for depth in (0, 1, 2):
            for other in (False, True):
                off, m = summed[p, depth, other]
                finals[p, depth, other] = (pl.multiple_of(c * half + off, 16), m)
        finals[p, "core", True] = (pl.multiple_of((1 - c) * half + base, 16), n)
    shard = (z, z1, z2, z3)

    def shard_of(k):
        k0, kh = k % 2, k // 2
        return z0 + k0 - 2 * z0 * k0 + 2 * (zh + kh - 2 * zh * kh)

    def remote(src, dst, ssem, rsem, dev):
        return pltpu.make_async_remote_copy(
            src_ref=src, dst_ref=dst, send_sem=ssem, recv_sem=rsem, device_id=dev, device_id_type=MESH
        )

    pending = []

    def send(make, group="early"):
        remote(*make()).start()
        pending.append((group, make))

    def flush(group):
        for item in [item for item in pending if item[0] == group]:
            remote(*item[1]()).wait_send()
            pending.remove(item)

    small = rest[:9]
    loc_sem, ag_s, ag_r, gr_s, gr_r, x_s, x_r, b_s, b_r, v_s, v_r, e_s, e_r = rest[9:]
    barrier = pltpu.get_barrier_semaphore()
    extra = [dp + (1 << b) * (1 - 2 * ((dp // (1 << b)) % 2)) for b in range(3, bits)]
    greet = [(p_c, z), (p_f, z), (p_s, z), (p_x, z), (dp, z1), (dp, z2), (dp, z3)] + [(e, z) for e in extra]
    for dev in greet:
        pl.semaphore_signal(barrier, inc=1, device_id=dev, device_id_type=MESH)
    att_loads = [
        pltpu.make_async_copy(ref, wbuf.at[ATT, z, pl.ds(j * ml, ml)], loc_sem.at[j])
        for j, ref in enumerate((wq, wk, wv, wo))
    ]
    vec_loads = [
        pltpu.make_async_copy(ref, dst, loc_sem.at[4 + j])
        for j, (ref, dst) in enumerate(zip((bq, bv, bi, bo, g1, s1, be, g2, s2), small))
    ]
    seg_loads = [
        pltpu.make_async_copy(seg_in, seg, loc_sem.at[13]),
        pltpu.make_async_copy(live_in, live, loc_sem.at[14]),
        pltpu.make_async_copy(tok, xs.at[pl.ds(0, rows)], loc_sem.at[15]),
    ]
    late_loads = [
        pltpu.make_async_copy(wi, wbuf.at[INN, z], loc_sem.at[16]),
        pltpu.make_async_copy(wout, wbuf.at[OUT, z], loc_sem.at[17]),
        pltpu.make_async_copy(cot, cots, loc_sem.at[18]),
    ]
    for cp in att_loads + vec_loads + seg_loads + late_loads:
        cp.start()
    for cp in att_loads:
        cp.wait()
    pl.semaphore_wait(barrier, len(greet))

    def own(piece, off, n):
        if piece == ATT:
            return wbuf.at[ATT, z, pl.ds(off, n)]
        return (wi, wout)[piece - 1].at[pl.ds(off, n)]

    def reg(piece, k, off, n):
        return wbuf.at[piece, shard[k], pl.ds(off, n)]

    def ag_send(a, slot, k, rows_of, dev, mine=False):
        piece = GATHERED[a][0]

        def make():
            region = reg(piece, k, *rows_of)
            return own(piece, *rows_of) if mine else region, region, ag_s.at[a, slot], ag_r.at[a, slot], dev

        send(make)

    def ag_wait(a, slot, k, rows_of):
        region = reg(GATHERED[a][0], k, *rows_of)
        remote(region, region, ag_s.at[a, slot], ag_r.at[a, slot], (dp, z1)).wait_recv()

    def first(a):
        return gathered[a, GATHERED[a][3], False]

    def a_z1(a, _):
        ag_send(a, 1, 0, first(a), (dp, z1), True)

    def a_z2(a, _):
        ag_send(a, 0, 0, first(a), (dp, z2), True)

    def a_zf(a, _):
        ag_wait(a, 0, 2, first(a))
        ag_send(a, 2, 2, first(a), (dp, z1))

    def a_arrive(a, k):
        if k != 2:
            ag_wait(a, {1: 1, 3: 2}[k], k, first(a))

    def a_s(a, k):
        a_arrive(a, k)
        ag_send(a, 2 + k, k, gathered[a, 3, False], (p_s, z))

    def a_f(a, k):
        if GATHERED[a][3] < 3:
            a_arrive(a, k)
        else:
            ag_wait(a, 2 + k, k, gathered[a, 3, True])
        ag_send(a, 5 + k, k, gathered[a, 2, False], (p_f, z))

    def a_c(a, k):
        if GATHERED[a][3] < 2:
            a_arrive(a, k)
        else:
            ag_wait(a, 5 + k, k, gathered[a, 2, True])
        ag_send(a, 8 + k, k, gathered[a, 1, False], (p_c, z))

    def a_d(a, k):
        ag_wait(a, 8 + k, k, gathered[a, 1, True])

    X_TOK, X_N, X_FG, X_A, X_DI, X_KA, X_G = 0, 1, 2, 4, 8, 12, 16

    def core_send(slot, pair):
        send(lambda: (*pair(), x_s.at[slot], x_r.at[slot], (p_c, z)))

    def core_wait(slot, dst):
        remote(dst, dst, x_s.at[slot], x_r.at[slot], (p_c, z)).wait_recv()

    def g_sem(p, slot):
        return gr_s.at[p, slot], gr_r.at[p, slot]

    def g_send(p, slot, pair, dev):
        send(lambda: (*pair(), *g_sem(p, slot), dev), p if slot < 11 else "late")

    def g_wait(p, slot, dst):
        remote(dst, dst, *g_sem(p, slot), (dp, z1)).wait_recv()

    def add_into(dst, src, n):
        m = 48 if n % 48 == 0 else (32 if n % 32 == 0 else 16)

        def blk(j, carry):
            sl = pl.ds(pl.multiple_of(j * m, 16), m)
            dst[sl, :] = (dst[sl, :].astype(F32) + src[sl, :].astype(F32)).astype(BF)
            return carry

        lax.fori_loop(0, n // m, blk, 0)

    def chunk(p, k, depth, other=False):
        off, n = summed[p, depth, other]
        return gr.at[SUMMED[p][0], k, pl.ds(off, n)]

    def final(p, depth, other=False):
        off, n = finals[p, depth, other]
        return whole.at[SUMMED[p][0], pl.ds(off, n)]

    def final_across(p, side):
        _, base, n, _ = SUMMED[p]
        off = pl.multiple_of(c * half + base + (1 - f) * (n // 2) + side * (n // 4), 16)
        return whole.at[SUMMED[p][0], pl.ds(off, n // 4)]

    def f_slot(p, k):
        piece, base, n, _ = SUMMED[p]
        return rf.at[piece, k, pl.ds(base // 2, n // 2)]

    def s_slot(p, k):
        piece, base, n, _ = SUMMED[p]
        return rs.at[piece, k, pl.ds(base // 4, n // 4)]

    def z_slot(p, slot):
        return rz.at[pl.ds(*z_rows(p, slot))]

    def g_fs(p, k):
        g_send(p, k, lambda: (chunk(p, k, 1, True), f_slot(p, k)), (p_f, z))

    def g_fr(p, k):
        g_wait(p, k, f_slot(p, k))
        add_into(chunk(p, k, 1), f_slot(p, k), SUMMED[p][2] // 2)

    def g_ss(p, k):
        g_send(p, 4 + k, lambda: (chunk(p, k, 2, True), s_slot(p, k)), (p_s, z))

    def g_sr(p, k):
        g_wait(p, 4 + k, s_slot(p, k))
        add_into(chunk(p, k, 2), s_slot(p, k), SUMMED[p][2] // 4)

    def g_1s(p, k):
        slot = 0 if k == 3 else 1
        g_send(p, 8 + slot, lambda: (chunk(p, k, depth_at(p, "1")), z_slot(p, slot)), (dp, z1))

    def g_1r(p, k):
        slot = 0 if k == 2 else 1
        g_wait(p, 8 + slot, z_slot(p, slot))
        depth = depth_at(p, "1")
        add_into(chunk(p, k, depth), z_slot(p, slot), SUMMED[p][2] >> depth)

    def g_2s(p, k):
        g_send(p, 10, lambda: (chunk(p, 2, depth_at(p, "2")), z_slot(p, 2)), (dp, z2))

    def g_2r(p, k):
        g_wait(p, 10, z_slot(p, 2))
        depth = depth_at(p, "2")
        add_into(chunk(p, 0, depth), z_slot(p, 2), SUMMED[p][2] >> depth)

    def g_zs(p, k):
        depth = depth_at(p, "Z")
        g_send(p, 7 + k, lambda: (chunk(p, k, depth), z_slot(p, k - 1)), (dp, shard[k]))

    def g_zr(p, k):
        depth = depth_at(p, "Z")
        g_wait(p, 7 + k, z_slot(p, k - 1))
        add_into(chunk(p, 0, depth), z_slot(p, k - 1), SUMMED[p][2] >> depth)

    def g_s2s(p, _):
        piece, base, n, _ = SUMMED[p]
        for j, partner in enumerate(extra):
            slot = rx.at[piece, j, pl.ds(base // 4, n // 4)]
            cp = remote(chunk(p, 0, 2), slot, e_s.at[p, j], e_r.at[p, j], (partner, z))
            cp.start()
            cp.wait()
            add_into(chunk(p, 0, 2), slot, n // 4)
        mine, target = chunk(p, 0, 2), final(p, 2)
        for lo in range(0, n // 4, 16):
            target[pl.ds(lo, 16), :] = mine[pl.ds(lo, 16), :]
        g_send(p, 11, lambda: (final(p, 2),) * 2, (p_s, z))
        if SUMMED[p][3].endswith("d"):
            g_send(p, 12, lambda: (final(p, 2),) * 2, (p_f, z))
            g_send(p, 14, lambda: (final(p, 2),) * 2, (p_x, z))

    def g_s2r(p, _):
        g_wait(p, 11, final(p, 2, True))
        g_send(p, 12, lambda: (final(p, 1),) * 2, (p_f, z))

    def g_d2sr(p, _):
        g_wait(p, 11, final(p, 2, True))

    def g_d2fr(p, _):
        g_wait(p, 12, final_across(p, s))

    def g_f2r(p, _):
        if SUMMED[p][3].endswith("d"):
            g_wait(p, 14, final_across(p, 1 - s))
        else:
            g_wait(p, 12, final(p, 1, True))
        g_send(p, 13, lambda: (final(p, 0),) * 2, (p_c, z))
        flush(p)

    def g_c2r(p, _):
        g_wait(p, 13, final(p, "core", True))

    partners = [(p_c, z), (p_f, z), (p_s, z), (dp, z1), (dp, z2)] + [(e, z) for e in extra]

    def v_half(mine):
        return vec_ref.at[pl.ds(pl.multiple_of(8 * (c if mine else 1 - c), 8), 8)]

    def v_copy(j):
        return remote(v_half(j > 0), vrecv.at[j], v_s.at[j], v_r.at[j], partners[j])

    def v_send(j, _):
        v_copy(j).start()

    def v_back():
        return remote(v_half(True), v_half(True), v_s.at[len(partners)], v_r.at[len(partners)], (p_c, z))

    def v_recv(j, _):
        v_copy(j).wait()
        half_ref = v_half(True)
        half_ref[...] = half_ref[...] + vrecv[j]
        if j == len(partners) - 1:
            v_back().start()

    events = {
        "az1": a_z1, "az2": a_z2, "zf": a_zf, "s": a_s, "f": a_f, "c": a_c, "d": a_d,
        "gFs": g_fs, "gFr": g_fr, "gSs": g_ss, "gSr": g_sr, "g1s": g_1s, "g1r": g_1r, "g2s": g_2s, "g2r": g_2r,
        "gZs": g_zs, "gZr": g_zr, "gd2Fr": g_d2fr, "gd2Sr": g_d2sr, "gS2s": g_s2s, "gS2r": g_s2r, "gF2r": g_f2r, "gC2r": g_c2r, "vs": v_send, "vr": v_recv,
    }

    def do(listed):
        for kind, piece, k in listed:
            events[kind](piece, k)

    def at(place, index):
        for n, listed in PLAN.get(place, {}).items():
            pl.when(index == n)(functools.partial(do, listed))

    def once(place):
        do(PLAN.get(place, {}).get(0, ()))

    once("x0")
    for cp in vec_loads:
        cp.wait()
    vin[...] = jnp.zeros_like(vin)
    vin[pl.ds(0, 1), pl.ds(0, ml)] = small[0][...].astype(F32).reshape(1, ml)
    vin[pl.ds(0, 1), pl.ds(2 * ml, ml)] = small[1][...].astype(F32).reshape(1, ml)
    for j, ref in enumerate(small[2:]):
        vin[pl.ds(j + 1, 1), :] = ref[...].astype(F32).reshape(1, d)
    bias[z] = vin[...]
    third = d // 3
    short[z] = jnp.zeros((8, third), F32)
    short[z, pl.ds(0, 1), pl.ds(0, ml)] = vin[pl.ds(0, 1), pl.ds(0, ml)]
    short[z, pl.ds(1, 1), pl.ds(0, ml)] = vin[pl.ds(0, 1), pl.ds(2 * ml, ml)]
    for j in range(3):
        short[z, pl.ds(2 + j, 1), :] = vin[pl.ds(1, 1), pl.ds(j * third, third)]
    for j, zz in enumerate((z1, z2, z3)):
        send(lambda j=j, zz=zz: (short.at[z], short.at[z], b_s.at[j], b_r.at[j], (dp, zz)))
    core_send(X_TOK, lambda: (tok, xs.at[pl.ds(rows, rows)]))
    for cp in seg_loads:
        cp.wait()

    for r in range(rows):
        seg_row = seg[pl.ds(z * rows + r, 1), :]
        live_row = live[pl.ds(z * rows + r, 1), :]
        code = jnp.where(live_row == 1, seg_row, -1)
        ids = lax.broadcasted_iota(jnp.int32, (8, seq), 0)
        key_hot = (jnp.broadcast_to(code, (8, seq)) == ids).astype(F32).astype(BF)
        query_hot = (jnp.broadcast_to(seg_row, (8, seq)) == ids).astype(F32).astype(BF)
        mask[r] = jnp.where(dot(key_hot, query_hot, TN) > 0.5, 0.0, NEG_FILL)
    acc[...] = jnp.zeros_like(acc)
    first_row = (lax.broadcasted_iota(jnp.int32, (8, seq), 0) == 0).astype(F32).astype(BF)

    def attend(i, carry):
        t = shard_of(i)

        def row(r, inner_carry):
            at("att", i * rows + r)

            @pl.when((i == 1) & (r == 0))
            def _():
                for j, zz in enumerate((z1, z2, z3)):
                    remote(short.at[zz], short.at[zz], b_s.at[j], b_r.at[j], (dp, zz)).wait_recv()
                    bias[zz] = jnp.zeros((8, d), F32)
                    bias[zz, pl.ds(0, 1), pl.ds(0, ml)] = short[zz, pl.ds(0, 1), pl.ds(0, ml)]
                    bias[zz, pl.ds(0, 1), pl.ds(2 * ml, ml)] = short[zz, pl.ds(1, 1), pl.ds(0, ml)]
                    for n in range(3):
                        bias[zz, pl.ds(1, 1), pl.ds(n * third, third)] = short[zz, pl.ds(2 + n, 1), :]

            x_row = xs[r]
            bias_rows = bias[t].astype(BF)[:, : 3 * ml]
            qkv[t, r] = (
                dot(wbuf[ATT, t, pl.ds(0, 3 * ml), :], x_row, NT) + dot(bias_rows, first_row, TN)
            ).astype(BF)
            for h in range(hs):
                query = qkv[t, r, pl.ds(h * DH, DH), :]
                key = qkv[t, r, pl.ds(ml + h * DH, DH), :]
                value = qkv[t, r, pl.ds(2 * ml + h * DH, DH), :]
                scores = dot(key, query, TN) * scale + mask[r]
                top = jnp.max(scores, 0, keepdims=True)
                exponent = jnp.exp(scores - top)
                total = jnp.sum(exponent, 0, keepdims=True)
                prob_t = (exponent * (1.0 / total)).astype(BF)
                prob[t, r, h] = prob_t
                ka[t, r, pl.ds(3 * ml + h * DH, DH), :] = dot(value, prob_t, NN).astype(BF)
            part_sum = dot(ka[t, r, pl.ds(3 * ml, ml), :], wbuf[ATT, t, pl.ds(3 * ml, ml), :], TN)
            sl = pl.ds(pl.multiple_of(r * seq, 16), seq)
            acc[sl, :] = acc[sl, :] + part_sum
            return inner_carry

        lax.fori_loop(0, rows, row, 0)
        return carry

    lax.fori_loop(0, 4, attend, 0)

    rb = seq

    def norm_rows(summed):
        mean = jnp.mean(summed, -1, keepdims=True)
        centred = summed - mean
        variance = jnp.mean(centred * centred, -1, keepdims=True)
        rs_ = lax.rsqrt(variance + EPSILON)
        return centred * rs_, rs_

    def norm_back(grad, hat, rs_):
        return rs_ * (grad - jnp.mean(grad, -1, keepdims=True) - hat * jnp.mean(grad * hat, -1, keepdims=True))

    def vrow(j):
        return vin[pl.ds(j, 1), :]

    once("n1")

    def norm1(j, carry):
        sl = pl.ds(pl.multiple_of(j * rb, 16), rb)
        per = seq // rb
        x_blk = xs[j // per, pl.ds(pl.multiple_of((j % per) * rb, 16), rb), :].astype(F32)
        hat, rs_ = norm_rows(acc[sl, :] + vrow(2) + x_blk)
        nh1[sl, :] = hat
        r1[sl, :] = jnp.broadcast_to(rs_, (rb, 128))
        nb[sl, :] = (hat * vrow(3) + vrow(4)).astype(BF)
        acc[sl, :] = jnp.zeros((rb, d), F32)
        return carry

    lax.fori_loop(0, tl // rb, norm1, 0)
    core_send(X_N, lambda: (nb.at[:, pl.ds(ho, half)], nhalf.at[pl.ds(tl, tl)]))
    nhalf[pl.ds(0, tl), :] = nb[:, pl.ds(h0, half)]

    late_loads[0].wait()

    def up(i, carry):
        at("up", i)
        t = shard_of(i)
        tmp[...] = dot(nb[...], wbuf[INN, t], NN)
        b_row = bias[t, pl.ds(1, 1), :]

        def act(j, carry):
            sl = pl.ds(pl.multiple_of(j * rb, 16), rb)
            u = tmp[sl, :] + b_row
            cdf = 0.5 * (1.0 + lax.erf(u * ROOT_HALF))
            af[t, sl, :] = (u * cdf).astype(BF)
            gp[t, sl, :] = (cdf + u * (PDF_SCALE * jnp.exp(-0.5 * u * u))).astype(BF)
            return carry

        lax.fori_loop(0, tl // rb, act, 0)
        remote(af.at[t, :, pl.ds(ho, half)], asib.at[t], x_s.at[X_A + i], x_r.at[X_A + i], (p_c, z)).start()
        return carry

    lax.fori_loop(0, 4, up, 0)
    late_loads[1].wait()
    late_loads[2].wait()

    def down(i, carry):
        at("dn", i)
        t = shard_of(i)
        acc[...] += dot(af[t], wbuf[OUT, t], NN)
        return carry

    lax.fori_loop(0, 4, down, 0)

    once("l2")
    vec_ref[...] = jnp.zeros_like(vec_ref)

    def add_vec(row, value):
        vec_ref[pl.ds(row, 1), :] = vec_ref[pl.ds(row, 1), :] + value

    def norm2(j, carry):
        sl = pl.ds(pl.multiple_of(j * rb, 16), rb)
        normed = nh1[sl, :] * vrow(3) + vrow(4)
        hat, rs_ = norm_rows(acc[sl, :] + vrow(5) + normed)
        c_blk = cots[sl, :].astype(F32)
        out_ref[sl, :] = (hat * vrow(6) + vrow(7)).astype(BF)
        back = norm_back(c_blk * vrow(6), hat, rs_)
        sg[sl, :] = back
        g[sl, :] = back.astype(BF)
        acc[sl, :] = jnp.zeros((rb, d), F32)
        add_vec(V_G2, jnp.sum(c_blk * hat, 0, keepdims=True))
        add_vec(V_S2, jnp.sum(c_blk, 0, keepdims=True))
        add_vec(V_EB, jnp.sum(back, 0, keepdims=True))
        return carry

    def g_copy(j):
        src = g.at[pl.ds(pl.multiple_of(j * rb, 16), rb)]
        dst = g.at[pl.ds(pl.multiple_of(tl + j * rb, 16), rb)]
        return remote(src, dst, x_s.at[X_G + j], x_r.at[X_G + j], (p_c, z))

    for j in range(tl // rb):
        norm2(j, 0)
        g_copy(j).start()
    def order(i):
        return 3 - 2 * (i % 2) - i // 2

    def ffn_back(i, carry):
        @pl.when(i < 4)
        def _():
            at("da", i)
            k = order(i)
            t = shard_of(k)
            tmp[...] = dot(g[pl.ds(0, tl), :], wbuf[OUT, t], NT)

            def act(j, total):
                sl = pl.ds(pl.multiple_of(j * rb, 16), rb)
                blk = (tmp[sl, :] * gp[t, sl, :].astype(F32)).astype(BF)
                di[t, sl, :] = blk
                return total + jnp.sum(blk.astype(F32), 0, keepdims=True)

            vec_ref[pl.ds(4 + t, 1), :] = lax.fori_loop(0, tl // rb, act, jnp.zeros((1, d), F32))
            remote(
                di.at[t, pl.ds(0, tl)], di.at[t, pl.ds(tl, tl)], x_s.at[X_DI + k], x_r.at[X_DI + k], (p_c, z)
            ).start()
            at("gwo", i)

            @pl.when(i == 0)
            def _():
                for j in range(tl // rb):
                    g_copy(j).wait_recv()
                core_wait(X_N, nhalf.at[pl.ds(tl, tl)])

            core_wait(X_A + k, asib.at[t])
            al[pl.ds(0, tl), :] = af[t, :, pl.ds(h0, half)]
            al[pl.ds(tl, tl), :] = asib[t]
            gr[OUT, k] = dot(al[...], g[...], TN).astype(BF)
            at("dn2", i)
            acc[...] += dot(di[t, pl.ds(0, tl), :], wbuf[INN, t], NT)

        @pl.when(i > 0)
        def _():
            at("gwi", i - 1)
            k = order(i - 1)
            t = shard_of(k)
            core_wait(X_DI + k, di.at[t, pl.ds(tl, tl)])
            gr[INN, k] = dot(nhalf[...], di[t], TN).astype(BF)

        return carry

    lax.fori_loop(0, 5, ffn_back, 0)
    once("l1b")

    def norm1_back(j, carry):
        sl = pl.ds(pl.multiple_of(j * rb, 16), rb)
        per = seq // rb
        hat = nh1[sl, :]
        total = acc[sl, :] + sg[sl, :]
        back = norm_back(total * vrow(3), hat, r1[sl, 0:1])
        sg[sl, :] = back
        fg[j // per, pl.ds(pl.multiple_of((j % per) * rb, 16), rb), :] = back.astype(BF)
        acc[sl, :] = jnp.zeros((rb, d), F32)
        add_vec(V_G1, jnp.sum(total * hat, 0, keepdims=True))
        add_vec(V_S1, jnp.sum(total, 0, keepdims=True))
        add_vec(V_OB, jnp.sum(back, 0, keepdims=True))
        return carry

    lax.fori_loop(0, tl // rb, norm1_back, 0)
    core_send(X_FG, lambda: (fg.at[pl.ds(0, rows)], fg.at[pl.ds(rows, rows)]))
    ones = jnp.ones((8, seq), BF)

    def att_back(i, carry):
        @pl.when(i < 4)
        def _():
            k = order(i)
            t = shard_of(k)

            def row(r, inner_carry):
                at("ab", i * rows + r)
                dctx = dot(wbuf[ATT, t, pl.ds(3 * ml, ml), :], fg[r], NT).astype(BF)
                for h in range(hs):
                    query = qkv[t, r, pl.ds(h * DH, DH), :]
                    key = qkv[t, r, pl.ds(ml + h * DH, DH), :]
                    value = qkv[t, r, pl.ds(2 * ml + h * DH, DH), :]
                    prob_t = prob[t, r, h]
                    grad = dctx[h * DH : (h + 1) * DH]
                    ka[t, r, pl.ds(2 * ml + h * DH, DH), :] = dot(grad, prob_t, NT).astype(BF)
                    prob_grad = dot(value, grad, TN)
                    wide_prob = prob_t.astype(F32)
                    inner = jnp.sum(wide_prob * prob_grad, 0, keepdims=True)
                    score_grad = (wide_prob * (prob_grad - inner)).astype(BF)
                    ka[t, r, pl.ds(h * DH, DH), :] = (dot(key, score_grad, NN) * scale).astype(BF)
                    ka[t, r, pl.ds(ml + h * DH, DH), :] = (dot(query, score_grad, NT) * scale).astype(BF)
                grads = ka[t, r, pl.ds(0, 3 * ml), :]
                vec_ref[pl.ds(t, 1), pl.ds(0, 3 * ml)] += dot(ones, grads, NT)[0:1]
                sl = pl.ds(pl.multiple_of(r * seq, 16), seq)
                acc[sl, :] = acc[sl, :] + dot(grads, wbuf[ATT, t, pl.ds(0, 3 * ml), :], TN)
                return inner_carry

            lax.fori_loop(0, rows, row, 0)
            remote(
                ka.at[t, :, pl.ds(ho, half)], ks.at[t], x_s.at[X_KA + k], x_r.at[X_KA + k], (p_c, z)
            ).start()

        @pl.when(i == 0)
        def _():
            core_wait(X_TOK, xs.at[pl.ds(rows, rows)])
            core_wait(X_FG, fg.at[pl.ds(rows, rows)])

        @pl.when(i > 0)
        def _():
            at("gwa", i - 1)
            k = order(i - 1)
            t = shard_of(k)
            core_wait(X_KA + k, ks.at[t])
            for j in range(2):
                rowsel = pl.ds(pl.multiple_of(h0 + j * ml, 16), ml)
                use = c * j
                total = jnp.zeros((ml, d), F32)
                for r in range(rows):
                    right_own = xs[r] if j == 0 else jnp.where(use == 1, fg[r], xs[r])
                    right_sib = xs[rows + r] if j == 0 else jnp.where(use == 1, fg[rows + r], xs[rows + r])
                    total += dot(ka[t, r, rowsel, :], right_own, NN)
                    total += dot(ks[t, r, pl.ds(j * ml, ml), :], right_sib, NN)
                gr[ATT, k, pl.ds(j * ml, ml), :] = total.astype(BF)

        return carry

    lax.fori_loop(0, 5, att_back, 0)
    once("fin")

    def finish(j, carry):
        sl = pl.ds(pl.multiple_of(j * rb, 16), rb)
        dx_ref[sl, :] = (sg[sl, :] + acc[sl, :]).astype(BF)
        return carry

    lax.fori_loop(0, tl // rb, finish, 0)


    flush("early")

    def sent(k, carry):
        t = shard_of(k)
        remote(af.at[t, :, pl.ds(ho, half)], asib.at[t], x_s.at[X_A + k], x_r.at[X_A + k], (p_c, z)).wait_send()
        remote(
            di.at[t, pl.ds(0, tl)], di.at[t, pl.ds(tl, tl)], x_s.at[X_DI + k], x_r.at[X_DI + k], (p_c, z)
        ).wait_send()
        remote(ka.at[t, :, pl.ds(ho, half)], ks.at[t], x_s.at[X_KA + k], x_r.at[X_KA + k], (p_c, z)).wait_send()
        return carry

    lax.fori_loop(0, 4, sent, 0)
    for j in range(tl // rb):
        g_copy(j).wait_send()

    once("end")
    for j in range(5, len(partners)):
        v_send(j, 0)
        v_recv(j, 0)
    other_half = v_half(False)
    remote(other_half, other_half, v_s.at[len(partners)], v_r.at[len(partners)], (p_c, z)).wait_recv()
    v_back().wait_send()

    flush("late")
    assert not pending


def spread_kernel(
    ml, grads, vec, out_in, dx_in,
    out_ref, dx_ref, gq, gk, gv, go, gi, ge, bq, bv, bo, g1, s1, bi, be, g2, s2,
    wide_v, *rest,
):
    z = lax.axis_index("mp")
    n = 2 * ml
    outs = []
    small, sem = rest[:9], rest[9]

    def put(src, dst):
        cp = pltpu.make_async_copy(src, dst, sem.at[len(outs)])
        cp.start()
        outs.append(cp)

    put(out_in, out_ref)
    put(dx_in, dx_ref)
    picks = [(z, 0, ml, bq), (z, 2 * ml, ml, bv), (4 + z, 0, 4 * ml, bi)]
    picks += [
        (row, 0, 4 * ml, ref)
        for row, ref in ((V_OB, bo), (V_G1, g1), (V_S1, s1), (V_EB, be), (V_G2, g2), (V_S2, s2))
    ]
    steps = [(piece, lo, [(ref, lo, n)]) for piece, ref in ((1, gi), (2, ge)) for lo in (0, n)]
    steps += [(0, 0, [(gq, 0, ml), (gk, 0, ml)]), (0, n, [(gv, 0, ml), (go, 0, ml)])]
    for piece, lo, refs in steps:
        wide_v[piece, pl.ds(lo, n), :] = grads[piece, pl.ds(lo, n), :].astype(F32)
        at = lo
        for ref, row, m in refs:
            put(wide_v.at[piece, pl.ds(at, m)], ref.at[pl.ds(row, m)])
            at += m
    for (row, lo, m, ref), buf in zip(picks, small):
        buf[...] = vec[pl.ds(row, 1), pl.ds(lo, m)].reshape(m)
        put(buf, ref)
    for cp in outs:
        cp.wait()


def per_device(
    n_dp,
    tokens, segment_ids, live_mask, query_weight, key_weight, value_weight, query_bias, value_bias,
    output_weight, output_bias, first_gain, first_shift, inner_weight, inner_bias, outer_weight,
    outer_bias, second_gain, second_shift, cotangent,
):
    tl, d = tokens.shape
    seq_rows, seq = segment_ids.shape
    rows = tl // seq
    ml = query_weight.shape[1]
    ff = inner_weight.shape[1]
    half, qtr, eig = d // 2, d // 4, d // 8
    bits = n_dp.bit_length() - 1
    n_extra = max(bits - 3, 1)
    n_vec = bits + 3
    cfg = {"dp": n_dp, "d": d, "seq": seq, "rows": rows}
    vmem = pl.BlockSpec(memory_space=pltpu.VMEM)
    hbm = pl.BlockSpec(memory_space=pl.ANY)
    scratch = [
        pltpu.VMEM((3, 4, d, d), BF),
        pltpu.VMEM((4, 8, d), F32),
        pltpu.VMEM((2 * rows, seq, d), BF),
        pltpu.VMEM((tl, d), BF),
        pltpu.VMEM((4, rows, 3 * ml, seq), BF),
        pltpu.VMEM((4, rows, d, seq), BF),
        pltpu.VMEM((4, rows, half, seq), BF),
        pltpu.VMEM((4, rows, ml // DH, seq, seq), BF),
        pltpu.VMEM((rows, seq, seq), F32),
        pltpu.VMEM((tl, d), F32),
        pltpu.VMEM((tl, d), F32),
        pltpu.VMEM((tl, d), F32),
        pltpu.VMEM((tl, 128), F32),
        pltpu.VMEM((tl, d), BF),
        pltpu.VMEM((2 * tl, half), BF),
        pltpu.VMEM((4, tl, d), BF),
        pltpu.VMEM((4, tl, half), BF),
        pltpu.VMEM((2 * tl, half), BF),
        pltpu.VMEM((4, tl, d), BF),
        pltpu.VMEM((2 * tl, d), BF),
        pltpu.VMEM((tl, d), F32),
        pltpu.VMEM((4, 2 * tl, d), BF),
        pltpu.VMEM((2 * rows, seq, d), BF),
        pltpu.VMEM((3, 4, half, d), BF),
        pltpu.VMEM((3, 4, qtr, d), BF),
        pltpu.VMEM((sum(z_rows(len(SUMMED) - 1, 2)), d), BF),
        pltpu.VMEM((3, 4, eig, d), BF),
        pltpu.VMEM((3, n_extra, eig, d), BF) if bits > 3 else pltpu.VMEM((1, 1, 16, 128), BF),
        pltpu.VMEM((n_vec - 1, 8, d), F32),
        pltpu.VMEM((8, d), F32),
        pltpu.VMEM((4, 8, d // 3), F32),
        pltpu.VMEM((seq_rows, seq), jnp.int32),
        pltpu.VMEM((seq_rows, seq), jnp.int32),
    ]
    scratch += [pltpu.VMEM((n,), BF) for n in (ml, ml, ff, d, d, d, d, d, d)]
    scratch += [
        pltpu.SemaphoreType.DMA(shape)
        for shape in [(24,)] + [(len(GATHERED), 12)] * 2 + [(len(SUMMED), 15)] * 2 + [(16 + rows,)] * 2 + [(3,)] * 2
        + [(n_vec,)] * 2 + [(len(SUMMED), n_extra)] * 2
    ]
    out, dx, grads, vec = pl.pallas_call(
        functools.partial(layer_kernel, cfg),
        out_shape=(
            pltpu.VMEM((tl, d), BF),
            pltpu.VMEM((tl, d), BF),
            pltpu.VMEM((3, d, d), BF),
            pltpu.VMEM((16, d), F32),
        ),
        in_specs=[hbm] * 19,
        out_specs=(vmem,) * 4,
        scratch_shapes=scratch,
        compiler_params=pltpu.CompilerParams(
            collective_id=0, has_side_effects=True, vmem_limit_bytes=LIMIT
        ),
        name="layer",
    )(
        tokens.reshape(rows, seq, d), cotangent, query_weight.T, key_weight.T, value_weight.T, output_weight,
        inner_weight, outer_weight, query_bias, value_bias, inner_bias, output_bias, first_gain, first_shift,
        outer_bias, second_gain, second_shift, segment_ids, live_mask,
    )
    out, dx, gq, gk, gv, go, gi, ge, bq, bv, bo, g1, s1, bi, be, g2, s2 = pl.pallas_call(
        functools.partial(spread_kernel, ml),
        out_shape=tuple(
            jax.ShapeDtypeStruct(shape, dtype)
            for shape, dtype in [((tl, d), BF)] * 2
            + [((ml, d), F32)] * 4
            + [((d, ff), F32), ((ff, d), F32)]
            + [((ml,), F32)] * 2
            + [((d,), F32)] * 7
        ),
        in_specs=[vmem] * 4,
        out_specs=(hbm,) * 17,
        scratch_shapes=[pltpu.VMEM((3, d, d), F32)]
        + [pltpu.VMEM((n,), F32) for n in (ml, ml, ff, d, d, d, d, d, d)]
        + [pltpu.SemaphoreType.DMA((19,))],
        compiler_params=pltpu.CompilerParams(vmem_limit_bytes=24 * 1024 * 1024),
        name="spread",
    )(*(pltpu.with_memory_space_constraint(x, pltpu.VMEM) for x in (grads, vec, out, dx)))
    return out, dx, gq.T, gk.T, gv.T, bq, bv, go, bo, g1, s1, gi, bi, ge, be, g2, s2


def solution(mesh):
    tok, shared = P(("dp", "mp"), None), P()
    cols, rows, vec = P(None, "mp"), P("mp", None), P("mp")
    in_specs = (
        tok, P("dp", None), P("dp", None), cols, cols, cols, vec, vec, rows, shared, shared, shared,
        cols, vec, rows, shared, shared, shared, tok,
    )
    out_specs = (
        tok, tok, cols, cols, cols, vec, vec, rows, shared, shared, shared, cols, vec, rows,
        shared, shared, shared,
    )
    return jax.shard_map(
        functools.partial(per_device, mesh.shape["dp"]),
        mesh=mesh,
        in_specs=in_specs,
        out_specs=out_specs,
        check_vma=False,
    )
```

```python
import functools

import jax
import jax.numpy as jnp
from jax import lax
from jax.experimental import pallas as pl
from jax.experimental.pallas import tpu as pltpu
from jax.sharding import PartitionSpec as P

DH = 64
EPSILON = 1e-06
NEG_FILL = -1000000000.0
ROOT_HALF = 0.7071067811865476
PDF_SCALE = 0.3989422804014327
BF = jnp.bfloat16
F32 = jnp.float32
MESH = pl.DeviceIdType.MESH
LIMIT = 59 * 1024 * 1024

NN = (((1,), (0,)), ((), ()))
NT = (((1,), (1,)), ((), ()))
TN = (((0,), (0,)), ((), ()))

ATT, INN, OUT = 0, 1, 2
GATHERED = (
    (0, 0, 384, 3),
    (0, 384, 384, 3),
    (1, 0, 384, 3),
    (1, 384, 384, 2),
    (2, 0, 384, 3),
    (2, 384, 256, 2),
    (2, 640, 128, 1),
)
SUMMED = (
    (0, 0, 192, "FS12"),
    (0, 192, 192, "FS12"),
    (1, 0, 192, "F12S"),
    (1, 192, 192, "F12S"),
    (2, 0, 192, "1F2S"),
    (2, 192, 192, "F12S"),
)
PLAN = {
    "x0": {
        0: (("az2", 0, 0), ("az1", 0, 0), ("az1", 1, 0), ("az2", 1, 0), ("zf", 0, 0), ("s", 0, 2), ("az1", 4, 0),),
    },
    "att": {
        0: (("s", 0, 1), ("az2", 2, 0), ("s", 1, 1), ("f", 0, 2), ("zf", 1, 0), ("s", 1, 2), ("s", 0, 3), ("az2", 4, 0), ("f", 0, 1), ("s", 4, 1), ("f", 1, 2), ("az1", 2, 0),),
        1: (("f", 1, 1), ("az1", 3, 0), ("s", 1, 3), ("az2", 3, 0), ("zf", 2, 0), ("f", 0, 3), ("c", 0, 1),),
        2: (("d", 0, 1), ("s", 2, 2), ("s", 2, 1), ("f", 4, 1), ("zf", 4, 0), ("c", 1, 1), ("c", 0, 2), ("az2", 5, 0), ("d", 1, 1), ("f", 1, 3),),
        3: (("s", 4, 2), ("c", 0, 3), ("f", 2, 2), ("d", 0, 2), ("c", 1, 2), ("f", 2, 1),),
        4: (("c", 1, 3), ("zf", 3, 0), ("s", 2, 3), ("s", 4, 3), ("d", 1, 2), ("f", 3, 1), ("az1", 5, 0),),
        5: (("f", 4, 2), ("c", 2, 1), ("d", 1, 3), ("az2", 6, 0), ("f", 3, 2), ("c", 4, 1), ("c", 2, 2), ("d", 0, 3),),
        6: (("zf", 5, 0), ("d", 4, 1), ("f", 2, 3), ("f", 3, 3),),
        7: (("d", 2, 1), ("c", 3, 1), ("f", 5, 2), ("az1", 6, 0),),
    },
    "n1": {
        0: (("d", 2, 2), ("f", 5, 1),),
    },
    "up": {
        0: (("c", 4, 2), ("d", 3, 1), ("f", 4, 3), ("c", 3, 2), ("zf", 6, 0),),
        1: (("c", 2, 3), ("c", 3, 3), ("c", 6, 2), ("f", 5, 3),),
        2: (("d", 3, 2),),
        3: (("d", 3, 3), ("c", 5, 1), ("d", 2, 3), ("c", 5, 2),),
    },
    "dn": {
        0: (("c", 6, 1), ("d", 6, 2), ("c", 4, 3),),
        1: (("d", 5, 1), ("c", 6, 3), ("c", 5, 3), ("d", 5, 2), ("d", 6, 1), ("d", 4, 2),),
        3: (("d", 4, 3), ("d", 6, 3), ("d", 5, 3),),
    },
    "l2": {
    },
    "da": {
        1: (("gFs", 5, 3),),
        2: (("gFs", 3, 3), ("gFr", 5, 3),),
        3: (("gFs", 3, 1),),
    },
    "gwo": {
        2: (("gFs", 2, 3), ("g1s", 5, 3),),
        3: (("gFr", 3, 3), ("g1r", 4, 2), ("gFs", 4, 2),),
    },
    "dn2": {
        0: (("g1s", 4, 3),),
        1: (("gFs", 5, 1), ("g1s", 4, 1),),
        3: (("g1s", 3, 3), ("gFs", 5, 0),),
    },
    "gwi": {
    },
    "l1b": {
        0: (("gFs", 3, 2), ("gFr", 5, 1), ("gFs", 5, 2), ("gFs", 2, 0),),
    },
    "ab": {
        1: (("gFs", 2, 2), ("g1r", 4, 0), ("gFr", 4, 2),),
        2: (("g2s", 4, 2),),
        3: (("gFs", 3, 0), ("g1s", 5, 1),),
        4: (("gFs", 2, 1), ("gFr", 3, 2),),
        5: (("gFs", 1, 3), ("gFr", 2, 3), ("g1r", 3, 2),),
        6: (("gFs", 1, 1),),
        7: (("g1s", 2, 3), ("gFs", 0, 1), ("gFr", 4, 0),),
    },
    "gwa": {
        0: (("gFs", 4, 0), ("gFr", 3, 1), ("g1s", 3, 1),),
        1: (("gFs", 0, 3), ("g2s", 3, 2),),
        2: (("g2r", 4, 0), ("gSs", 4, 0), ("gFr", 1, 3), ("gFr", 5, 2), ("g1r", 5, 2), ("g2s", 5, 2), ("gSs", 1, 3),),
        3: (("gFs", 0, 2), ("gFr", 3, 0), ("gFr", 2, 1), ("gFs", 1, 2), ("gFr", 2, 2),),
    },
    "fin": {
    },
    "end": {
        0: (("g1r", 3, 0), ("gFs", 0, 0), ("vs", 0, 0), ("gFr", 5, 0), ("g2r", 3, 0), ("gFr", 0, 3), ("gSs", 3, 0), ("gSr", 1, 3), ("vr", 0, 0), ("g1s", 2, 1), ("gSr", 4, 0), ("gFr", 0, 1), ("gFs", 1, 0), ("gFr", 1, 1), ("gFr", 1, 2), ("gSs", 0, 3), ("gS2s", 4, 0), ("gSs", 1, 1), ("g1r", 2, 2), ("g2s", 2, 2), ("gSs", 0, 1), ("vs", 1, 0), ("gFr", 2, 0), ("g1r", 5, 0), ("gSs", 1, 2), ("gFr", 0, 0), ("g2r", 5, 0), ("gSs", 5, 0), ("gSr", 3, 0), ("gS2s", 3, 0), ("g1s", 1, 3), ("gFr", 0, 2), ("gSs", 0, 2), ("gSr", 1, 1), ("gFr", 1, 0), ("gSr", 0, 3), ("g1r", 2, 0), ("g1s", 0, 3), ("gSs", 1, 0), ("gSs", 0, 0), ("gS2r", 4, 0), ("g1s", 1, 1), ("gSr", 5, 0), ("g2r", 2, 0), ("vr", 1, 0), ("gSr", 1, 2), ("gSs", 2, 0), ("vs", 2, 0), ("g1r", 1, 2), ("g2s", 1, 2), ("gSr", 0, 1), ("gS2s", 5, 0), ("gSr", 0, 2), ("g1r", 0, 2), ("g1s", 0, 1), ("gS2r", 3, 0), ("g2s", 0, 2), ("gSr", 2, 0), ("gSr", 1, 0), ("gSr", 0, 0), ("g1r", 1, 0), ("gF2r", 4, 0), ("gS2s", 2, 0), ("gS2r", 5, 0), ("vr", 2, 0), ("g2r", 1, 0), ("gS2s", 1, 0), ("vs", 3, 0), ("gC2r", 4, 0), ("gF2r", 3, 0), ("gS2r", 2, 0), ("g1r", 0, 0), ("gC2r", 3, 0), ("g2r", 0, 0), ("gS2s", 0, 0), ("gF2r", 5, 0), ("gS2r", 1, 0), ("vr", 3, 0), ("vs", 4, 0), ("gS2r", 0, 0), ("gF2r", 2, 0), ("vr", 4, 0), ("gC2r", 5, 0), ("gC2r", 2, 0), ("gF2r", 1, 0), ("gF2r", 0, 0), ("gC2r", 1, 0), ("gC2r", 0, 0),),
    },
}
V_OB, V_G1, V_S1, V_EB, V_G2, V_S2 = 8, 9, 10, 11, 12, 13


def dot(left, right, dims):
    return lax.dot_general(left, right, dims, preferred_element_type=F32)


def depth_at(p, stage):
    done = SUMMED[p][3].split(stage)[0]
    return ("F" in done) + ("S" in done)


def z_rows(p, slot):
    sizes = {}
    for q, (_, _, n, chain) in enumerate(SUMMED):
        for t in range(3):
            sizes[q, t] = n >> depth_at(q, "Z" if "Z" in chain else "112"[t])
    return sum(n for key, n in sizes.items() if key < (p, slot)), sizes[p, slot]


def layer_kernel(
    cfg,
    tok, cot, wq, wk, wv, wo, wi, wout, bq, bv, bi, bo, g1, s1, be, g2, s2, seg_in, live_in,
    out_ref, dx_ref, whole, vec_ref,
    wbuf, bias, xs, cots, qkv, ka, ks, prob, mask, acc, tmp, nh1, r1,
    nb, nhalf, af, asib, al, gp, g, sg, di, fg,
    gr, rf, rz, rs, rx, vrecv, vin, short,
    seg, live, *rest,
):
    n_dp, d, seq, rows = cfg["dp"], cfg["d"], cfg["seq"], cfg["rows"]
    tl = seq * rows
    ml = d // 4
    hs = ml // DH
    half, qtr, eig = d // 2, d // 4, d // 8
    scale = DH ** (-0.5)
    bits = n_dp.bit_length() - 1
    dp, z = lax.axis_index("dp"), lax.axis_index("mp")
    c = dp % 2
    df = 2 + 2 * c
    ds_ = 6 - df
    f, s = (dp // df) % 2, (dp // ds_) % 2
    p_x = dp + df * (1 - 2 * f) + ds_ * (1 - 2 * s)
    p_f, p_s, p_c = dp + df * (1 - 2 * f), dp + ds_ * (1 - 2 * s), dp + 1 - 2 * c
    z0, zh = z % 2, z // 2
    z1, z2, z3 = z + 1 - 2 * z0, z + 2 - 4 * zh, 3 - z
    h0 = pl.multiple_of(c * half, 128)
    ho = pl.multiple_of((1 - c) * half, 128)

    def sub(base, n, depth, other=False):
        off = base
        for level, bit in enumerate((c, f, s)[:depth]):
            n //= 2
            off = off + n * (1 - bit if other and level == depth - 1 else bit)
        return (pl.multiple_of(off, 16) if depth else off), n

    def cut(base, n, depth, other=False):
        off = base
        for level, bit in enumerate((f, s)[:depth]):
            n //= 2
            off = off + n * (1 - bit if other and level == depth - 1 else bit)
        return (pl.multiple_of(off, 16) if depth else off), n

    gathered = {}
    for a, (piece, base, n, cuts) in enumerate(GATHERED):
        for depth in (1, 2, 3):
            for other in (False, True):
                gathered[a, depth, other] = sub(base, n, depth, other)
    summed = {}
    for p, (piece, base, n, chain) in enumerate(SUMMED):
        for depth in (0, 1, 2):
            for other in (False, True):
                summed[p, depth, other] = cut(base, n, depth, other)

    finals = {}
    for p, (piece, base, n, chain) in enumerate(SUMMED):
        for depth in (0, 1, 2):
            for other in (False, True):
                off, m = summed[p, depth, other]
                finals[p, depth, other] = (pl.multiple_of(c * half + off, 16), m)
        finals[p, "core", True] = (pl.multiple_of((1 - c) * half + base, 16), n)
    shard = (z, z1, z2, z3)

    def shard_of(k):
        k0, kh = k % 2, k // 2
        return z0 + k0 - 2 * z0 * k0 + 2 * (zh + kh - 2 * zh * kh)

    def remote(src, dst, ssem, rsem, dev):
        return pltpu.make_async_remote_copy(
            src_ref=src, dst_ref=dst, send_sem=ssem, recv_sem=rsem, device_id=dev, device_id_type=MESH
        )

    pending = []

    def send(make, group="early"):
        remote(*make()).start()
        pending.append((group, make))

    def flush(group):
        for item in [item for item in pending if item[0] == group]:
            remote(*item[1]()).wait_send()
            pending.remove(item)

    small = rest[:9]
    loc_sem, ag_s, ag_r, gr_s, gr_r, x_s, x_r, b_s, b_r, v_s, v_r, e_s, e_r = rest[9:]
    barrier = pltpu.get_barrier_semaphore()
    extra = [dp + (1 << b) * (1 - 2 * ((dp // (1 << b)) % 2)) for b in range(3, bits)]
    greet = [(p_c, z), (p_f, z), (p_s, z), (p_x, z), (dp, z1), (dp, z2), (dp, z3)] + [(e, z) for e in extra]
    for dev in greet:
        pl.semaphore_signal(barrier, inc=1, device_id=dev, device_id_type=MESH)
    att_loads = [
        pltpu.make_async_copy(ref, wbuf.at[ATT, z, pl.ds(j * ml, ml)], loc_sem.at[j])
        for j, ref in enumerate((wq, wk, wv, wo))
    ]
    vec_loads = [
        pltpu.make_async_copy(ref, dst, loc_sem.at[4 + j])
        for j, (ref, dst) in enumerate(zip((bq, bv, bi, bo, g1, s1, be, g2, s2), small))
    ]
    seg_loads = [
        pltpu.make_async_copy(seg_in, seg, loc_sem.at[13]),
        pltpu.make_async_copy(live_in, live, loc_sem.at[14]),
        pltpu.make_async_copy(tok, xs.at[pl.ds(0, rows)], loc_sem.at[15]),
    ]
    late_loads = [
        pltpu.make_async_copy(wi, wbuf.at[INN, z], loc_sem.at[16]),
        pltpu.make_async_copy(wout, wbuf.at[OUT, z], loc_sem.at[17]),
        pltpu.make_async_copy(cot, cots, loc_sem.at[18]),
    ]
    for cp in att_loads + vec_loads + seg_loads + late_loads:
        cp.start()
    for cp in att_loads:
        cp.wait()
    pl.semaphore_wait(barrier, len(greet))

    def own(piece, off, n):
        if piece == ATT:
            return wbuf.at[ATT, z, pl.ds(off, n)]
        return (wi, wout)[piece - 1].at[pl.ds(off, n)]

    def reg(piece, k, off, n):
        return wbuf.at[piece, shard[k], pl.ds(off, n)]

    def ag_send(a, slot, k, rows_of, dev, mine=False):
        piece = GATHERED[a][0]

        def make():
            region = reg(piece, k, *rows_of)
            return own(piece, *rows_of) if mine else region, region, ag_s.at[a, slot], ag_r.at[a, slot], dev

        send(make)

    def ag_wait(a, slot, k, rows_of):
        region = reg(GATHERED[a][0], k, *rows_of)
        remote(region, region, ag_s.at[a, slot], ag_r.at[a, slot], (dp, z1)).wait_recv()

    def first(a):
        return gathered[a, GATHERED[a][3], False]

    def a_z1(a, _):
        ag_send(a, 1, 0, first(a), (dp, z1), True)

    def a_z2(a, _):
        ag_send(a, 0, 0, first(a), (dp, z2), True)

    def a_zf(a, _):
        ag_wait(a, 0, 2, first(a))
        ag_send(a, 2, 2, first(a), (dp, z1))

    def a_arrive(a, k):
        if k != 2:
            ag_wait(a, {1: 1, 3: 2}[k], k, first(a))

    def a_s(a, k):
        a_arrive(a, k)
        ag_send(a, 2 + k, k, gathered[a, 3, False], (p_s, z))

    def a_f(a, k):
        if GATHERED[a][3] < 3:
            a_arrive(a, k)
        else:
            ag_wait(a, 2 + k, k, gathered[a, 3, True])
        ag_send(a, 5 + k, k, gathered[a, 2, False], (p_f, z))

    def a_c(a, k):
        if GATHERED[a][3] < 2:
            a_arrive(a, k)
        else:
            ag_wait(a, 5 + k, k, gathered[a, 2, True])
        ag_send(a, 8 + k, k, gathered[a, 1, False], (p_c, z))

    def a_d(a, k):
        ag_wait(a, 8 + k, k, gathered[a, 1, True])

    X_TOK, X_N, X_FG, X_A, X_DI, X_KA, X_G = 0, 1, 2, 4, 8, 12, 16

    def core_send(slot, pair):
        send(lambda: (*pair(), x_s.at[slot], x_r.at[slot], (p_c, z)))

    def core_wait(slot, dst):
        remote(dst, dst, x_s.at[slot], x_r.at[slot], (p_c, z)).wait_recv()

    def g_sem(p, slot):
        return gr_s.at[p, slot], gr_r.at[p, slot]

    def g_send(p, slot, pair, dev):
        send(lambda: (*pair(), *g_sem(p, slot), dev), p if slot < 11 else "late")

    def g_wait(p, slot, dst):
        remote(dst, dst, *g_sem(p, slot), (dp, z1)).wait_recv()

    def add_into(dst, src, n):
        m = 48 if n % 48 == 0 else (32 if n % 32 == 0 else 16)

        def blk(j, carry):
            sl = pl.ds(pl.multiple_of(j * m, 16), m)
            dst[sl, :] = (dst[sl, :].astype(F32) + src[sl, :].astype(F32)).astype(BF)
            return carry

        lax.fori_loop(0, n // m, blk, 0)

    def chunk(p, k, depth, other=False):
        off, n = summed[p, depth, other]
        return gr.at[SUMMED[p][0], k, pl.ds(off, n)]

    def final(p, depth, other=False):
        off, n = finals[p, depth, other]
        return whole.at[SUMMED[p][0], pl.ds(off, n)]

    def final_across(p, side):
        _, base, n, _ = SUMMED[p]
        off = pl.multiple_of(c * half + base + (1 - f) * (n // 2) + side * (n // 4), 16)
        return whole.at[SUMMED[p][0], pl.ds(off, n // 4)]

    def f_slot(p, k):
        piece, base, n, _ = SUMMED[p]
        return rf.at[piece, k, pl.ds(base // 2, n // 2)]

    def s_slot(p, k):
        piece, base, n, _ = SUMMED[p]
        return rs.at[piece, k, pl.ds(base // 4, n // 4)]

    def z_slot(p, slot):
        return rz.at[pl.ds(*z_rows(p, slot))]

    def g_fs(p, k):
        g_send(p, k, lambda: (chunk(p, k, 1, True), f_slot(p, k)), (p_f, z))

    def g_fr(p, k):
        g_wait(p, k, f_slot(p, k))
        add_into(chunk(p, k, 1), f_slot(p, k), SUMMED[p][2] // 2)

    def g_ss(p, k):
        g_send(p, 4 + k, lambda: (chunk(p, k, 2, True), s_slot(p, k)), (p_s, z))

    def g_sr(p, k):
        g_wait(p, 4 + k, s_slot(p, k))
        add_into(chunk(p, k, 2), s_slot(p, k), SUMMED[p][2] // 4)

    def g_1s(p, k):
        slot = 0 if k == 3 else 1
        g_send(p, 8 + slot, lambda: (chunk(p, k, depth_at(p, "1")), z_slot(p, slot)), (dp, z1))

    def g_1r(p, k):
        slot = 0 if k == 2 else 1
        g_wait(p, 8 + slot, z_slot(p, slot))
        depth = depth_at(p, "1")
        add_into(chunk(p, k, depth), z_slot(p, slot), SUMMED[p][2] >> depth)

    def g_2s(p, k):
        g_send(p, 10, lambda: (chunk(p, 2, depth_at(p, "2")), z_slot(p, 2)), (dp, z2))

    def g_2r(p, k):
        g_wait(p, 10, z_slot(p, 2))
        depth = depth_at(p, "2")
        add_into(chunk(p, 0, depth), z_slot(p, 2), SUMMED[p][2] >> depth)

    def g_zs(p, k):
        depth = depth_at(p, "Z")
        g_send(p, 7 + k, lambda: (chunk(p, k, depth), z_slot(p, k - 1)), (dp, shard[k]))

    def g_zr(p, k):
        depth = depth_at(p, "Z")
        g_wait(p, 7 + k, z_slot(p, k - 1))
        add_into(chunk(p, 0, depth), z_slot(p, k - 1), SUMMED[p][2] >> depth)

    def g_s2s(p, _):
        piece, base, n, _ = SUMMED[p]
        for j, partner in enumerate(extra):
            slot = rx.at[piece, j, pl.ds(base // 4, n // 4)]
            cp = remote(chunk(p, 0, 2), slot, e_s.at[p, j], e_r.at[p, j], (partner, z))
            cp.start()
            cp.wait()
            add_into(chunk(p, 0, 2), slot, n // 4)
        mine, target = chunk(p, 0, 2), final(p, 2)
        for lo in range(0, n // 4, 16):
            target[pl.ds(lo, 16), :] = mine[pl.ds(lo, 16), :]
        g_send(p, 11, lambda: (final(p, 2),) * 2, (p_s, z))
        if SUMMED[p][3].endswith("d"):
            g_send(p, 12, lambda: (final(p, 2),) * 2, (p_f, z))
            g_send(p, 14, lambda: (final(p, 2),) * 2, (p_x, z))

    def g_s2r(p, _):
        g_wait(p, 11, final(p, 2, True))
        g_send(p, 12, lambda: (final(p, 1),) * 2, (p_f, z))

    def g_d2sr(p, _):
        g_wait(p, 11, final(p, 2, True))

    def g_d2fr(p, _):
        g_wait(p, 12, final_across(p, s))

    def g_f2r(p, _):
        if SUMMED[p][3].endswith("d"):
            g_wait(p, 14, final_across(p, 1 - s))
        else:
            g_wait(p, 12, final(p, 1, True))
        g_send(p, 13, lambda: (final(p, 0),) * 2, (p_c, z))
        flush(p)

    def g_c2r(p, _):
        g_wait(p, 13, final(p, "core", True))

    partners = [(p_c, z), (p_f, z), (p_s, z), (dp, z1), (dp, z2)] + [(e, z) for e in extra]

    def v_half(mine):
        return vec_ref.at[pl.ds(pl.multiple_of(8 * (c if mine else 1 - c), 8), 8)]

    def v_copy(j):
        return remote(v_half(j > 0), vrecv.at[j], v_s.at[j], v_r.at[j], partners[j])

    def v_send(j, _):
        v_copy(j).start()

    def v_back():
        return remote(v_half(True), v_half(True), v_s.at[len(partners)], v_r.at[len(partners)], (p_c, z))

    def v_recv(j, _):
        v_copy(j).wait()
        half_ref = v_half(True)
        half_ref[...] = half_ref[...] + vrecv[j]
        if j == len(partners) - 1:
            v_back().start()

    events = {
        "az1": a_z1, "az2": a_z2, "zf": a_zf, "s": a_s, "f": a_f, "c": a_c, "d": a_d,
        "gFs": g_fs, "gFr": g_fr, "gSs": g_ss, "gSr": g_sr, "g1s": g_1s, "g1r": g_1r, "g2s": g_2s, "g2r": g_2r,
        "gZs": g_zs, "gZr": g_zr, "gd2Fr": g_d2fr, "gd2Sr": g_d2sr, "gS2s": g_s2s, "gS2r": g_s2r, "gF2r": g_f2r, "gC2r": g_c2r, "vs": v_send, "vr": v_recv,
    }

    def do(listed):
        for kind, piece, k in listed:
            events[kind](piece, k)

    def at(place, index):
        for n, listed in PLAN.get(place, {}).items():
            pl.when(index == n)(functools.partial(do, listed))

    def once(place):
        do(PLAN.get(place, {}).get(0, ()))

    once("x0")
    for cp in vec_loads:
        cp.wait()
    vin[...] = jnp.zeros_like(vin)
    vin[pl.ds(0, 1), pl.ds(0, ml)] = small[0][...].astype(F32).reshape(1, ml)
    vin[pl.ds(0, 1), pl.ds(2 * ml, ml)] = small[1][...].astype(F32).reshape(1, ml)
    for j, ref in enumerate(small[2:]):
        vin[pl.ds(j + 1, 1), :] = ref[...].astype(F32).reshape(1, d)
    bias[z] = vin[...]
    third = d // 3
    short[z] = jnp.zeros((8, third), F32)
    short[z, pl.ds(0, 1), pl.ds(0, ml)] = vin[pl.ds(0, 1), pl.ds(0, ml)]
    short[z, pl.ds(1, 1), pl.ds(0, ml)] = vin[pl.ds(0, 1), pl.ds(2 * ml, ml)]
    for j in range(3):
        short[z, pl.ds(2 + j, 1), :] = vin[pl.ds(1, 1), pl.ds(j * third, third)]
    for j, zz in enumerate((z1, z2, z3)):
        send(lambda j=j, zz=zz: (short.at[z], short.at[z], b_s.at[j], b_r.at[j], (dp, zz)))
    core_send(X_TOK, lambda: (tok, xs.at[pl.ds(rows, rows)]))
    for cp in seg_loads:
        cp.wait()

    for r in range(rows):
        seg_row = seg[pl.ds(z * rows + r, 1), :]
        live_row = live[pl.ds(z * rows + r, 1), :]
        code = jnp.where(live_row == 1, seg_row, -1)
        ids = lax.broadcasted_iota(jnp.int32, (8, seq), 0)
        key_hot = (jnp.broadcast_to(code, (8, seq)) == ids).astype(F32).astype(BF)
        query_hot = (jnp.broadcast_to(seg_row, (8, seq)) == ids).astype(F32).astype(BF)
        mask[r] = jnp.where(dot(key_hot, query_hot, TN) > 0.5, 0.0, NEG_FILL)
    acc[...] = jnp.zeros_like(acc)
    first_row = (lax.broadcasted_iota(jnp.int32, (8, seq), 0) == 0).astype(F32).astype(BF)

    def attend(i, carry):
        t = shard_of(i)

        def row(r, inner_carry):
            at("att", i * rows + r)

            @pl.when((i == 1) & (r == 0))
            def _():
                for j, zz in enumerate((z1, z2, z3)):
                    remote(short.at[zz], short.at[zz], b_s.at[j], b_r.at[j], (dp, zz)).wait_recv()
                    bias[zz] = jnp.zeros((8, d), F32)
                    bias[zz, pl.ds(0, 1), pl.ds(0, ml)] = short[zz, pl.ds(0, 1), pl.ds(0, ml)]
                    bias[zz, pl.ds(0, 1), pl.ds(2 * ml, ml)] = short[zz, pl.ds(1, 1), pl.ds(0, ml)]
                    for n in range(3):
                        bias[zz, pl.ds(1, 1), pl.ds(n * third, third)] = short[zz, pl.ds(2 + n, 1), :]

            x_row = xs[r]
            bias_rows = bias[t].astype(BF)[:, : 3 * ml]
            qkv[t, r] = (
                dot(wbuf[ATT, t, pl.ds(0, 3 * ml), :], x_row, NT) + dot(bias_rows, first_row, TN)
            ).astype(BF)
            for h in range(hs):
                query = qkv[t, r, pl.ds(h * DH, DH), :]
                key = qkv[t, r, pl.ds(ml + h * DH, DH), :]
                value = qkv[t, r, pl.ds(2 * ml + h * DH, DH), :]
                scores = dot(key, query, TN) * scale + mask[r]
                top = jnp.max(scores, 0, keepdims=True)
                exponent = jnp.exp(scores - top)
                total = jnp.sum(exponent, 0, keepdims=True)
                prob_t = (exponent * (1.0 / total)).astype(BF)
                prob[t, r, h] = prob_t
                ka[t, r, pl.ds(3 * ml + h * DH, DH), :] = dot(value, prob_t, NN).astype(BF)
            part_sum = dot(ka[t, r, pl.ds(3 * ml, ml), :], wbuf[ATT, t, pl.ds(3 * ml, ml), :], TN)
            sl = pl.ds(pl.multiple_of(r * seq, 16), seq)
            acc[sl, :] = acc[sl, :] + part_sum
            return inner_carry

        lax.fori_loop(0, rows, row, 0)
        return carry

    lax.fori_loop(0, 4, attend, 0)

    rb = seq

    def norm_rows(summed):
        mean = jnp.mean(summed, -1, keepdims=True)
        centred = summed - mean
        variance = jnp.mean(centred * centred, -1, keepdims=True)
        rs_ = lax.rsqrt(variance + EPSILON)
        return centred * rs_, rs_

    def norm_back(grad, hat, rs_):
        return rs_ * (grad - jnp.mean(grad, -1, keepdims=True) - hat * jnp.mean(grad * hat, -1, keepdims=True))

    def vrow(j):
        return vin[pl.ds(j, 1), :]

    once("n1")

    def norm1(j, carry):
        sl = pl.ds(pl.multiple_of(j * rb, 16), rb)
        per = seq // rb
        x_blk = xs[j // per, pl.ds(pl.multiple_of((j % per) * rb, 16), rb), :].astype(F32)
        hat, rs_ = norm_rows(acc[sl, :] + vrow(2) + x_blk)
        nh1[sl, :] = hat
        r1[sl, :] = jnp.broadcast_to(rs_, (rb, 128))
        nb[sl, :] = (hat * vrow(3) + vrow(4)).astype(BF)
        acc[sl, :] = jnp.zeros((rb, d), F32)
        return carry

    lax.fori_loop(0, tl // rb, norm1, 0)
    core_send(X_N, lambda: (nb.at[:, pl.ds(ho, half)], nhalf.at[pl.ds(tl, tl)]))
    nhalf[pl.ds(0, tl), :] = nb[:, pl.ds(h0, half)]

    late_loads[0].wait()

    def up(i, carry):
        at("up", i)
        t = shard_of(i)
        tmp[...] = dot(nb[...], wbuf[INN, t], NN)
        b_row = bias[t, pl.ds(1, 1), :]

        def act(j, carry):
            sl = pl.ds(pl.multiple_of(j * rb, 16), rb)
            u = tmp[sl, :] + b_row
            cdf = 0.5 * (1.0 + lax.erf(u * ROOT_HALF))
            af[t, sl, :] = (u * cdf).astype(BF)
            gp[t, sl, :] = (cdf + u * (PDF_SCALE * jnp.exp(-0.5 * u * u))).astype(BF)
            return carry

        lax.fori_loop(0, tl // rb, act, 0)
        remote(af.at[t, :, pl.ds(ho, half)], asib.at[t], x_s.at[X_A + i], x_r.at[X_A + i], (p_c, z)).start()
        return carry

    lax.fori_loop(0, 4, up, 0)
    late_loads[1].wait()
    late_loads[2].wait()

    def down(i, carry):
        at("dn", i)
        t = shard_of(i)
        acc[...] += dot(af[t], wbuf[OUT, t], NN)
        return carry

    lax.fori_loop(0, 4, down, 0)

    once("l2")
    vec_ref[...] = jnp.zeros_like(vec_ref)

    def add_vec(row, value):
        vec_ref[pl.ds(row, 1), :] = vec_ref[pl.ds(row, 1), :] + value

    def norm2(j, carry):
        sl = pl.ds(pl.multiple_of(j * rb, 16), rb)
        normed = nh1[sl, :] * vrow(3) + vrow(4)
        hat, rs_ = norm_rows(acc[sl, :] + vrow(5) + normed)
        c_blk = cots[sl, :].astype(F32)
        out_ref[sl, :] = (hat * vrow(6) + vrow(7)).astype(BF)
        back = norm_back(c_blk * vrow(6), hat, rs_)
        sg[sl, :] = back
        g[sl, :] = back.astype(BF)
        acc[sl, :] = jnp.zeros((rb, d), F32)
        add_vec(V_G2, jnp.sum(c_blk * hat, 0, keepdims=True))
        add_vec(V_S2, jnp.sum(c_blk, 0, keepdims=True))
        add_vec(V_EB, jnp.sum(back, 0, keepdims=True))
        return carry

    def g_copy(j):
        src = g.at[pl.ds(pl.multiple_of(j * rb, 16), rb)]
        dst = g.at[pl.ds(pl.multiple_of(tl + j * rb, 16), rb)]
        return remote(src, dst, x_s.at[X_G + j], x_r.at[X_G + j], (p_c, z))

    for j in range(tl // rb):
        norm2(j, 0)
        g_copy(j).start()
    def order(i):
        return 3 - 2 * (i % 2) - i // 2

    def ffn_back(i, carry):
        @pl.when(i < 4)
        def _():
            at("da", i)
            k = order(i)
            t = shard_of(k)
            tmp[...] = dot(g[pl.ds(0, tl), :], wbuf[OUT, t], NT)

            def act(j, total):
                sl = pl.ds(pl.multiple_of(j * rb, 16), rb)
                blk = (tmp[sl, :] * gp[t, sl, :].astype(F32)).astype(BF)
                di[t, sl, :] = blk
                return total + jnp.sum(blk.astype(F32), 0, keepdims=True)

            vec_ref[pl.ds(4 + t, 1), :] = lax.fori_loop(0, tl // rb, act, jnp.zeros((1, d), F32))
            remote(
                di.at[t, pl.ds(0, tl)], di.at[t, pl.ds(tl, tl)], x_s.at[X_DI + k], x_r.at[X_DI + k], (p_c, z)
            ).start()
            at("gwo", i)

            @pl.when(i == 0)
            def _():
                for j in range(tl // rb):
                    g_copy(j).wait_recv()
                core_wait(X_N, nhalf.at[pl.ds(tl, tl)])

            core_wait(X_A + k, asib.at[t])
            al[pl.ds(0, tl), :] = af[t, :, pl.ds(h0, half)]
            al[pl.ds(tl, tl), :] = asib[t]
            gr[OUT, k] = dot(al[...], g[...], TN).astype(BF)
            at("dn2", i)
            acc[...] += dot(di[t, pl.ds(0, tl), :], wbuf[INN, t], NT)

        @pl.when(i > 0)
        def _():
            at("gwi", i - 1)
            k = order(i - 1)
            t = shard_of(k)
            core_wait(X_DI + k, di.at[t, pl.ds(tl, tl)])
            gr[INN, k] = dot(nhalf[...], di[t], TN).astype(BF)

        return carry

    lax.fori_loop(0, 5, ffn_back, 0)
    once("l1b")

    def norm1_back(j, carry):
        sl = pl.ds(pl.multiple_of(j * rb, 16), rb)
        per = seq // rb
        hat = nh1[sl, :]
        total = acc[sl, :] + sg[sl, :]
        back = norm_back(total * vrow(3), hat, r1[sl, 0:1])
        sg[sl, :] = back
        fg[j // per, pl.ds(pl.multiple_of((j % per) * rb, 16), rb), :] = back.astype(BF)
        acc[sl, :] = jnp.zeros((rb, d), F32)
        add_vec(V_G1, jnp.sum(total * hat, 0, keepdims=True))
        add_vec(V_S1, jnp.sum(total, 0, keepdims=True))
        add_vec(V_OB, jnp.sum(back, 0, keepdims=True))
        return carry

    lax.fori_loop(0, tl // rb, norm1_back, 0)
    core_send(X_FG, lambda: (fg.at[pl.ds(0, rows)], fg.at[pl.ds(rows, rows)]))
    ones = jnp.ones((8, seq), BF)

    def att_back(i, carry):
        @pl.when(i < 4)
        def _():
            k = order(i)
            t = shard_of(k)

            def row(r, inner_carry):
                at("ab", i * rows + r)
                dctx = dot(wbuf[ATT, t, pl.ds(3 * ml, ml), :], fg[r], NT).astype(BF)
                for h in range(hs):
                    query = qkv[t, r, pl.ds(h * DH, DH), :]
                    key = qkv[t, r, pl.ds(ml + h * DH, DH), :]
                    value = qkv[t, r, pl.ds(2 * ml + h * DH, DH), :]
                    prob_t = prob[t, r, h]
                    grad = dctx[h * DH : (h + 1) * DH]
                    ka[t, r, pl.ds(2 * ml + h * DH, DH), :] = dot(grad, prob_t, NT).astype(BF)
                    prob_grad = dot(value, grad, TN)
                    wide_prob = prob_t.astype(F32)
                    inner = jnp.sum(wide_prob * prob_grad, 0, keepdims=True)
                    score_grad = (wide_prob * (prob_grad - inner)).astype(BF)
                    ka[t, r, pl.ds(h * DH, DH), :] = (dot(key, score_grad, NN) * scale).astype(BF)
                    ka[t, r, pl.ds(ml + h * DH, DH), :] = (dot(query, score_grad, NT) * scale).astype(BF)
                grads = ka[t, r, pl.ds(0, 3 * ml), :]
                vec_ref[pl.ds(t, 1), pl.ds(0, 3 * ml)] += dot(ones, grads, NT)[0:1]
                sl = pl.ds(pl.multiple_of(r * seq, 16), seq)
                acc[sl, :] = acc[sl, :] + dot(grads, wbuf[ATT, t, pl.ds(0, 3 * ml), :], TN)
                return inner_carry

            lax.fori_loop(0, rows, row, 0)
            remote(
                ka.at[t, :, pl.ds(ho, half)], ks.at[t], x_s.at[X_KA + k], x_r.at[X_KA + k], (p_c, z)
            ).start()

        @pl.when(i == 0)
        def _():
            core_wait(X_TOK, xs.at[pl.ds(rows, rows)])
            core_wait(X_FG, fg.at[pl.ds(rows, rows)])

        @pl.when(i > 0)
        def _():
            at("gwa", i - 1)
            k = order(i - 1)
            t = shard_of(k)
            core_wait(X_KA + k, ks.at[t])
            for j in range(2):
                rowsel = pl.ds(pl.multiple_of(h0 + j * ml, 16), ml)
                use = c * j
                total = jnp.zeros((ml, d), F32)
                for r in range(rows):
                    right_own = xs[r] if j == 0 else jnp.where(use == 1, fg[r], xs[r])
                    right_sib = xs[rows + r] if j == 0 else jnp.where(use == 1, fg[rows + r], xs[rows + r])
                    total += dot(ka[t, r, rowsel, :], right_own, NN)
                    total += dot(ks[t, r, pl.ds(j * ml, ml), :], right_sib, NN)
                gr[ATT, k, pl.ds(j * ml, ml), :] = total.astype(BF)

        return carry

    lax.fori_loop(0, 5, att_back, 0)
    once("fin")

    def finish(j, carry):
        sl = pl.ds(pl.multiple_of(j * rb, 16), rb)
        dx_ref[sl, :] = (sg[sl, :] + acc[sl, :]).astype(BF)
        return carry

    lax.fori_loop(0, tl // rb, finish, 0)


    flush("early")

    def sent(k, carry):
        t = shard_of(k)
        remote(af.at[t, :, pl.ds(ho, half)], asib.at[t], x_s.at[X_A + k], x_r.at[X_A + k], (p_c, z)).wait_send()
        remote(
            di.at[t, pl.ds(0, tl)], di.at[t, pl.ds(tl, tl)], x_s.at[X_DI + k], x_r.at[X_DI + k], (p_c, z)
        ).wait_send()
        remote(ka.at[t, :, pl.ds(ho, half)], ks.at[t], x_s.at[X_KA + k], x_r.at[X_KA + k], (p_c, z)).wait_send()
        return carry

    lax.fori_loop(0, 4, sent, 0)
    for j in range(tl // rb):
        g_copy(j).wait_send()

    once("end")
    for j in range(5, len(partners)):
        v_send(j, 0)
        v_recv(j, 0)
    other_half = v_half(False)
    remote(other_half, other_half, v_s.at[len(partners)], v_r.at[len(partners)], (p_c, z)).wait_recv()
    v_back().wait_send()

    flush("late")
    assert not pending


def spread_kernel(
    ml, grads, vec, out_in, dx_in,
    out_ref, dx_ref, gq, gk, gv, go, gi, ge, bq, bv, bo, g1, s1, bi, be, g2, s2,
    wide_v, *rest,
):
    z = lax.axis_index("mp")
    n = 2 * ml
    outs = []
    small, sem = rest[:9], rest[9]

    def put(src, dst):
        cp = pltpu.make_async_copy(src, dst, sem.at[len(outs)])
        cp.start()
        outs.append(cp)

    put(out_in, out_ref)
    put(dx_in, dx_ref)
    picks = [(z, 0, ml, bq), (z, 2 * ml, ml, bv), (4 + z, 0, 4 * ml, bi)]
    picks += [
        (row, 0, 4 * ml, ref)
        for row, ref in ((V_OB, bo), (V_G1, g1), (V_S1, s1), (V_EB, be), (V_G2, g2), (V_S2, s2))
    ]
    steps = [(piece, lo, [(ref, lo, n)]) for piece, ref in ((1, gi), (2, ge)) for lo in (0, n)]
    steps += [(0, 0, [(gq, 0, ml), (gk, 0, ml)]), (0, n, [(gv, 0, ml), (go, 0, ml)])]
    for piece, lo, refs in steps:
        wide_v[piece, pl.ds(lo, n), :] = grads[piece, pl.ds(lo, n), :].astype(F32)
        at = lo
        for ref, row, m in refs:
            put(wide_v.at[piece, pl.ds(at, m)], ref.at[pl.ds(row, m)])
            at += m
    for (row, lo, m, ref), buf in zip(picks, small):
        buf[...] = vec[pl.ds(row, 1), pl.ds(lo, m)].reshape(m)
        put(buf, ref)
    for cp in outs:
        cp.wait()


def per_device(
    n_dp,
    tokens, segment_ids, live_mask, query_weight, key_weight, value_weight, query_bias, value_bias,
    output_weight, output_bias, first_gain, first_shift, inner_weight, inner_bias, outer_weight,
    outer_bias, second_gain, second_shift, cotangent,
):
    tl, d = tokens.shape
    seq_rows, seq = segment_ids.shape
    rows = tl // seq
    ml = query_weight.shape[1]
    ff = inner_weight.shape[1]
    half, qtr, eig = d // 2, d // 4, d // 8
    bits = n_dp.bit_length() - 1
    n_extra = max(bits - 3, 1)
    n_vec = bits + 3
    cfg = {"dp": n_dp, "d": d, "seq": seq, "rows": rows}
    vmem = pl.BlockSpec(memory_space=pltpu.VMEM)
    hbm = pl.BlockSpec(memory_space=pl.ANY)
    scratch = [
        pltpu.VMEM((3, 4, d, d), BF),
        pltpu.VMEM((4, 8, d), F32),
        pltpu.VMEM((2 * rows, seq, d), BF),
        pltpu.VMEM((tl, d), BF),
        pltpu.VMEM((4, rows, 3 * ml, seq), BF),
        pltpu.VMEM((4, rows, d, seq), BF),
        pltpu.VMEM((4, rows, half, seq), BF),
        pltpu.VMEM((4, rows, ml // DH, seq, seq), BF),
        pltpu.VMEM((rows, seq, seq), F32),
        pltpu.VMEM((tl, d), F32),
        pltpu.VMEM((tl, d), F32),
        pltpu.VMEM((tl, d), F32),
        pltpu.VMEM((tl, 128), F32),
        pltpu.VMEM((tl, d), BF),
        pltpu.VMEM((2 * tl, half), BF),
        pltpu.VMEM((4, tl, d), BF),
        pltpu.VMEM((4, tl, half), BF),
        pltpu.VMEM((2 * tl, half), BF),
        pltpu.VMEM((4, tl, d), BF),
        pltpu.VMEM((2 * tl, d), BF),
        pltpu.VMEM((tl, d), F32),
        pltpu.VMEM((4, 2 * tl, d), BF),
        pltpu.VMEM((2 * rows, seq, d), BF),
        pltpu.VMEM((3, 4, half, d), BF),
        pltpu.VMEM((3, 4, qtr, d), BF),
        pltpu.VMEM((sum(z_rows(len(SUMMED) - 1, 2)), d), BF),
        pltpu.VMEM((3, 4, eig, d), BF),
        pltpu.VMEM((3, n_extra, eig, d), BF) if bits > 3 else pltpu.VMEM((1, 1, 16, 128), BF),
        pltpu.VMEM((n_vec - 1, 8, d), F32),
        pltpu.VMEM((8, d), F32),
        pltpu.VMEM((4, 8, d // 3), F32),
        pltpu.VMEM((seq_rows, seq), jnp.int32),
        pltpu.VMEM((seq_rows, seq), jnp.int32),
    ]
    scratch += [pltpu.VMEM((n,), BF) for n in (ml, ml, ff, d, d, d, d, d, d)]
    scratch += [
        pltpu.SemaphoreType.DMA(shape)
        for shape in [(24,)] + [(len(GATHERED), 12)] * 2 + [(len(SUMMED), 15)] * 2 + [(16 + rows,)] * 2 + [(3,)] * 2
        + [(n_vec,)] * 2 + [(len(SUMMED), n_extra)] * 2
    ]
    out, dx, grads, vec = pl.pallas_call(
        functools.partial(layer_kernel, cfg),
        out_shape=(
            pltpu.VMEM((tl, d), BF),
            pltpu.VMEM((tl, d), BF),
            pltpu.VMEM((3, d, d), BF),
            pltpu.VMEM((16, d), F32),
        ),
        in_specs=[hbm] * 19,
        out_specs=(vmem,) * 4,
        scratch_shapes=scratch,
        compiler_params=pltpu.CompilerParams(
            collective_id=0, has_side_effects=True, vmem_limit_bytes=LIMIT
        ),
        name="layer",
    )(
        tokens.reshape(rows, seq, d), cotangent, query_weight.T, key_weight.T, value_weight.T, output_weight,
        inner_weight, outer_weight, query_bias, value_bias, inner_bias, output_bias, first_gain, first_shift,
        outer_bias, second_gain, second_shift, segment_ids, live_mask,
    )
    out, dx, gq, gk, gv, go, gi, ge, bq, bv, bo, g1, s1, bi, be, g2, s2 = pl.pallas_call(
        functools.partial(spread_kernel, ml),
        out_shape=tuple(
            jax.ShapeDtypeStruct(shape, dtype)
            for shape, dtype in [((tl, d), BF)] * 2
            + [((ml, d), F32)] * 4
            + [((d, ff), F32), ((ff, d), F32)]
            + [((ml,), F32)] * 2
            + [((d,), F32)] * 7
        ),
        in_specs=[vmem] * 4,
        out_specs=(hbm,) * 17,
        scratch_shapes=[pltpu.VMEM((3, d, d), F32)]
        + [pltpu.VMEM((n,), F32) for n in (ml, ml, ff, d, d, d, d, d, d)]
        + [pltpu.SemaphoreType.DMA((19,))],
        compiler_params=pltpu.CompilerParams(vmem_limit_bytes=24 * 1024 * 1024),
        name="spread",
    )(*(pltpu.with_memory_space_constraint(x, pltpu.VMEM) for x in (grads, vec, out, dx)))
    return out, dx, gq.T, gk.T, gv.T, bq, bv, go, bo, g1, s1, gi, bi, ge, be, g2, s2


def solution(mesh):
    tok, shared = P(("dp", "mp"), None), P()
    cols, rows, vec = P(None, "mp"), P("mp", None), P("mp")
    in_specs = (
        tok, P("dp", None), P("dp", None), cols, cols, cols, vec, vec, rows, shared, shared, shared,
        cols, vec, rows, shared, shared, shared, tok,
    )
    out_specs = (
        tok, tok, cols, cols, cols, vec, vec, rows, shared, shared, shared, cols, vec, rows,
        shared, shared, shared,
    )
    return jax.shard_map(
        functools.partial(per_device, mesh.shape["dp"]),
        mesh=mesh,
        in_specs=in_specs,
        out_specs=out_specs,
        check_vma=False,
    )
```

```python
import functools

import jax
import jax.numpy as jnp
from jax import lax
from jax.experimental import pallas as pl
from jax.experimental.pallas import tpu as pltpu
from jax.sharding import PartitionSpec as P

DH = 64
EPSILON = 1e-06
NEG_FILL = -1000000000.0
ROOT_HALF = 0.7071067811865476
PDF_SCALE = 0.3989422804014327
BF = jnp.bfloat16
F32 = jnp.float32
MESH = pl.DeviceIdType.MESH
LIMIT = 59 * 1024 * 1024

NN = (((1,), (0,)), ((), ()))
NT = (((1,), (1,)), ((), ()))
TN = (((0,), (0,)), ((), ()))

ATT, INN, OUT = 0, 1, 2
GATHERED = (
    (0, 0, 384, 3),
    (0, 384, 384, 3),
    (1, 0, 384, 3),
    (1, 384, 384, 2),
    (2, 0, 384, 3),
    (2, 384, 256, 2),
    (2, 640, 128, 1),
)
SUMMED = (
    (0, 0, 192, "FS12"),
    (0, 192, 192, "FS12"),
    (1, 0, 192, "F12S"),
    (1, 192, 192, "F12S"),
    (2, 0, 192, "1F2S"),
    (2, 192, 192, "F12S"),
)
PLAN = {
    "x0": {
        0: (("az2", 0, 0), ("az1", 0, 0), ("az1", 1, 0), ("az2", 1, 0), ("zf", 0, 0), ("s", 0, 2), ("az1", 4, 0),),
    },
    "att": {
        0: (("s", 0, 1), ("az2", 2, 0), ("s", 1, 1), ("f", 0, 2), ("zf", 1, 0), ("s", 1, 2), ("s", 0, 3), ("az2", 4, 0), ("f", 0, 1), ("s", 4, 1), ("f", 1, 2), ("az1", 2, 0),),
        1: (("f", 1, 1), ("az1", 3, 0), ("s", 1, 3), ("az2", 3, 0), ("zf", 2, 0), ("f", 0, 3), ("c", 0, 1),),
        2: (("d", 0, 1), ("s", 2, 2), ("s", 2, 1), ("f", 4, 1), ("zf", 4, 0), ("c", 1, 1), ("c", 0, 2), ("az2", 5, 0), ("d", 1, 1), ("f", 1, 3),),
        3: (("s", 4, 2), ("c", 0, 3), ("f", 2, 2), ("d", 0, 2), ("c", 1, 2), ("f", 2, 1),),
        4: (("c", 1, 3), ("zf", 3, 0), ("s", 2, 3), ("s", 4, 3), ("d", 1, 2), ("f", 3, 1), ("az1", 5, 0),),
        5: (("f", 4, 2), ("c", 2, 1), ("d", 1, 3), ("az2", 6, 0), ("f", 3, 2), ("c", 4, 1), ("c", 2, 2), ("d", 0, 3),),
        6: (("zf", 5, 0), ("d", 4, 1), ("f", 2, 3), ("f", 3, 3),),
        7: (("d", 2, 1), ("c", 3, 1), ("f", 5, 2), ("az1", 6, 0),),
    },
    "n1": {
        0: (("d", 2, 2), ("f", 5, 1),),
    },
    "up": {
        0: (("c", 4, 2), ("d", 3, 1), ("f", 4, 3), ("c", 3, 2), ("zf", 6, 0),),
        1: (("c", 2, 3), ("c", 3, 3), ("c", 6, 2), ("f", 5, 3),),
        2: (("d", 3, 2),),
        3: (("d", 3, 3), ("c", 5, 1), ("d", 2, 3), ("c", 5, 2),),
    },
    "dn": {
        0: (("c", 6, 1), ("d", 6, 2), ("c", 4, 3),),
        1: (("d", 5, 1), ("c", 6, 3), ("c", 5, 3), ("d", 5, 2), ("d", 6, 1), ("d", 4, 2),),
        3: (("d", 4, 3), ("d", 6, 3), ("d", 5, 3),),
    },
    "l2": {
    },
    "da": {
        1: (("gFs", 5, 3),),
        2: (("gFs", 3, 3), ("gFr", 5, 3),),
        3: (("gFs", 3, 1),),
    },
    "gwo": {
        2: (("gFs", 2, 3), ("g1s", 5, 3),),
        3: (("gFr", 3, 3), ("g1r", 4, 2), ("gFs", 4, 2),),
    },
    "dn2": {
        0: (("g1s", 4, 3),),
        1: (("gFs", 5, 1), ("g1s", 4, 1),),
        3: (("g1s", 3, 3), ("gFs", 5, 0),),
    },
    "gwi": {
    },
    "l1b": {
        0: (("gFs", 3, 2), ("gFr", 5, 1), ("gFs", 5, 2), ("gFs", 2, 0),),
    },
    "ab": {
        1: (("gFs", 2, 2), ("g1r", 4, 0), ("gFr", 4, 2),),
        2: (("g2s", 4, 2),),
        3: (("gFs", 3, 0), ("g1s", 5, 1),),
        4: (("gFs", 2, 1), ("gFr", 3, 2),),
        5: (("gFs", 1, 3), ("gFr", 2, 3), ("g1r", 3, 2),),
        6: (("gFs", 1, 1),),
        7: (("g1s", 2, 3), ("gFs", 0, 1), ("gFr", 4, 0),),
    },
    "gwa": {
        0: (("gFs", 4, 0), ("gFr", 3, 1), ("g1s", 3, 1),),
        1: (("gFs", 0, 3), ("g2s", 3, 2),),
        2: (("g2r", 4, 0), ("gSs", 4, 0), ("gFr", 1, 3), ("gFr", 5, 2), ("g1r", 5, 2), ("g2s", 5, 2), ("gSs", 1, 3),),
        3: (("gFs", 0, 2), ("gFr", 3, 0), ("gFr", 2, 1), ("gFs", 1, 2), ("gFr", 2, 2),),
    },
    "fin": {
    },
    "end": {
        0: (("g1r", 3, 0), ("gFs", 0, 0), ("vs", 0, 0), ("gFr", 5, 0), ("g2r", 3, 0), ("gFr", 0, 3), ("gSs", 3, 0), ("gSr", 1, 3), ("vr", 0, 0), ("g1s", 2, 1), ("gSr", 4, 0), ("gFr", 0, 1), ("gFs", 1, 0), ("gFr", 1, 1), ("gFr", 1, 2), ("gSs", 0, 3), ("gS2s", 4, 0), ("gSs", 1, 1), ("g1r", 2, 2), ("g2s", 2, 2), ("gSs", 0, 1), ("vs", 1, 0), ("gFr", 2, 0), ("g1r", 5, 0), ("gSs", 1, 2), ("gFr", 0, 0), ("g2r", 5, 0), ("gSs", 5, 0), ("gSr", 3, 0), ("gS2s", 3, 0), ("g1s", 1, 3), ("gFr", 0, 2), ("gSs", 0, 2), ("gSr", 1, 1), ("gFr", 1, 0), ("gSr", 0, 3), ("g1r", 2, 0), ("g1s", 0, 3), ("gSs", 1, 0), ("gSs", 0, 0), ("gS2r", 4, 0), ("g1s", 1, 1), ("gSr", 5, 0), ("g2r", 2, 0), ("vr", 1, 0), ("gSr", 1, 2), ("gSs", 2, 0), ("vs", 2, 0), ("g1r", 1, 2), ("g2s", 1, 2), ("gSr", 0, 1), ("gS2s", 5, 0), ("gSr", 0, 2), ("g1r", 0, 2), ("g1s", 0, 1), ("gS2r", 3, 0), ("g2s", 0, 2), ("gSr", 2, 0), ("gSr", 1, 0), ("gSr", 0, 0), ("g1r", 1, 0), ("gF2r", 4, 0), ("gS2s", 2, 0), ("gS2r", 5, 0), ("vr", 2, 0), ("g2r", 1, 0), ("gS2s", 1, 0), ("vs", 3, 0), ("gC2r", 4, 0), ("gF2r", 3, 0), ("gS2r", 2, 0), ("g1r", 0, 0), ("gC2r", 3, 0), ("g2r", 0, 0), ("gS2s", 0, 0), ("gF2r", 5, 0), ("gS2r", 1, 0), ("vr", 3, 0), ("vs", 4, 0), ("gS2r", 0, 0), ("gF2r", 2, 0), ("vr", 4, 0), ("gC2r", 5, 0), ("gC2r", 2, 0), ("gF2r", 1, 0), ("gF2r", 0, 0), ("gC2r", 1, 0), ("gC2r", 0, 0),),
    },
}
V_OB, V_G1, V_S1, V_EB, V_G2, V_S2 = 8, 9, 10, 11, 12, 13


def dot(left, right, dims):
    return lax.dot_general(left, right, dims, preferred_element_type=F32)


def depth_at(p, stage):
    done = SUMMED[p][3].split(stage)[0]
    return ("F" in done) + ("S" in done)


def z_rows(p, slot):
    sizes = {}
    for q, (_, _, n, chain) in enumerate(SUMMED):
        for t in range(3):
            sizes[q, t] = n >> depth_at(q, "Z" if "Z" in chain else "112"[t])
    return sum(n for key, n in sizes.items() if key < (p, slot)), sizes[p, slot]


def layer_kernel(
    cfg,
    tok, cot, wq, wk, wv, wo, wi, wout, bq, bv, bi, bo, g1, s1, be, g2, s2, seg_in, live_in,
    out_ref, dx_ref, whole, vec_ref,
    wbuf, bias, xs, cots, qkv, ka, ks, prob, mask, acc, tmp, nh1, r1,
    nb, nhalf, af, asib, al, gp, g, sg, di, fg,
    gr, rf, rz, rs, rx, vrecv, vin, short,
    seg, live, *rest,
):
    n_dp, d, seq, rows = cfg["dp"], cfg["d"], cfg["seq"], cfg["rows"]
    tl = seq * rows
    ml = d // 4
    hs = ml // DH
    half, qtr, eig = d // 2, d // 4, d // 8
    scale = DH ** (-0.5)
    bits = n_dp.bit_length() - 1
    dp, z = lax.axis_index("dp"), lax.axis_index("mp")
    c = dp % 2
    df = 2 + 2 * c
    ds_ = 6 - df
    f, s = (dp // df) % 2, (dp // ds_) % 2
    p_x = dp + df * (1 - 2 * f) + ds_ * (1 - 2 * s)
    p_f, p_s, p_c = dp + df * (1 - 2 * f), dp + ds_ * (1 - 2 * s), dp + 1 - 2 * c
    z0, zh = z % 2, z // 2
    z1, z2, z3 = z + 1 - 2 * z0, z + 2 - 4 * zh, 3 - z
    h0 = pl.multiple_of(c * half, 128)
    ho = pl.multiple_of((1 - c) * half, 128)

    def sub(base, n, depth, other=False):
        off = base
        for level, bit in enumerate((c, f, s)[:depth]):
            n //= 2
            off = off + n * (1 - bit if other and level == depth - 1 else bit)
        return (pl.multiple_of(off, 16) if depth else off), n

    def cut(base, n, depth, other=False):
        off = base
        for level, bit in enumerate((f, s)[:depth]):
            n //= 2
            off = off + n * (1 - bit if other and level == depth - 1 else bit)
        return (pl.multiple_of(off, 16) if depth else off), n

    gathered = {}
    for a, (piece, base, n, cuts) in enumerate(GATHERED):
        for depth in (1, 2, 3):
            for other in (False, True):
                gathered[a, depth, other] = sub(base, n, depth, other)
    summed = {}
    for p, (piece, base, n, chain) in enumerate(SUMMED):
        for depth in (0, 1, 2):
            for other in (False, True):
                summed[p, depth, other] = cut(base, n, depth, other)

    finals = {}
    for p, (piece, base, n, chain) in enumerate(SUMMED):
        for depth in (0, 1, 2):
            for other in (False, True):
                off, m = summed[p, depth, other]
                finals[p, depth, other] = (pl.multiple_of(c * half + off, 16), m)
        finals[p, "core", True] = (pl.multiple_of((1 - c) * half + base, 16), n)
    shard = (z, z1, z2, z3)

    def shard_of(k):
        k0, kh = k % 2, k // 2
        return z0 + k0 - 2 * z0 * k0 + 2 * (zh + kh - 2 * zh * kh)

    def remote(src, dst, ssem, rsem, dev):
        return pltpu.make_async_remote_copy(
            src_ref=src, dst_ref=dst, send_sem=ssem, recv_sem=rsem, device_id=dev, device_id_type=MESH
        )

    pending = []

    def send(make, group="early"):
        remote(*make()).start()
        pending.append((group, make))

    def flush(group):
        for item in [item for item in pending if item[0] == group]:
            remote(*item[1]()).wait_send()
            pending.remove(item)

    small = rest[:9]
    loc_sem, ag_s, ag_r, gr_s, gr_r, x_s, x_r, b_s, b_r, v_s, v_r, e_s, e_r = rest[9:]
    barrier = pltpu.get_barrier_semaphore()
    extra = [dp + (1 << b) * (1 - 2 * ((dp // (1 << b)) % 2)) for b in range(3, bits)]
    greet = [(p_c, z), (p_f, z), (p_s, z), (p_x, z), (dp, z1), (dp, z2), (dp, z3)] + [(e, z) for e in extra]
    for dev in greet:
        pl.semaphore_signal(barrier, inc=1, device_id=dev, device_id_type=MESH)
    att_loads = [
        pltpu.make_async_copy(ref, wbuf.at[ATT, z, pl.ds(j * ml, ml)], loc_sem.at[j])
        for j, ref in enumerate((wq, wk, wv, wo))
    ]
    vec_loads = [
        pltpu.make_async_copy(ref, dst, loc_sem.at[4 + j])
        for j, (ref, dst) in enumerate(zip((bq, bv, bi, bo, g1, s1, be, g2, s2), small))
    ]
    seg_loads = [
        pltpu.make_async_copy(seg_in, seg, loc_sem.at[13]),
        pltpu.make_async_copy(live_in, live, loc_sem.at[14]),
        pltpu.make_async_copy(tok, xs.at[pl.ds(0, rows)], loc_sem.at[15]),
    ]
    late_loads = [
        pltpu.make_async_copy(wi, wbuf.at[INN, z], loc_sem.at[16]),
        pltpu.make_async_copy(wout, wbuf.at[OUT, z], loc_sem.at[17]),
        pltpu.make_async_copy(cot, cots, loc_sem.at[18]),
    ]
    for cp in att_loads + vec_loads + seg_loads + late_loads:
        cp.start()
    for cp in att_loads:
        cp.wait()
    pl.semaphore_wait(barrier, len(greet))

    def own(piece, off, n):
        if piece == ATT:
            return wbuf.at[ATT, z, pl.ds(off, n)]
        return (wi, wout)[piece - 1].at[pl.ds(off, n)]

    def reg(piece, k, off, n):
        return wbuf.at[piece, shard[k], pl.ds(off, n)]

    def ag_send(a, slot, k, rows_of, dev, mine=False):
        piece = GATHERED[a][0]

        def make():
            region = reg(piece, k, *rows_of)
            return own(piece, *rows_of) if mine else region, region, ag_s.at[a, slot], ag_r.at[a, slot], dev

        send(make)

    def ag_wait(a, slot, k, rows_of):
        region = reg(GATHERED[a][0], k, *rows_of)
        remote(region, region, ag_s.at[a, slot], ag_r.at[a, slot], (dp, z1)).wait_recv()

    def first(a):
        return gathered[a, GATHERED[a][3], False]

    def a_z1(a, _):
        ag_send(a, 1, 0, first(a), (dp, z1), True)

    def a_z2(a, _):
        ag_send(a, 0, 0, first(a), (dp, z2), True)

    def a_zf(a, _):
        ag_wait(a, 0, 2, first(a))
        ag_send(a, 2, 2, first(a), (dp, z1))

    def a_arrive(a, k):
        if k != 2:
            ag_wait(a, {1: 1, 3: 2}[k], k, first(a))

    def a_s(a, k):
        a_arrive(a, k)
        ag_send(a, 2 + k, k, gathered[a, 3, False], (p_s, z))

    def a_f(a, k):
        if GATHERED[a][3] < 3:
            a_arrive(a, k)
        else:
            ag_wait(a, 2 + k, k, gathered[a, 3, True])
        ag_send(a, 5 + k, k, gathered[a, 2, False], (p_f, z))

    def a_c(a, k):
        if GATHERED[a][3] < 2:
            a_arrive(a, k)
        else:
            ag_wait(a, 5 + k, k, gathered[a, 2, True])
        ag_send(a, 8 + k, k, gathered[a, 1, False], (p_c, z))

    def a_d(a, k):
        ag_wait(a, 8 + k, k, gathered[a, 1, True])

    X_TOK, X_N, X_FG, X_A, X_DI, X_KA, X_G = 0, 1, 2, 4, 8, 12, 16

    def core_send(slot, pair):
        send(lambda: (*pair(), x_s.at[slot], x_r.at[slot], (p_c, z)))

    def core_wait(slot, dst):
        remote(dst, dst, x_s.at[slot], x_r.at[slot], (p_c, z)).wait_recv()

    def g_sem(p, slot):
        return gr_s.at[p, slot], gr_r.at[p, slot]

    def g_send(p, slot, pair, dev):
        send(lambda: (*pair(), *g_sem(p, slot), dev), p if slot < 11 else "late")

    def g_wait(p, slot, dst):
        remote(dst, dst, *g_sem(p, slot), (dp, z1)).wait_recv()

    def add_into(dst, src, n):
        m = 96 if n % 96 == 0 else (48 if n % 48 == 0 else (32 if n % 32 == 0 else 16))

        def blk(j, carry):
            sl = pl.ds(pl.multiple_of(j * m, 16), m)
            dst[sl, :] = (dst[sl, :].astype(F32) + src[sl, :].astype(F32)).astype(BF)
            return carry

        lax.fori_loop(0, n // m, blk, 0)

    def chunk(p, k, depth, other=False):
        off, n = summed[p, depth, other]
        return gr.at[SUMMED[p][0], k, pl.ds(off, n)]

    def final(p, depth, other=False):
        off, n = finals[p, depth, other]
        return whole.at[SUMMED[p][0], pl.ds(off, n)]

    def final_across(p, side):
        _, base, n, _ = SUMMED[p]
        off = pl.multiple_of(c * half + base + (1 - f) * (n // 2) + side * (n // 4), 16)
        return whole.at[SUMMED[p][0], pl.ds(off, n // 4)]

    def f_slot(p, k):
        piece, base, n, _ = SUMMED[p]
        return rf.at[piece, k, pl.ds(base // 2, n // 2)]

    def s_slot(p, k):
        piece, base, n, _ = SUMMED[p]
        return rs.at[piece, k, pl.ds(base // 4, n // 4)]

    def z_slot(p, slot):
        return rz.at[pl.ds(*z_rows(p, slot))]

    def g_fs(p, k):
        g_send(p, k, lambda: (chunk(p, k, 1, True), f_slot(p, k)), (p_f, z))

    def g_fr(p, k):
        g_wait(p, k, f_slot(p, k))
        add_into(chunk(p, k, 1), f_slot(p, k), SUMMED[p][2] // 2)

    def g_ss(p, k):
        g_send(p, 4 + k, lambda: (chunk(p, k, 2, True), s_slot(p, k)), (p_s, z))

    def g_sr(p, k):
        g_wait(p, 4 + k, s_slot(p, k))
        add_into(chunk(p, k, 2), s_slot(p, k), SUMMED[p][2] // 4)

    def g_1s(p, k):
        slot = 0 if k == 3 else 1
        g_send(p, 8 + slot, lambda: (chunk(p, k, depth_at(p, "1")), z_slot(p, slot)), (dp, z1))

    def g_1r(p, k):
        slot = 0 if k == 2 else 1
        g_wait(p, 8 + slot, z_slot(p, slot))
        depth = depth_at(p, "1")
        add_into(chunk(p, k, depth), z_slot(p, slot), SUMMED[p][2] >> depth)

    def g_2s(p, k):
        g_send(p, 10, lambda: (chunk(p, 2, depth_at(p, "2")), z_slot(p, 2)), (dp, z2))

    def g_2r(p, k):
        g_wait(p, 10, z_slot(p, 2))
        depth = depth_at(p, "2")
        add_into(chunk(p, 0, depth), z_slot(p, 2), SUMMED[p][2] >> depth)

    def g_zs(p, k):
        depth = depth_at(p, "Z")
        g_send(p, 7 + k, lambda: (chunk(p, k, depth), z_slot(p, k - 1)), (dp, shard[k]))

    def g_zr(p, k):
        depth = depth_at(p, "Z")
        g_wait(p, 7 + k, z_slot(p, k - 1))
        add_into(chunk(p, 0, depth), z_slot(p, k - 1), SUMMED[p][2] >> depth)

    def g_s2s(p, _):
        piece, base, n, _ = SUMMED[p]
        for j, partner in enumerate(extra):
            slot = rx.at[piece, j, pl.ds(base // 4, n // 4)]
            cp = remote(chunk(p, 0, 2), slot, e_s.at[p, j], e_r.at[p, j], (partner, z))
            cp.start()
            cp.wait()
            add_into(chunk(p, 0, 2), slot, n // 4)
        mine, target = chunk(p, 0, 2), final(p, 2)
        for lo in range(0, n // 4, 16):
            target[pl.ds(lo, 16), :] = mine[pl.ds(lo, 16), :]
        g_send(p, 11, lambda: (final(p, 2),) * 2, (p_s, z))
        if SUMMED[p][3].endswith("d"):
            g_send(p, 12, lambda: (final(p, 2),) * 2, (p_f, z))
            g_send(p, 14, lambda: (final(p, 2),) * 2, (p_x, z))

    def g_s2r(p, _):
        g_wait(p, 11, final(p, 2, True))
        g_send(p, 12, lambda: (final(p, 1),) * 2, (p_f, z))

    def g_d2sr(p, _):
        g_wait(p, 11, final(p, 2, True))

    def g_d2fr(p, _):
        g_wait(p, 12, final_across(p, s))

    def g_f2r(p, _):
        if SUMMED[p][3].endswith("d"):
            g_wait(p, 14, final_across(p, 1 - s))
        else:
            g_wait(p, 12, final(p, 1, True))
        g_send(p, 13, lambda: (final(p, 0),) * 2, (p_c, z))
        flush(p)

    def g_c2r(p, _):
        g_wait(p, 13, final(p, "core", True))

    partners = [(p_c, z), (p_f, z), (p_s, z), (dp, z1), (dp, z2)] + [(e, z) for e in extra]

    def v_half(mine):
        return vec_ref.at[pl.ds(pl.multiple_of(8 * (c if mine else 1 - c), 8), 8)]

    def v_copy(j):
        return remote(v_half(j > 0), vrecv.at[j], v_s.at[j], v_r.at[j], partners[j])

    def v_send(j, _):
        v_copy(j).start()

    def v_back():
        return remote(v_half(True), v_half(True), v_s.at[len(partners)], v_r.at[len(partners)], (p_c, z))

    def v_recv(j, _):
        v_copy(j).wait()
        half_ref = v_half(True)
        half_ref[...] = half_ref[...] + vrecv[j]
        if j == len(partners) - 1:
            v_back().start()

    events = {
        "az1": a_z1, "az2": a_z2, "zf": a_zf, "s": a_s, "f": a_f, "c": a_c, "d": a_d,
        "gFs": g_fs, "gFr": g_fr, "gSs": g_ss, "gSr": g_sr, "g1s": g_1s, "g1r": g_1r, "g2s": g_2s, "g2r": g_2r,
        "gZs": g_zs, "gZr": g_zr, "gd2Fr": g_d2fr, "gd2Sr": g_d2sr, "gS2s": g_s2s, "gS2r": g_s2r, "gF2r": g_f2r, "gC2r": g_c2r, "vs": v_send, "vr": v_recv,
    }

    def do(listed):
        for kind, piece, k in listed:
            events[kind](piece, k)

    def at(place, index):
        for n, listed in PLAN.get(place, {}).items():
            pl.when(index == n)(functools.partial(do, listed))

    def once(place):
        do(PLAN.get(place, {}).get(0, ()))

    once("x0")
    for cp in vec_loads:
        cp.wait()
    vin[...] = jnp.zeros_like(vin)
    vin[pl.ds(0, 1), pl.ds(0, ml)] = small[0][...].astype(F32).reshape(1, ml)
    vin[pl.ds(0, 1), pl.ds(2 * ml, ml)] = small[1][...].astype(F32).reshape(1, ml)
    for j, ref in enumerate(small[2:]):
        vin[pl.ds(j + 1, 1), :] = ref[...].astype(F32).reshape(1, d)
    bias[z] = vin[...]
    third = d // 3
    short[z] = jnp.zeros((8, third), F32)
    short[z, pl.ds(0, 1), pl.ds(0, ml)] = vin[pl.ds(0, 1), pl.ds(0, ml)]
    short[z, pl.ds(1, 1), pl.ds(0, ml)] = vin[pl.ds(0, 1), pl.ds(2 * ml, ml)]
    for j in range(3):
        short[z, pl.ds(2 + j, 1), :] = vin[pl.ds(1, 1), pl.ds(j * third, third)]
    for j, zz in enumerate((z1, z2, z3)):
        send(lambda j=j, zz=zz: (short.at[z], short.at[z], b_s.at[j], b_r.at[j], (dp, zz)))
    core_send(X_TOK, lambda: (tok, xs.at[pl.ds(rows, rows)]))
    for cp in seg_loads:
        cp.wait()

    for r in range(rows):
        seg_row = seg[pl.ds(z * rows + r, 1), :]
        live_row = live[pl.ds(z * rows + r, 1), :]
        code = jnp.where(live_row == 1, seg_row, -1)
        ids = lax.broadcasted_iota(jnp.int32, (8, seq), 0)
        key_hot = (jnp.broadcast_to(code, (8, seq)) == ids).astype(F32).astype(BF)
        query_hot = (jnp.broadcast_to(seg_row, (8, seq)) == ids).astype(F32).astype(BF)
        mask[r] = jnp.where(dot(key_hot, query_hot, TN) > 0.5, 0.0, NEG_FILL)
    acc[...] = jnp.zeros_like(acc)
    first_row = (lax.broadcasted_iota(jnp.int32, (8, seq), 0) == 0).astype(F32).astype(BF)

    def attend(i, carry):
        t = shard_of(i)

        def row(r, inner_carry):
            at("att", i * rows + r)

            @pl.when((i == 1) & (r == 0))
            def _():
                for j, zz in enumerate((z1, z2, z3)):
                    remote(short.at[zz], short.at[zz], b_s.at[j], b_r.at[j], (dp, zz)).wait_recv()
                    bias[zz] = jnp.zeros((8, d), F32)
                    bias[zz, pl.ds(0, 1), pl.ds(0, ml)] = short[zz, pl.ds(0, 1), pl.ds(0, ml)]
                    bias[zz, pl.ds(0, 1), pl.ds(2 * ml, ml)] = short[zz, pl.ds(1, 1), pl.ds(0, ml)]
                    for n in range(3):
                        bias[zz, pl.ds(1, 1), pl.ds(n * third, third)] = short[zz, pl.ds(2 + n, 1), :]

            x_row = xs[r]
            bias_rows = bias[t].astype(BF)[:, : 3 * ml]
            qkv[t, r] = (
                dot(wbuf[ATT, t, pl.ds(0, 3 * ml), :], x_row, NT) + dot(bias_rows, first_row, TN)
            ).astype(BF)
            for h in range(hs):
                query = qkv[t, r, pl.ds(h * DH, DH), :]
                key = qkv[t, r, pl.ds(ml + h * DH, DH), :]
                value = qkv[t, r, pl.ds(2 * ml + h * DH, DH), :]
                scores = dot(key, query, TN) * scale + mask[r]
                top = jnp.max(scores, 0, keepdims=True)
                exponent = jnp.exp(scores - top)
                total = jnp.sum(exponent, 0, keepdims=True)
                prob_t = (exponent * (1.0 / total)).astype(BF)
                prob[t, r, h] = prob_t
                ka[t, r, pl.ds(3 * ml + h * DH, DH), :] = dot(value, prob_t, NN).astype(BF)
            part_sum = dot(ka[t, r, pl.ds(3 * ml, ml), :], wbuf[ATT, t, pl.ds(3 * ml, ml), :], TN)
            sl = pl.ds(pl.multiple_of(r * seq, 16), seq)
            acc[sl, :] = acc[sl, :] + part_sum
            return inner_carry

        lax.fori_loop(0, rows, row, 0)
        return carry

    lax.fori_loop(0, 4, attend, 0)

    rb = seq

    def norm_rows(summed):
        mean = jnp.mean(summed, -1, keepdims=True)
        centred = summed - mean
        variance = jnp.mean(centred * centred, -1, keepdims=True)
        rs_ = lax.rsqrt(variance + EPSILON)
        return centred * rs_, rs_

    def norm_back(grad, hat, rs_):
        return rs_ * (grad - jnp.mean(grad, -1, keepdims=True) - hat * jnp.mean(grad * hat, -1, keepdims=True))

    def vrow(j):
        return vin[pl.ds(j, 1), :]

    once("n1")

    def norm1(j, carry):
        sl = pl.ds(pl.multiple_of(j * rb, 16), rb)
        per = seq // rb
        x_blk = xs[j // per, pl.ds(pl.multiple_of((j % per) * rb, 16), rb), :].astype(F32)
        hat, rs_ = norm_rows(acc[sl, :] + vrow(2) + x_blk)
        nh1[sl, :] = hat
        r1[sl, :] = jnp.broadcast_to(rs_, (rb, 128))
        nb[sl, :] = (hat * vrow(3) + vrow(4)).astype(BF)
        acc[sl, :] = jnp.zeros((rb, d), F32)
        return carry

    lax.fori_loop(0, tl // rb, norm1, 0)
    core_send(X_N, lambda: (nb.at[:, pl.ds(ho, half)], nhalf.at[pl.ds(tl, tl)]))
    nhalf[pl.ds(0, tl), :] = nb[:, pl.ds(h0, half)]

    late_loads[0].wait()

    def up(i, carry):
        at("up", i)
        t = shard_of(i)
        tmp[...] = dot(nb[...], wbuf[INN, t], NN)
        b_row = bias[t, pl.ds(1, 1), :]

        def act(j, carry):
            sl = pl.ds(pl.multiple_of(j * rb, 16), rb)
            u = tmp[sl, :] + b_row
            cdf = 0.5 * (1.0 + lax.erf(u * ROOT_HALF))
            af[t, sl, :] = (u * cdf).astype(BF)
            gp[t, sl, :] = (cdf + u * (PDF_SCALE * jnp.exp(-0.5 * u * u))).astype(BF)
            return carry

        lax.fori_loop(0, tl // rb, act, 0)
        remote(af.at[t, :, pl.ds(ho, half)], asib.at[t], x_s.at[X_A + i], x_r.at[X_A + i], (p_c, z)).start()
        return carry

    lax.fori_loop(0, 4, up, 0)
    late_loads[1].wait()
    late_loads[2].wait()

    def down(i, carry):
        at("dn", i)
        t = shard_of(i)
        acc[...] += dot(af[t], wbuf[OUT, t], NN)
        return carry

    lax.fori_loop(0, 4, down, 0)

    once("l2")
    vec_ref[...] = jnp.zeros_like(vec_ref)

    def add_vec(row, value):
        vec_ref[pl.ds(row, 1), :] = vec_ref[pl.ds(row, 1), :] + value

    def norm2(j, carry):
        sl = pl.ds(pl.multiple_of(j * rb, 16), rb)
        normed = nh1[sl, :] * vrow(3) + vrow(4)
        hat, rs_ = norm_rows(acc[sl, :] + vrow(5) + normed)
        c_blk = cots[sl, :].astype(F32)
        out_ref[sl, :] = (hat * vrow(6) + vrow(7)).astype(BF)
        back = norm_back(c_blk * vrow(6), hat, rs_)
        sg[sl, :] = back
        g[sl, :] = back.astype(BF)
        acc[sl, :] = jnp.zeros((rb, d), F32)
        add_vec(V_G2, jnp.sum(c_blk * hat, 0, keepdims=True))
        add_vec(V_S2, jnp.sum(c_blk, 0, keepdims=True))
        add_vec(V_EB, jnp.sum(back, 0, keepdims=True))
        return carry

    def g_copy(j):
        src = g.at[pl.ds(pl.multiple_of(j * rb, 16), rb)]
        dst = g.at[pl.ds(pl.multiple_of(tl + j * rb, 16), rb)]
        return remote(src, dst, x_s.at[X_G + j], x_r.at[X_G + j], (p_c, z))

    for j in range(tl // rb):
        norm2(j, 0)
        g_copy(j).start()
    def order(i):
        return 3 - 2 * (i % 2) - i // 2

    def ffn_back(i, carry):
        @pl.when(i < 4)
        def _():
            at("da", i)
            k = order(i)
            t = shard_of(k)
            tmp[...] = dot(g[pl.ds(0, tl), :], wbuf[OUT, t], NT)

            def act(j, total):
                sl = pl.ds(pl.multiple_of(j * rb, 16), rb)
                blk = (tmp[sl, :] * gp[t, sl, :].astype(F32)).astype(BF)
                di[t, sl, :] = blk
                return total + jnp.sum(blk.astype(F32), 0, keepdims=True)

            vec_ref[pl.ds(4 + t, 1), :] = lax.fori_loop(0, tl // rb, act, jnp.zeros((1, d), F32))
            remote(
                di.at[t, pl.ds(0, tl)], di.at[t, pl.ds(tl, tl)], x_s.at[X_DI + k], x_r.at[X_DI + k], (p_c, z)
            ).start()
            at("gwo", i)

            @pl.when(i == 0)
            def _():
                for j in range(tl // rb):
                    g_copy(j).wait_recv()
                core_wait(X_N, nhalf.at[pl.ds(tl, tl)])

            core_wait(X_A + k, asib.at[t])
            al[pl.ds(0, tl), :] = af[t, :, pl.ds(h0, half)]
            al[pl.ds(tl, tl), :] = asib[t]
            gr[OUT, k] = dot(al[...], g[...], TN).astype(BF)
            at("dn2", i)
            acc[...] += dot(di[t, pl.ds(0, tl), :], wbuf[INN, t], NT)

        @pl.when(i > 0)
        def _():
            at("gwi", i - 1)
            k = order(i - 1)
            t = shard_of(k)
            core_wait(X_DI + k, di.at[t, pl.ds(tl, tl)])
            gr[INN, k] = dot(nhalf[...], di[t], TN).astype(BF)

        return carry

    lax.fori_loop(0, 5, ffn_back, 0)
    once("l1b")

    def norm1_back(j, carry):
        sl = pl.ds(pl.multiple_of(j * rb, 16), rb)
        per = seq // rb
        hat = nh1[sl, :]
        total = acc[sl, :] + sg[sl, :]
        back = norm_back(total * vrow(3), hat, r1[sl, 0:1])
        sg[sl, :] = back
        fg[j // per, pl.ds(pl.multiple_of((j % per) * rb, 16), rb), :] = back.astype(BF)
        acc[sl, :] = jnp.zeros((rb, d), F32)
        add_vec(V_G1, jnp.sum(total * hat, 0, keepdims=True))
        add_vec(V_S1, jnp.sum(total, 0, keepdims=True))
        add_vec(V_OB, jnp.sum(back, 0, keepdims=True))
        return carry

    lax.fori_loop(0, tl // rb, norm1_back, 0)
    core_send(X_FG, lambda: (fg.at[pl.ds(0, rows)], fg.at[pl.ds(rows, rows)]))
    ones = jnp.ones((8, seq), BF)

    def att_back(i, carry):
        @pl.when(i < 4)
        def _():
            k = order(i)
            t = shard_of(k)

            def row(r, inner_carry):
                at("ab", i * rows + r)
                dctx = dot(wbuf[ATT, t, pl.ds(3 * ml, ml), :], fg[r], NT).astype(BF)
                for h in range(hs):
                    query = qkv[t, r, pl.ds(h * DH, DH), :]
                    key = qkv[t, r, pl.ds(ml + h * DH, DH), :]
                    value = qkv[t, r, pl.ds(2 * ml + h * DH, DH), :]
                    prob_t = prob[t, r, h]
                    grad = dctx[h * DH : (h + 1) * DH]
                    ka[t, r, pl.ds(2 * ml + h * DH, DH), :] = dot(grad, prob_t, NT).astype(BF)
                    prob_grad = dot(value, grad, TN)
                    wide_prob = prob_t.astype(F32)
                    inner = jnp.sum(wide_prob * prob_grad, 0, keepdims=True)
                    score_grad = (wide_prob * (prob_grad - inner)).astype(BF)
                    ka[t, r, pl.ds(h * DH, DH), :] = (dot(key, score_grad, NN) * scale).astype(BF)
                    ka[t, r, pl.ds(ml + h * DH, DH), :] = (dot(query, score_grad, NT) * scale).astype(BF)
                grads = ka[t, r, pl.ds(0, 3 * ml), :]
                vec_ref[pl.ds(t, 1), pl.ds(0, 3 * ml)] += dot(ones, grads, NT)[0:1]
                sl = pl.ds(pl.multiple_of(r * seq, 16), seq)
                acc[sl, :] = acc[sl, :] + dot(grads, wbuf[ATT, t, pl.ds(0, 3 * ml), :], TN)
                return inner_carry

            lax.fori_loop(0, rows, row, 0)
            remote(
                ka.at[t, :, pl.ds(ho, half)], ks.at[t], x_s.at[X_KA + k], x_r.at[X_KA + k], (p_c, z)
            ).start()

        @pl.when(i == 0)
        def _():
            core_wait(X_TOK, xs.at[pl.ds(rows, rows)])
            core_wait(X_FG, fg.at[pl.ds(rows, rows)])

        @pl.when(i > 0)
        def _():
            at("gwa", i - 1)
            k = order(i - 1)
            t = shard_of(k)
            core_wait(X_KA + k, ks.at[t])
            for j in range(2):
                rowsel = pl.ds(pl.multiple_of(h0 + j * ml, 16), ml)
                use = c * j
                total = jnp.zeros((ml, d), F32)
                for r in range(rows):
                    right_own = xs[r] if j == 0 else jnp.where(use == 1, fg[r], xs[r])
                    right_sib = xs[rows + r] if j == 0 else jnp.where(use == 1, fg[rows + r], xs[rows + r])
                    total += dot(ka[t, r, rowsel, :], right_own, NN)
                    total += dot(ks[t, r, pl.ds(j * ml, ml), :], right_sib, NN)
                gr[ATT, k, pl.ds(j * ml, ml), :] = total.astype(BF)

        return carry

    lax.fori_loop(0, 5, att_back, 0)
    once("fin")

    def finish(j, carry):
        sl = pl.ds(pl.multiple_of(j * rb, 16), rb)
        dx_ref[sl, :] = (sg[sl, :] + acc[sl, :]).astype(BF)
        return carry

    lax.fori_loop(0, tl // rb, finish, 0)


    flush("early")

    def sent(k, carry):
        t = shard_of(k)
        remote(af.at[t, :, pl.ds(ho, half)], asib.at[t], x_s.at[X_A + k], x_r.at[X_A + k], (p_c, z)).wait_send()
        remote(
            di.at[t, pl.ds(0, tl)], di.at[t, pl.ds(tl, tl)], x_s.at[X_DI + k], x_r.at[X_DI + k], (p_c, z)
        ).wait_send()
        remote(ka.at[t, :, pl.ds(ho, half)], ks.at[t], x_s.at[X_KA + k], x_r.at[X_KA + k], (p_c, z)).wait_send()
        return carry

    lax.fori_loop(0, 4, sent, 0)
    for j in range(tl // rb):
        g_copy(j).wait_send()

    once("end")
    for j in range(5, len(partners)):
        v_send(j, 0)
        v_recv(j, 0)
    other_half = v_half(False)
    remote(other_half, other_half, v_s.at[len(partners)], v_r.at[len(partners)], (p_c, z)).wait_recv()
    v_back().wait_send()

    flush("late")
    assert not pending


def spread_kernel(
    ml, grads, vec, out_in, dx_in,
    out_ref, dx_ref, gq, gk, gv, go, gi, ge, bq, bv, bo, g1, s1, bi, be, g2, s2,
    wide_v, *rest,
):
    z = lax.axis_index("mp")
    n = 2 * ml
    outs = []
    small, sem = rest[:9], rest[9]

    def put(src, dst):
        cp = pltpu.make_async_copy(src, dst, sem.at[len(outs)])
        cp.start()
        outs.append(cp)

    put(out_in, out_ref)
    put(dx_in, dx_ref)
    picks = [(z, 0, ml, bq), (z, 2 * ml, ml, bv), (4 + z, 0, 4 * ml, bi)]
    picks += [
        (row, 0, 4 * ml, ref)
        for row, ref in ((V_OB, bo), (V_G1, g1), (V_S1, s1), (V_EB, be), (V_G2, g2), (V_S2, s2))
    ]
    steps = [(0, j * ml, ref, 0, ml) for j, ref in enumerate((gq, gk, gv, go))]
    steps += [(piece, lo, ref, lo, n) for piece, ref in ((1, gi), (2, ge)) for lo in (0, n)]
    for count, (piece, lo, ref, row, m) in enumerate(steps):
        wide_v[piece, pl.ds(lo, m), :] = grads[piece, pl.ds(lo, m), :].astype(F32)
        put(wide_v.at[piece, pl.ds(lo, m)], ref.at[pl.ds(row, m)])
        if count == 3:
            for (src_row, src_lo, width, dst), buf in zip(picks, small):
                buf[...] = vec[pl.ds(src_row, 1), pl.ds(src_lo, width)].reshape(width)
                put(buf, dst)
    for cp in outs:
        cp.wait()


def per_device(
    n_dp,
    tokens, segment_ids, live_mask, query_weight, key_weight, value_weight, query_bias, value_bias,
    output_weight, output_bias, first_gain, first_shift, inner_weight, inner_bias, outer_weight,
    outer_bias, second_gain, second_shift, cotangent,
):
    tl, d = tokens.shape
    seq_rows, seq = segment_ids.shape
    rows = tl // seq
    ml = query_weight.shape[1]
    ff = inner_weight.shape[1]
    half, qtr, eig = d // 2, d // 4, d // 8
    bits = n_dp.bit_length() - 1
    n_extra = max(bits - 3, 1)
    n_vec = bits + 3
    cfg = {"dp": n_dp, "d": d, "seq": seq, "rows": rows}
    vmem = pl.BlockSpec(memory_space=pltpu.VMEM)
    hbm = pl.BlockSpec(memory_space=pl.ANY)
    scratch = [
        pltpu.VMEM((3, 4, d, d), BF),
        pltpu.VMEM((4, 8, d), F32),
        pltpu.VMEM((2 * rows, seq, d), BF),
        pltpu.VMEM((tl, d), BF),
        pltpu.VMEM((4, rows, 3 * ml, seq), BF),
        pltpu.VMEM((4, rows, d, seq), BF),
        pltpu.VMEM((4, rows, half, seq), BF),
        pltpu.VMEM((4, rows, ml // DH, seq, seq), BF),
        pltpu.VMEM((rows, seq, seq), F32),
        pltpu.VMEM((tl, d), F32),
        pltpu.VMEM((tl, d), F32),
        pltpu.VMEM((tl, d), F32),
        pltpu.VMEM((tl, 128), F32),
        pltpu.VMEM((tl, d), BF),
        pltpu.VMEM((2 * tl, half), BF),
        pltpu.VMEM((4, tl, d), BF),
        pltpu.VMEM((4, tl, half), BF),
        pltpu.VMEM((2 * tl, half), BF),
        pltpu.VMEM((4, tl, d), BF),
        pltpu.VMEM((2 * tl, d), BF),
        pltpu.VMEM((tl, d), F32),
        pltpu.VMEM((4, 2 * tl, d), BF),
        pltpu.VMEM((2 * rows, seq, d), BF),
        pltpu.VMEM((3, 4, half, d), BF),
        pltpu.VMEM((3, 4, qtr, d), BF),
        pltpu.VMEM((sum(z_rows(len(SUMMED) - 1, 2)), d), BF),
        pltpu.VMEM((3, 4, eig, d), BF),
        pltpu.VMEM((3, n_extra, eig, d), BF) if bits > 3 else pltpu.VMEM((1, 1, 16, 128), BF),
        pltpu.VMEM((n_vec - 1, 8, d), F32),
        pltpu.VMEM((8, d), F32),
        pltpu.VMEM((4, 8, d // 3), F32),
        pltpu.VMEM((seq_rows, seq), jnp.int32),
        pltpu.VMEM((seq_rows, seq), jnp.int32),
    ]
    scratch += [pltpu.VMEM((n,), BF) for n in (ml, ml, ff, d, d, d, d, d, d)]
    scratch += [
        pltpu.SemaphoreType.DMA(shape)
        for shape in [(24,)] + [(len(GATHERED), 12)] * 2 + [(len(SUMMED), 15)] * 2 + [(16 + rows,)] * 2 + [(3,)] * 2
        + [(n_vec,)] * 2 + [(len(SUMMED), n_extra)] * 2
    ]
    out, dx, grads, vec = pl.pallas_call(
        functools.partial(layer_kernel, cfg),
        out_shape=(
            pltpu.VMEM((tl, d), BF),
            pltpu.VMEM((tl, d), BF),
            pltpu.VMEM((3, d, d), BF),
            pltpu.VMEM((16, d), F32),
        ),
        in_specs=[hbm] * 19,
        out_specs=(vmem,) * 4,
        scratch_shapes=scratch,
        compiler_params=pltpu.CompilerParams(
            collective_id=0, has_side_effects=True, vmem_limit_bytes=LIMIT
        ),
        name="layer",
    )(
        tokens.reshape(rows, seq, d), cotangent, query_weight.T, key_weight.T, value_weight.T, output_weight,
        inner_weight, outer_weight, query_bias, value_bias, inner_bias, output_bias, first_gain, first_shift,
        outer_bias, second_gain, second_shift, segment_ids, live_mask,
    )
    out, dx, gq, gk, gv, go, gi, ge, bq, bv, bo, g1, s1, bi, be, g2, s2 = pl.pallas_call(
        functools.partial(spread_kernel, ml),
        out_shape=tuple(
            jax.ShapeDtypeStruct(shape, dtype)
            for shape, dtype in [((tl, d), BF)] * 2
            + [((ml, d), F32)] * 4
            + [((d, ff), F32), ((ff, d), F32)]
            + [((ml,), F32)] * 2
            + [((d,), F32)] * 7
        ),
        in_specs=[vmem] * 4,
        out_specs=(hbm,) * 17,
        scratch_shapes=[pltpu.VMEM((3, d, d), F32)]
        + [pltpu.VMEM((n,), F32) for n in (ml, ml, ff, d, d, d, d, d, d)]
        + [pltpu.SemaphoreType.DMA((19,))],
        compiler_params=pltpu.CompilerParams(vmem_limit_bytes=24 * 1024 * 1024),
        name="spread",
    )(*(pltpu.with_memory_space_constraint(x, pltpu.VMEM) for x in (grads, vec, out, dx)))
    return out, dx, gq.T, gk.T, gv.T, bq, bv, go, bo, g1, s1, gi, bi, ge, be, g2, s2


def solution(mesh):
    tok, shared = P(("dp", "mp"), None), P()
    cols, rows, vec = P(None, "mp"), P("mp", None), P("mp")
    in_specs = (
        tok, P("dp", None), P("dp", None), cols, cols, cols, vec, vec, rows, shared, shared, shared,
        cols, vec, rows, shared, shared, shared, tok,
    )
    out_specs = (
        tok, tok, cols, cols, cols, vec, vec, rows, shared, shared, shared, cols, vec, rows,
        shared, shared, shared,
    )
    return jax.shard_map(
        functools.partial(per_device, mesh.shape["dp"]),
        mesh=mesh,
        in_specs=in_specs,
        out_specs=out_specs,
        check_vma=False,
    )
```
